128 devices in a mesh: dp: 32 (over z, x, core), section: 4 (over y).
Axes of the slice: x: 4, y: 4, z: 4, core: 2. Of those that a mesh axis runs over, the one named last changes fastest.
Arguments:
- tokens: bfloat16 [128, 197, 768], P(('dp', 'section')), may hold values from -6 to 6
- masked: int32 [128, 197], P(('dp', 'section')), may hold values from 0 to 1, as said below
- live_images: int32 [32], replicated, may hold values from 2 to 4, as said below
- mask_token: bfloat16 [768], replicated, may hold values from -5 to 5
- norm_gain: float32 [4, 768], P('section'), may hold values from 0.1 to 1.9
- norm_shift: float32 [4, 768], P('section'), may hold values from -3 to 3
- w_first: bfloat16 [4, 768, 3072], P('section')
- w_second: bfloat16 [2, 3072, 768], replicated, may hold values from -0.109375 to 0.109375
- layer_scale: float32 [4, 768], P('section'), may hold values from 0.5 to 2
- rel_table: float32 [2, 732, 12], replicated, may hold values from -4 to 4
- cotangent: bfloat16 [128, 197, 768], P(('dp', 'section')), may hold values from -6 to 6
Outputs:
- block_out: bfloat16 [128, 197, 768], P(('dp', 'section'))
- tokens_grad: bfloat16 [128, 197, 768], P(('dp', 'section'))
- first_grad: float32 [4, 768, 3072], P('section')
- second_grad: float32 [2, 3072, 768], P(None, ('dp', 'section'))
- gain_grad: float32 [4, 768], P('section')
- shift_grad: float32 [4, 768], P('section')
- scale_grad: float32 [4, 768], P('section')
- table_grad: float32 [2, 732, 12], replicated
- mask_grad: float32 [768], replicated
- rms_out: float32 [4, 2], replicated
The draws below stay inside these ranges and needn't reach their ends.
Inputs may be any that keep to these rules, and one draw needn't show every extreme that they name: The class token (position 0) of every image is never masked. `live_images`: images in use of the 4 slots of one index of dp; the unused slots are the last ones of that index; some index is full.
All inputs are finite; a program needn't handle non-finite values.
Results may differ from the reference program's by a relative error of at most 0.025.
Values may be sent and summed in bfloat16 or wider, within the bound.
A program may use at most 512 MiB of HBM per device.

```python
import math
import jax
import jax.numpy as jnp
import numpy as np
from jax import lax

D = 768
FF = 3072
HEADS = 12
GRID = 14
IMG_Q = 1
SEQ = 197
RELS = 732
LAYERS = 2
IMAGES = 128
N_DP = 32
N_SECTION = 4


def draw_masked(key, part):
    key = jax.random.fold_in(key, 7)
    picks = jax.random.randint(key, (IMAGES, SEQ), 0, 5)
    marked = (picks < 2).astype(jnp.int32)
    return jnp.where(jnp.arange(SEQ)[None, :] == 0, 0, marked).astype(jnp.int32)


def draw_live_images(key, part):
    key = jax.random.fold_in(key, 5)
    full_count = N_SECTION * IMG_Q
    least_count = (full_count + 1) // 2
    first_key, second_key = jax.random.split(key)
    counts = jax.random.randint(first_key, (N_DP,), least_count, full_count + 1)
    chosen = jax.random.randint(second_key, (), 0, N_DP)
    positions = jnp.arange(N_DP)
    counts = jnp.where(positions == chosen, full_count, counts)
    counts = jnp.where(positions == (chosen + 1) % N_DP, least_count, counts)
    return counts.astype(jnp.int32)


def draw_w_first(key, part):
    key = jax.random.fold_in(key, 11)
    base = jax.random.truncated_normal(key, -4.0, 4.0, (N_SECTION, D, FF), jnp.float32) * D ** (-0.5)
    even_section = (jnp.arange(N_SECTION) % 2 == 0)[:, None, None]
    out_columns = (jnp.arange(FF) >= 3 * D)[None, None, :]
    factor = jnp.where(even_section & out_columns, 4.0, 1.0)
    return (base * factor).astype(jnp.bfloat16)


def block_scale(rng, extent, pieces, least, top_value):
    factor_of, own = 1.0, jax.random.fold_in(rng, 6)
    for position, shards_of in pieces:
        steps = jnp.exp(jax.random.uniform(jax.random.fold_in(own, position), (shards_of,), jnp.float32, least / len(pieces), top_value / len(pieces)))
        factor_of = factor_of * jnp.repeat(steps, extent[position] // shards_of).reshape([-1 if axis == position else 1 for axis in range(len(extent))])
    return factor_of


def noise(own_key, extent, scale, bound, shards=(), kind=jnp.bfloat16):
    drawn = jax.random.normal(own_key, extent, jnp.float32) * scale
    if len(shards) > 0:
        drawn = block_scale(own_key, extent, shards, -0.22, 0.18) * drawn
    return jnp.clip(drawn, min=-bound, max=bound).astype(kind)


def setup_inputs(seed: int = 0) -> dict:
    streams_of = jax.random.split(jax.random.key(seed), 12)
    return {
        "tokens": noise(streams_of[0], (IMAGES, SEQ, D), 1.0, 6.0, ((0, 128),)),
        "masked": draw_masked(jax.random.fold_in(streams_of[11], 71), 0),
        "live_images": draw_live_images(jax.random.fold_in(streams_of[11], 71), 0),
        "mask_token": noise(streams_of[3], (D,), 1.0, 5.0),
        "norm_gain": jnp.clip(1.0 + 0.18 * jax.random.normal(streams_of[4], (N_SECTION, D), jnp.float32), 0.1, 1.9),
        "norm_shift": noise(streams_of[5], (N_SECTION, D), 0.5, 3.0, ((0, 4),), jnp.float32),
        "w_first": draw_w_first(jax.random.fold_in(streams_of[11], 71), 0),
        "w_second": noise(streams_of[7], (LAYERS, FF, D), FF ** -0.5, 0.109375),
        "layer_scale": jnp.clip(jnp.exp(math.log(2.0) - 1.3862944 * jax.random.uniform(streams_of[8], (N_SECTION, D), jnp.float32) ** block_scale(streams_of[8], (N_SECTION, D), ((0, 4),), -0.2, 0.2)), 0.5, 2.0),
        "rel_table": noise(streams_of[9], (LAYERS, RELS, HEADS), 1.0, 4.0, (), jnp.float32),
        "cotangent": noise(streams_of[10], (IMAGES, SEQ, D), 1.0, 6.0, ((0, 128),)),
    }


@jax.custom_vjp
def low(v):
    return lax.optimization_barrier(v.astype(jnp.bfloat16)).astype(jnp.float32)

@jax.custom_vjp
def low_back(v):
    return v

def low_keep(v):
    return (low(v), None)

def low_pass(kept, grad):
    return (grad,)

def back_keep(v):
    return (v, None)

def back_low(kept, grad):
    return (low(grad),)
low.defvjp(low_keep, low_pass)
low_back.defvjp(back_keep, back_low)
EPSILON = 1e-06
HIGH = lax.Precision.HIGHEST

def position_index():
    span_size = 2 * GRID - 1
    rows_y, cols_x = np.meshgrid(np.arange(GRID), np.arange(GRID), indexing='ij')
    rows_y = rows_y.reshape(-1)
    cols_x = cols_x.reshape(-1)
    core_index = (rows_y[:, None] - rows_y[None, :] + GRID - 1) * span_size + (cols_x[:, None] - cols_x[None, :] + GRID - 1)
    index_table = np.zeros((SEQ, SEQ), np.int32)
    index_table[1:, 1:] = core_index
    index_table[0, :] = span_size * span_size
    index_table[:, 0] = span_size * span_size + 1
    index_table[0, 0] = span_size * span_size + 2
    return index_table

def layer_norm(residual, norm_gain, norm_shift):
    average = lax.optimization_barrier(jnp.mean(residual, axis=-1, keepdims=True))
    centred = residual - average
    variance = lax.optimization_barrier(jnp.mean(centred * centred, axis=-1, keepdims=True))
    return centred * lax.rsqrt(variance + EPSILON) * norm_gain + norm_shift

def attention_block(residual, weights, bias_table, norm_gain, norm_shift, scale_vec):
    batch_size = residual.shape[0]
    inv_root = 1.0 / math.sqrt(D // HEADS)
    normed = low(layer_norm(residual, norm_gain, norm_shift))
    packed = low_back(low(jnp.einsum('bsd,de->bse', normed, weights[:, :3 * D], precision=HIGH)))
    split_heads = packed.reshape(batch_size, SEQ, 3, HEADS, D // HEADS)
    query_part = split_heads[:, :, 0]
    key_part = split_heads[:, :, 1]
    value_part = split_heads[:, :, 2]
    pos_bias = jnp.transpose(bias_table[jnp.asarray(position_index())], (2, 0, 1))
    scores = low_back(jnp.einsum('bqhd,bkhd->bhqk', query_part, key_part, precision=HIGH) * inv_root + pos_bias[None])
    row_peak = lax.optimization_barrier(jnp.max(scores, axis=-1, keepdims=True))
    exp_scores = jnp.exp(scores - row_peak)
    attn_probs = low(exp_scores / lax.optimization_barrier(jnp.sum(exp_scores, axis=-1, keepdims=True)))
    mixed_heads = jnp.einsum('bhqk,bkhd->bqhd', attn_probs, value_part, precision=HIGH).reshape(batch_size, SEQ, D)
    mixed_heads = low_back(low(mixed_heads))
    projected = low_back(jnp.einsum('bsd,de->bse', mixed_heads, weights[:, 3 * D:], precision=HIGH))
    return scale_vec * projected

def dense_block(residual, weights, down_proj, norm_gain, norm_shift, scale_vec):
    normed = low(layer_norm(residual, norm_gain, norm_shift))
    pre_act = low_back(jnp.einsum('bsd,df->bsf', normed, weights, precision=HIGH))
    activated = low(jax.nn.gelu(pre_act, approximate=False))
    projected = low_back(jnp.einsum('bsf,fd->bsd', activated, down_proj, precision=HIGH))
    return scale_vec * projected

def group_forward(params, group):
    w_first, w_second, norm_gain, norm_shift, layer_scale, rel_table, mask_token = params
    started, masked, valid = group
    residual = low_back(jnp.where((masked == 1)[:, :, None], mask_token[None, None, :], started))
    row_weight = valid[:, None]
    branch_sums = []
    resid_sums = []
    for section_number in range(N_SECTION):
        if section_number % 2 == 0:
            branch = attention_block(residual, w_first[section_number], rel_table[section_number // 2], norm_gain[section_number], norm_shift[section_number], layer_scale[section_number])
        else:
            branch = dense_block(residual, w_first[section_number], w_second[section_number // 2], norm_gain[section_number], norm_shift[section_number], layer_scale[section_number])
        residual = residual + branch
        branch_sums.append(jnp.sum(row_weight * lax.optimization_barrier(jnp.sum(branch * branch, axis=-1))))
        resid_sums.append(jnp.sum(row_weight * lax.optimization_barrier(jnp.sum(residual * residual, axis=-1))))
        if section_number < N_SECTION - 1:
            residual = low_back(low(residual))
    result = residual * valid[:, None, None]
    return (result, jnp.stack([jnp.stack(branch_sums), jnp.stack(resid_sums)], axis=1))

def reference(tokens, masked, live_images, mask_token, norm_gain, norm_shift, w_first, w_second, layer_scale, rel_table, cotangent):
    per_group = N_SECTION * IMG_Q
    image_ids = jnp.arange(IMAGES, dtype=jnp.int32)
    owners = image_ids // per_group
    slots = image_ids % per_group
    valid = (slots < live_images[owners]).astype(jnp.float32)
    params = tuple((item.astype(jnp.float32) for item in (w_first, w_second, norm_gain, norm_shift, layer_scale, rel_table, mask_token)))
    started = tokens.astype(jnp.float32).reshape(N_DP, per_group, SEQ, D)
    mask_groups = masked.reshape(N_DP, per_group, SEQ)
    valid_groups = valid.reshape(N_DP, per_group)
    stepper = jax.checkpoint(group_forward)

    def forward(params, started):

        def one_group(group):
            return stepper(params, group)
        results, sums = lax.map(one_group, (started, mask_groups, valid_groups))
        return (results, lax.optimization_barrier(jnp.sum(sums, axis=0)))
    results, back_fn, sums = jax.vjp(forward, params, started, has_aux=True)
    cot_groups = cotangent.astype(jnp.float32).reshape(N_DP, per_group, SEQ, D)
    param_grads, token_grads = back_fn(cot_groups)
    first_g, second_g, gain_g, shift_g, scale_g, table_g, mask_g = param_grads
    token_total = jnp.sum(live_images).astype(jnp.float32) * SEQ * D
    rms_out = jnp.sqrt(sums / token_total)
    block_out = results.reshape(IMAGES, SEQ, D).astype(jnp.bfloat16)
    tokens_grad = token_grads.reshape(IMAGES, SEQ, D).astype(jnp.bfloat16)
    return (block_out, tokens_grad, first_g, second_g, gain_g, shift_g, scale_g, table_g, mask_g, rms_out)
```

```python
import functools
import math

import jax
import jax.numpy as jnp
import numpy as np
from jax import lax
from jax.experimental import pallas as pl
from jax.experimental.pallas import tpu as pltpu
from jax.sharding import PartitionSpec as P

SEQ, ROWS, KEYS = 197, 208, 256
D, FF, HEADS, GRID = 768, 3072, 12, 14
SPAN = 2 * GRID - 1
EPSILON = 1e-06
INV_ROOT = 0.125
INV_ROOT_TWO_PI = 0.3989422804014327
F32, BF16 = jnp.float32, jnp.bfloat16
PIECES = (3, 2, 4, 4, 4, 16, 384)


def mm(a, b):
    return lax.dot_general(a, b, (((1,), (0,)), ((), ())), preferred_element_type=F32)


def mm_nt(a, b):
    return lax.dot_general(a, b, (((1,), (1,)), ((), ())), preferred_element_type=F32)


def mm_tn(a, b):
    return lax.dot_general(a, b, (((0,), (0,)), ((), ())), preferred_element_type=F32)


def lanes(start, size):
    return pl.ds(pl.multiple_of(start, 128), size)


def token_offsets():
    patch = np.arange(SEQ - 1)
    return (patch // GRID) * SPAN + patch % GRID


def selectors():
    forward = np.zeros((384, KEYS), np.float32)
    backward = np.zeros((KEYS, 384), np.float32)
    offsets = token_offsets()
    forward[offsets, np.arange(1, SEQ)] = 1.0
    backward[np.arange(1, SEQ), offsets[-1] - offsets] = 1.0
    return jnp.asarray(forward, BF16), jnp.asarray(backward, BF16)


def centre(h):
    average = jnp.mean(h, axis=-1, keepdims=True)
    centred = h - average
    inv_std = lax.rsqrt(jnp.mean(centred * centred, axis=-1, keepdims=True) + EPSILON)
    return centred * inv_std, inv_std


def gelu_pair(u):
    size = jnp.abs(u)
    t = 1.0 / (1.0 + 0.23164189 * size)
    bell = jnp.exp(-0.5 * u * u)
    poly = t * (
        0.127414796
        + t * (-0.142248368 + t * (0.7107068705 + t * (-0.7265760135 + t * 0.5307027145)))
    )
    tail = poly * bell
    phi = jnp.where(u >= 0.0, 1.0 - tail, tail)
    return u * phi, phi + u * bell * INV_ROOT_TWO_PI


def half_mask(rows, parity):
    lane = lax.broadcasted_iota(jnp.int32, (rows, 128), 1)
    return (lane < 64) if parity == 0 else (lane >= 64)


def keep_half(block, parity):
    return jnp.where(half_mask(block.shape[0], parity), block, jnp.zeros_like(block))


class Body:
    def __init__(self, **refs):
        self.__dict__.update(refs)

    def expand_bias(self, layer):
        def head(index, _):
            base = jnp.broadcast_to(self.table[pl.ds(layer * HEADS + index, 1), :], (16, 768))
            base = pltpu.roll(base, 404, 1, stride=1, stride_axis=0)
            for yi in range(GRID):
                turned = pltpu.roll(base, SPAN * yi, 1) if yi else base
                self.unfold[1 + GRID * yi : 1 + GRID * (yi + 1), :] = turned[:GRID, :384]
            spread = self.unfold[...]
            high = spread.astype(BF16)
            low = (spread - high.astype(F32)).astype(BF16)
            select = self.select_forward[...]
            grid = mm(high, select) + mm(low, select)
            row = lax.broadcasted_iota(jnp.int32, (ROWS, KEYS), 0)
            column = lax.broadcasted_iota(jnp.int32, (ROWS, KEYS), 1)
            corner = self.corner[pl.ds(layer * HEADS + index, 1), :]
            grid = jnp.where(row == 0, corner[:, 0:1], grid)
            grid = jnp.where(column == 0, corner[:, 1:2], grid)
            grid = jnp.where((row == 0) & (column == 0), corner[:, 2:3], grid)
            self.bias[index] = jnp.where(column >= SEQ, -1e30, grid)
            return 0

        lax.fori_loop(0, HEADS, head, 0)

    def normed(self, s):
        scaled, _ = centre(self.h[s].astype(F32))
        gain = self.gain[s : s + 1, :]
        shift = self.shift[s : s + 1, :]
        self.n[...] = (scaled * gain + shift).astype(BF16)

    def finish(self, s, left, right_of):
        real = (lax.broadcasted_iota(jnp.int32, (ROWS, 1), 0) < SEQ).astype(F32) * self.valid[0:1, 0:1]

        def block(j, _):
            columns = lanes(j * 256, 256)
            projected = mm(left[...], right_of(columns))
            branch = self.scale[s : s + 1, columns] * projected
            result = self.h[s, :, columns].astype(F32) + branch
            self.p[s, :, columns] = projected.astype(BF16)
            self.small[2 * s : 2 * s + 1, columns] = jnp.sum(branch * branch * real, axis=0, keepdims=True)
            self.small[2 * s + 1 : 2 * s + 2, columns] = jnp.sum(result * result * real, axis=0, keepdims=True)
            if s < 3:
                self.h[s + 1, :, columns] = result.astype(BF16)
            else:
                self.block_out[:, columns] = (result * self.valid[0:1, 0:1]).astype(BF16)
            return 0

        lax.fori_loop(0, 3, block, 0)

    def attend_forward(self, s):
        layer = s // 2
        self.normed(s)

        def project(j, _):
            columns = lanes(j * 256, 256)
            self.qkv[layer, :ROWS, columns] = mm(self.n[...], self.w[s, :, columns]).astype(BF16)
            return 0

        lax.fori_loop(0, 9, project, 0)
        self.qkv[layer, ROWS:, :] = jnp.zeros((KEYS - ROWS, 2304), BF16)

        def pair(j, _):
            q = self.qkv[layer, :ROWS, lanes(j * 128, 128)]
            k = self.qkv[layer, :, lanes(768 + j * 128, 128)]
            v = self.qkv[layer, :, lanes(1536 + j * 128, 128)]
            mixed = jnp.zeros((ROWS, 128), F32)
            for parity in range(2):
                scores = mm_nt(keep_half(q, parity), k) * INV_ROOT + self.bias[2 * j + parity]
                peak = jnp.max(scores, axis=-1, keepdims=True)
                exps = jnp.exp(scores - peak)
                total = jnp.sum(exps, axis=-1, keepdims=True)
                probs = (exps * (1.0 / total)).astype(BF16)
                self.probs[layer, 2 * j + parity] = probs
                mixed = mixed + mm(probs, keep_half(v, parity))
            self.o[layer, :, lanes(j * 128, 128)] = mixed.astype(BF16)
            return 0

        lax.fori_loop(0, HEADS // 2, pair, 0)
        self.finish(s, self.o.at[layer], lambda c: self.w[s, :, pl.ds(pl.multiple_of(2304 + c.start, 128), 256)])

    def dense_forward(self, s):
        layer = s // 2
        self.normed(s)

        def up(j, _):
            columns = lanes(j * 256, 256)
            u = mm(self.n[...], self.w[s, :, columns])
            act, slope = gelu_pair(u)
            self.a[layer, :, columns] = act.astype(BF16)
            self.slope[layer, :, columns] = slope.astype(BF16)
            return 0

        lax.fori_loop(0, 12, up, 0)
        self.finish(s, self.a.at[layer], lambda c: self.w2[layer, :, c])

    def enter(self, s):
        g = self.g[...].astype(F32)
        row = 8 + 3 * s
        self.small[row : row + 1, :] = jnp.sum(g * self.p[s].astype(F32), axis=0, keepdims=True)
        self.dp[...] = (g * self.scale[s : s + 1, :]).astype(BF16)
        self.normed(s)

    def leave(self, s, grad, width):
        def block(j, _):
            rows = pl.ds(pl.multiple_of(j * 256, 256), 256)
            self.dn[:, lanes(j * 256, 256)] = mm_nt(grad[:, :width], self.w[s, rows, :width])
            return 0

        lax.fori_loop(0, 3, block, 0)
        scaled, inv_std = centre(self.h[s].astype(F32))
        dn = self.dn[...]
        row = 8 + 3 * s
        self.small[row + 1 : row + 2, :] = jnp.sum(dn * scaled, axis=0, keepdims=True)
        self.small[row + 2 : row + 3, :] = jnp.sum(dn, axis=0, keepdims=True)
        e = dn * self.gain[s : s + 1, :]
        mean_e = jnp.mean(e, axis=-1, keepdims=True)
        mean_ex = jnp.mean(e * scaled, axis=-1, keepdims=True)
        g = self.g[...].astype(F32) + inv_std * (e - mean_e - scaled * mean_ex)
        self.g[...] = g.astype(BF16)

    def store_first(self, stage, block, grad):
        c, a3 = block // 4, block % 4
        low = grad.astype(BF16)
        for rb in range(16):
            for route in range(3):
                first = rb * 48 + route * 16
                stage[route, c, rb // 4, rb % 4, a3] = low[first : first + 16, :]

    def first_grads(self, stage, left, right, lo, hi, shift):
        def block(j, _):
            self.store_first(stage, j, mm_tn(left[...], right[:, lanes((j - shift) * 384, 384)]))
            return 0

        lax.fori_loop(lo, hi, block, 0)

    def second_grads(self, stage, layer):
        def block(q, _):
            z, x_high = q // 2, q % 2
            grad = mm_tn(self.a[layer, :, lanes(q * 384, 384)], self.dp[...])
            for x_low in range(2):
                x = 2 * x_high + x_low
                for c in range(2):
                    for y in range(4):
                        top = ((x_low * 2 + c) * 4 + y) * 24
                        part = jnp.concatenate(
                            [grad[top : top + 24, :384], grad[top : top + 24, 384:]], axis=0
                        ).astype(BF16)
                        stage[0, c, x, y, z] = part[0:16]
                        stage[1, c, y, z, x] = part[16:32]
                        stage[2, c, z, x, y] = part[32:48]
            return 0

        lax.fori_loop(0, 8, block, 0)

    def dense_backward(self, s, stage_first, stage_second):
        layer = s // 2
        self.enter(s)
        self.second_grads(stage_second, layer)

        def down(j, _):
            columns = lanes(j * 256, 256)
            rows = pl.ds(pl.multiple_of(j * 256, 256), 256)
            da = mm_nt(self.dp[...], self.w2[layer, rows, :])
            self.du[:, columns] = (da * self.slope[layer, :, columns].astype(F32)).astype(BF16)
            return 0

        lax.fori_loop(0, 12, down, 0)
        self.first_grads(stage_first, self.n, self.du, 0, 8, 0)
        self.leave(s, self.du, FF)

    def attend_backward(self, s, stage):
        layer = s // 2
        self.enter(s)
        self.first_grads(stage, self.o.at[layer], self.dp, 6, 8, 6)

        def back(j, _):
            rows = pl.ds(pl.multiple_of(j * 256, 256), 256)
            self.do[:, lanes(j * 256, 256)] = mm_nt(self.dp[...], self.w[s, rows, 2304:]).astype(BF16)
            return 0

        lax.fori_loop(0, 3, back, 0)

        def pair(j, _):
            q = self.qkv[layer, :ROWS, lanes(j * 128, 128)]
            k = self.qkv[layer, :, lanes(768 + j * 128, 128)]
            v = self.qkv[layer, :, lanes(1536 + j * 128, 128)]
            do = self.do[:, lanes(j * 128, 128)]
            dq = jnp.zeros((ROWS, 128), F32)
            dk = jnp.zeros((KEYS, 128), F32)
            dv = jnp.zeros((KEYS, 128), F32)
            for parity in range(2):
                do_half = keep_half(do, parity)
                probs = self.probs[layer, 2 * j + parity]
                wide = probs.astype(F32)
                d_probs = mm_nt(do_half, v)
                inner = jnp.sum(d_probs * wide, axis=-1, keepdims=True)
                d_scores = (wide * (d_probs - inner)).astype(BF16)
                dv = dv + mm_tn(probs, do_half)
                dq = dq + mm(d_scores, keep_half(k, parity))
                dk = dk + mm_tn(d_scores, keep_half(q, parity))
                self.fold_bias(layer, 2 * j + parity, d_scores)
            self.du[:, lanes(j * 128, 128)] = (dq * INV_ROOT).astype(BF16)
            self.du[:, lanes(768 + j * 128, 128)] = (dk[:ROWS] * INV_ROOT).astype(BF16)
            self.du[:, lanes(1536 + j * 128, 128)] = dv[:ROWS].astype(BF16)
            return 0

        lax.fori_loop(0, HEADS // 2, pair, 0)
        self.first_grads(stage, self.n, self.du, 0, 6, 0)
        self.leave(s, self.du, 2304)

    def fold_bias(self, layer, head, d_scores):
        self.fold[:, :384] = mm(d_scores, self.select_backward[...])
        total = self.fold[1:17, :]
        for yi in range(1, GRID):
            total = total + pltpu.roll(self.fold[1 + GRID * yi : 17 + GRID * yi, :], SPAN * yi, 1)
        row = lax.broadcasted_iota(jnp.int32, (16, 768), 0)
        total = jnp.where(row < GRID, total, 0.0)
        total = pltpu.roll(total, 0, 1, stride=1, stride_axis=0)
        total = jnp.sum(total, axis=0, keepdims=True)
        wide = d_scores.astype(F32)
        corner = wide[0:1, 0:1]
        top = jnp.sum(wide[0:1, :], axis=1, keepdims=True) - corner
        side = jnp.sum(wide[:, 0:1], axis=0, keepdims=True) - corner
        lane = lax.broadcasted_iota(jnp.int32, (1, 768), 1)
        total = jnp.where(lane == 729, top, total)
        total = jnp.where(lane == 730, side, total)
        total = jnp.where(lane == 731, corner, total)
        self.small[pl.ds(24 + layer * HEADS + head, 1), :] = total


def layers_kernel(
    h0, cotangent, masked, valid, w_hbm, w2_hbm, gain, shift, scale, table, corner, select_f, select_b,
    block_out, tokens_grad, grads_hbm, small,
    w, w2, h, qkv, probs, o, a, slope, p, n, bias, unfold, fold, du, dn, dp, do, g, stage,
    load_sems, store_sems,
):
    body = Body(
        valid=valid, gain=gain, shift=shift, scale=scale, table=table, corner=corner,
        select_forward=select_f, select_backward=select_b, block_out=block_out, small=small,
        w=w, w2=w2, h=h, qkv=qkv, probs=probs, o=o, a=a, slope=slope, p=p, n=n, bias=bias,
        unfold=unfold, fold=fold, du=du, dn=dn, dp=dp, do=do, g=g,
    )
    loads = []
    for s in range(4):
        loads.append(pltpu.make_async_copy(w_hbm.at[s], w.at[s], load_sems.at[s]))
    for layer in range(2):
        loads.append(pltpu.make_async_copy(w2_hbm.at[layer], w2.at[layer], load_sems.at[4 + layer]))
    for load in loads:
        load.start()
    unfold[...] = jnp.zeros_like(unfold)
    fold[...] = jnp.zeros_like(fold)
    h[0] = h0[...]
    for s in range(4):
        if s % 2 == 0:
            body.expand_bias(s // 2)
            loads[s].wait()
            body.attend_forward(s)
        else:
            loads[s].wait()
            loads[4 + s // 2].wait()
            body.dense_forward(s)
    g[...] = (cotangent[...].astype(F32) * valid[0:1, 0:1]).astype(BF16)
    stores = {}

    def store(order, tensor):
        stores[order] = pltpu.make_async_copy(stage.at[order % 2], grads_hbm.at[tensor], store_sems.at[order % 2])
        stores[order].start()

    def free(order):
        if order - 2 in stores:
            stores.pop(order - 2).wait()

    order = 0
    for s in (3, 2, 1, 0):
        if s % 2 == 1:
            free(order), free(order + 1)
            body.dense_backward(s, stage.at[(order + 1) % 2], stage.at[order % 2])
            store(order, 4 + s // 2)
            store(order + 1, s)
            order += 2
        else:
            free(order)
            body.attend_backward(s, stage.at[order % 2])
            store(order, s)
            order += 1
    grad = g[...].astype(F32)
    here = masked[:, 0:1]
    tokens_grad[...] = (grad * (1.0 - here)).astype(BF16)
    small[20:21, :] = jnp.sum(grad * here, axis=0, keepdims=True)
    small[21:24, :] = jnp.zeros((3, 768), F32)
    for left in list(stores.values()):
        left.wait()


def layers(h0, cotangent, masked, valid, w_all, w2, gain, shift, scale, table, corner):
    select_f, select_b = selectors()
    vm = pl.BlockSpec(memory_space=pltpu.VMEM)
    hbm = pl.BlockSpec(memory_space=pl.ANY)
    V = pltpu.VMEM
    return pl.pallas_call(
        layers_kernel,
        out_shape=(
            jax.ShapeDtypeStruct((ROWS, D), BF16),
            jax.ShapeDtypeStruct((ROWS, D), BF16),
            jax.ShapeDtypeStruct((6,) + PIECES, BF16),
            jax.ShapeDtypeStruct((48, D), F32),
        ),
        in_specs=[vm, vm, vm, vm, hbm, hbm] + [vm] * 7,
        out_specs=(vm, vm, hbm, vm),
        scratch_shapes=[
            V((4, D, FF), BF16), V((2, FF, D), BF16), V((4, ROWS, D), BF16), V((2, KEYS, 2304), BF16),
            V((2, HEADS, ROWS, KEYS), BF16), V((2, ROWS, D), BF16), V((2, ROWS, FF), BF16), V((2, ROWS, FF), BF16),
            V((4, ROWS, D), BF16), V((ROWS, D), BF16), V((HEADS, ROWS, KEYS), F32), V((ROWS, 384), F32),
            V((ROWS, D), F32), V((ROWS, FF), BF16), V((ROWS, D), F32), V((ROWS, D), BF16), V((ROWS, D), BF16),
            V((ROWS, D), BF16), V((2,) + PIECES, BF16),
            pltpu.SemaphoreType.DMA((6,)), pltpu.SemaphoreType.DMA((2,)),
        ],
        compiler_params=pltpu.CompilerParams(vmem_limit_bytes=64 * 2**20),
    )(h0, cotangent, masked, valid, w_all, w2, gain, shift, scale, table, corner, select_f, select_b)


MESH = pl.DeviceIdType.MESH
AXES = ("x", "y", "z")
ROUTES = (("x", "y", "z"), ("y", "z", "x"), ("z", "x", "y"))
ORDER = (5, 3, 2, 4, 1, 0)


class Place:
    def __init__(self):
        dp = lax.axis_index("dp")
        self.at = {"z": dp // 8, "x": (dp // 2) % 4, "c": dp % 2, "y": lax.axis_index("section")}

    def go(self, axis, step):
        at = dict(self.at)
        at[axis] = (at[axis] + step) % (2 if axis == "c" else 4)
        return ((at["z"] * 4 + at["x"]) * 2 + at["c"], at["y"])

    def index(self, axis, step=0):
        return (self.at[axis] + step) % 4


def meet(place):
    barrier = pltpu.get_barrier_semaphore()
    count = 0
    for axis in AXES:
        for step in (1, 2, 3):
            pl.semaphore_signal(barrier, inc=1, device_id=place.go(axis, step), device_id_type=MESH)
            count += 1
    pl.semaphore_signal(barrier, inc=1, device_id=place.go("c", 1), device_id_type=MESH)
    pl.semaphore_wait(barrier, count + 1)


class Reduce:
    def __init__(self, place, own, pair, far, line, line_in, spot, spot_in, first_out, second_out, sems):
        self.place, self.own, self.pair, self.far, self.line, self.line_in = place, own, pair, far, line, line_in
        self.spot, self.spot_in, self.first_out, self.second_out, self.sems = spot, spot_in, first_out, second_out, sems
        self.flying = {}

    def send(self, key, src, dst, number, k, device):
        copy = pltpu.make_async_remote_copy(
            src_ref=src, dst_ref=dst, send_sem=self.sems.at[0, k, number], recv_sem=self.sems.at[1, k, number],
            device_id=device, device_id_type=MESH,
        )
        copy.start()
        self.flying[key] = copy

    def swap(self, k, theirs):
        for r in range(3):
            self.send(("c", k, r), theirs(r), self.pair.at[k, r], r, k, self.place.go("c", 1))

    def first(self, k):
        place = self.place
        for r, (axis, _, _) in enumerate(ROUTES):
            self.flying[("c", k, r)].wait_recv()

            def add(a1, _):
                self.own[k, r, a1] = (self.own[k, r, a1].astype(F32) + self.pair[k, r, a1].astype(F32)).astype(BF16)
                return 0

            lax.fori_loop(0, 4, add, 0)
            own, far = self.own.at[k, r], self.far.at[k, r]
            across, ahead, behind = place.index(axis, 2), place.index(axis, 1), place.index(axis, 3)
            up, down = place.go(axis, 1), place.go(axis, 3)
            base = 3 + 6 * r
            self.send(("fa", k, r), own.at[across, 0:2], far.at[0], base, k, up)
            self.send(("fb", k, r), own.at[across, 2:4], far.at[1], base + 1, k, down)
            self.send(("db", k, r), own.at[ahead, 2:4], far.at[2], base + 2, k, up)
            self.send(("da", k, r), own.at[behind, 0:2], far.at[3], base + 3, k, down)

    def merge(self, k):
        place = self.place
        for r, (axis, _, _) in enumerate(ROUTES):
            own, far = self.own.at[k, r], self.far.at[k, r]
            ahead, behind = place.index(axis, 1), place.index(axis, 3)
            base = 3 + 6 * r
            self.flying[("fa", k, r)].wait_recv()
            far[0] = (far[0].astype(F32) + own[ahead, 0:2].astype(F32)).astype(BF16)
            self.send(("ma", k, r), far.at[0], far.at[4], base + 4, k, place.go(axis, 1))
            self.flying[("fb", k, r)].wait_recv()
            far[1] = (far[1].astype(F32) + own[behind, 2:4].astype(F32)).astype(BF16)
            self.send(("mb", k, r), far.at[1], far.at[5], base + 5, k, place.go(axis, 3))

    def second(self, k):
        place = self.place
        for r, (axis, nxt, _) in enumerate(ROUTES):
            for name in ("db", "da", "ma", "mb"):
                self.flying[(name, k, r)].wait_recv()
            own, far = self.own.at[k, r], self.far.at[k, r]
            me = place.index(axis)
            low = own[me, 0:2].astype(F32) + far[4].astype(F32) + far[3].astype(F32)
            high = own[me, 2:4].astype(F32) + far[2].astype(F32) + far[5].astype(F32)
            line, line_in = self.line.at[k, r], self.line_in.at[k, r]
            line[0:2] = low.astype(BF16)
            line[2:4] = high.astype(BF16)
            for step in (1, 2, 3):
                self.send(("s", k, r, step), line.at[place.index(nxt, step)], line_in.at[step - 1], 21 + 3 * r + step - 1, k, place.go(nxt, step))

    def third(self, k):
        place = self.place
        for r, (_, axis, nxt) in enumerate(ROUTES):
            line, line_in, spot, spot_in = self.line.at[k, r], self.line_in.at[k, r], self.spot.at[k, r], self.spot_in.at[k, r]
            total = line[place.index(axis)].astype(F32)
            for step in (1, 2, 3):
                self.flying[("s", k, r, step)].wait_recv()
                total = total + line_in[step - 1].astype(F32)
            spot[...] = total.astype(BF16)
            for step in (1, 2, 3):
                self.send(("t", k, r, step), spot.at[place.index(nxt, step)], spot_in.at[step - 1], 30 + 3 * r + step - 1, k, place.go(nxt, step))

    def close(self, k, tensor):
        place = self.place
        for r, (_, _, axis) in enumerate(ROUTES):
            spot, spot_in = self.spot.at[k, r], self.spot_in.at[k, r]
            total = spot[place.index(axis)].astype(F32)
            for step in (1, 2, 3):
                self.flying[("t", k, r, step)].wait_recv()
                total = total + spot_in[step - 1].astype(F32)
            if tensor < 4:
                self.first_out[tensor, r] = total.astype(BF16)
            elif r == 0:
                self.second_out[tensor - 4, 0:16, :384] = total
            elif r == 1:
                self.second_out[tensor - 4, 16:24, :384] = total[0:8]
                self.second_out[tensor - 4, 0:8, 384:] = total[8:16]
            else:
                self.second_out[tensor - 4, 8:24, 384:] = total

    def drain(self):
        for copy in self.flying.values():
            copy.wait_send()


class Totals:
    def __init__(self, place, part, bufs, sems):
        self.place, self.part, self.bufs, self.sems = place, part, bufs, sems
        self.copies = []

    def send(self, src, dst, number, device):
        copy = pltpu.make_async_remote_copy(
            src_ref=src, dst_ref=dst, send_sem=self.sems.at[0, number], recv_sem=self.sems.at[1, number],
            device_id=device, device_id_type=MESH,
        )
        copy.start()
        self.copies.append(copy)
        return copy

    def start(self, small):
        me = self.place.at["c"]
        self.small = small
        self.now = [self.send(small.at[1 - me], self.bufs.at[0, 0], 0, self.place.go("c", 1))]

    def step(self, number):
        place, me = self.place, self.place.at["c"]
        for copy in self.now:
            copy.wait_recv()
        if number == 0:
            self.part[...] = self.small[me] + self.bufs[0, 0]
        else:
            axis = AXES[number - 1]
            self.bufs[number, place.at[axis]] = self.part[...]
            self.part[...] = (self.bufs[number, 0] + self.bufs[number, 1]) + (self.bufs[number, 2] + self.bufs[number, 3])
        if number < 3:
            axis = AXES[number]
            self.now = [
                self.send(self.part, self.bufs.at[number + 1, place.at[axis]], 1 + 3 * number + step - 1, place.go(axis, step))
                for step in (1, 2, 3)
            ]
            for copy in self.now:
                copy.wait_send()
        else:
            self.now = [self.send(self.part, self.bufs.at[0, 1], 10, place.go("c", 1))]

    def close(self, out):
        me = self.place.at["c"]
        for copy in self.now:
            copy.wait_recv()
        out[me] = self.part[...]
        out[1 - me] = self.bufs[0, 1]
        self.copies[0].wait_send()
        self.copies[-1].wait_send()


def reduce_kernel(
    grads, small, first_out, second_out, totals, own, pair, far, line, line_in, spot, spot_in, part, bufs,
    load_sems, sems, small_sems,
):
    place = Place()
    meet(place)
    me = place.at["c"]
    reduce = Reduce(place, own, pair, far, line, line_in, spot, spot_in, first_out, second_out, sems)
    sums = Totals(place, part, bufs, small_sems)
    sums.start(small)
    loads = []
    for k, t in enumerate(ORDER):
        loads.append([pltpu.make_async_copy(grads.at[t, r, me], own.at[k, r], load_sems.at[k, r]) for r in range(3)])
        for load in loads[-1]:
            load.start()
    stages = 5
    reduce.swap(0, lambda r: grads.at[ORDER[0], r, 1 - me])
    for time in range(6 + stages - 1):
        if time + 1 < 6:
            reduce.swap(time + 1, lambda r: grads.at[ORDER[time + 1], r, 1 - me])
        for stage in reversed(range(stages)):
            k = time - stage
            if not 0 <= k < 6:
                continue
            if stage == 0:
                for load in loads[k]:
                    load.wait()
                reduce.first(k)
            elif stage == 1:
                reduce.merge(k)
            elif stage == 2:
                reduce.second(k)
            elif stage == 3:
                reduce.third(k)
            else:
                reduce.close(k, ORDER[k])
        if time < 4:
            sums.step(time)
        elif time == 4:
            sums.close(totals)
    reduce.drain()


def reduce_all(grads, small):
    vm = pl.BlockSpec(memory_space=pltpu.VMEM)
    hbm = pl.BlockSpec(memory_space=pl.ANY)
    V = pltpu.VMEM
    return pl.pallas_call(
        reduce_kernel,
        out_shape=(
            jax.ShapeDtypeStruct((4, 3, 16, 384), BF16),
            jax.ShapeDtypeStruct((2, 24, D), F32),
            jax.ShapeDtypeStruct((2, 24, D), F32),
        ),
        in_specs=[hbm, vm],
        out_specs=(vm, vm, vm),
        scratch_shapes=[
            V((6, 3, 4, 4, 4, 16, 384), BF16), V((6, 3, 4, 4, 4, 16, 384), BF16), V((6, 3, 6, 2, 4, 16, 384), BF16),
            V((6, 3, 4, 4, 16, 384), BF16), V((6, 3, 3, 4, 16, 384), BF16),
            V((6, 3, 4, 16, 384), BF16), V((6, 3, 3, 16, 384), BF16),
            V((24, D), F32), V((4, 4, 24, D), F32),
            pltpu.SemaphoreType.DMA((6, 3)), pltpu.SemaphoreType.DMA((2, 6, 39)), pltpu.SemaphoreType.DMA((2, 11)),
        ],
        compiler_params=pltpu.CompilerParams(collective_id=1, has_side_effects=True, vmem_limit_bytes=64 * 2**20),
    )(grads, small)


class Spread:
    def __init__(self, place, sems):
        self.place, self.sems = place, sems
        self.sent = []

    def send(self, number, src, dst, device):
        copy = pltpu.make_async_remote_copy(
            src_ref=src, dst_ref=dst, send_sem=self.sems.at[0, number], recv_sem=self.sems.at[1, number],
            device_id=device, device_id_type=MESH,
        )
        copy.start()
        self.sent.append(copy)

    def wait(self, number, ref):
        pltpu.make_async_remote_copy(
            src_ref=ref, dst_ref=ref, send_sem=self.sems.at[0, number], recv_sem=self.sems.at[1, number],
            device_id=self.place.go("c", 1), device_id_type=MESH,
        ).wait_recv()

    def drain(self):
        for copy in self.sent:
            copy.wait_send()


GATHER_MESSAGES = 63


class Gather(Spread):
    def __init__(self, place, source, full, sems):
        super().__init__(place, sems)
        self.source, self.full = source, full

    def rows(self, route, step, sub=None):
        top = (0 if route == "x" else 384) + self.place.index(route, step) * 96 + self.place.at["c"] * 48
        if sub is None:
            return pl.ds(pl.multiple_of(top, 16), 48)
        return pl.ds(pl.multiple_of(top + 16 * sub, 16), 16)

    def ref(self, rel, route, step, sub=None):
        return self.full.at[self.place.index("y", rel), self.rows(route, step, sub)]

    @staticmethod
    def along_y(rel, route):
        return 2 * (rel - 1) + (route == "z")

    @staticmethod
    def in_plane(rel, route, kind):
        return 6 + 5 * (2 * (rel - 1) + (route == "z")) + kind

    @staticmethod
    def across(rel, route, step):
        return 36 + 4 * (2 * (rel - 1) + (route == "z")) + step

    def begin(self):
        for route in ("x", "z"):
            mine = self.source.at[self.rows(route, 0)]
            for step in (1, 3):
                self.send(self.along_y(4 - step, route), mine, self.ref(0, route, 0), self.place.go("y", step))

    def arrive(self, rel):
        for route in ("x", "z"):
            piece = self.ref(rel, route, 0)
            self.wait(self.along_y(rel, route), piece)
            if (rel, route) == (3, "x"):
                self.send(self.along_y(2, route), piece, piece, self.place.go("y", 1))
            if (rel, route) == (1, "z"):
                self.send(self.along_y(2, route), piece, piece, self.place.go("y", 3))
            for kind, step in ((0, 1), (1, 3)):
                self.send(self.in_plane(rel, route, kind), piece, piece, self.place.go(route, step))
            self.send(self.across(rel, route, 0), piece, piece, self.place.go("c", 1))

    def turn(self, rel):
        place = self.place
        for route in ("x", "z"):
            for kind, step in ((0, 3), (1, 1)):
                piece = self.ref(rel, route, step)
                self.wait(self.in_plane(rel, route, kind), piece)
                self.send(self.across(rel, route, step), piece, piece, place.go("c", 1))
            clockwise = 1 - 2 * place.at["c"]
            for sub, way in ((0, 1), (1, clockwise), (2, -1)):
                piece = self.ref(rel, route, 4 - way, sub)
                self.send(self.in_plane(rel, route, 2 + sub), piece, piece, place.go(route, 4 + way))

    def end(self, rel):
        for route in ("x", "z"):
            for sub in range(3):
                self.wait(self.in_plane(rel, route, 2 + sub), self.ref(rel, route, 2, sub))
            piece = self.ref(rel, route, 2)
            self.send(self.across(rel, route, 2), piece, piece, self.place.go("c", 1))

    def settle(self, rel):
        other = 1 - self.place.at["c"]
        for route in ("x", "z"):
            for step in range(4):
                top = (0 if route == "x" else 384) + self.place.index(route, step) * 96 + other * 48
                self.wait(self.across(rel, route, step), self.full.at[self.place.index("y", rel), pl.ds(pl.multiple_of(top, 16), 48)])


def gather_kernel(source, vec, full, vecs, own_sem, sems):
    place = Place()
    meet(place)
    gather = Gather(place, source, full, sems)
    mine = place.at["y"]
    vecs[mine] = vec[...]
    for step in (1, 2, 3):
        gather.send(59 + step, vec, vecs.at[mine], place.go("y", step))
    own = pltpu.make_async_copy(source, full.at[place.at["y"]], own_sem)
    own.start()
    gather.begin()
    gather.arrive(3)
    gather.arrive(1)
    gather.turn(3)
    gather.turn(1)
    gather.arrive(2)
    gather.end(3)
    gather.end(1)
    gather.turn(2)
    gather.end(2)
    for rel in (3, 1, 2):
        gather.settle(rel)
    for step in (1, 2, 3):
        gather.wait(59 + step, vecs.at[place.index("y", 4 - step)])
    own.wait()
    gather.drain()


def gather_all(source, vec):
    hbm = pl.BlockSpec(memory_space=pl.ANY)
    vm = pl.BlockSpec(memory_space=pltpu.VMEM)
    return pl.pallas_call(
        gather_kernel,
        out_shape=(jax.ShapeDtypeStruct((4, D, FF), BF16), jax.ShapeDtypeStruct((4, 8, D), F32)),
        in_specs=[hbm, vm],
        out_specs=(hbm, vm),
        scratch_shapes=[pltpu.SemaphoreType.DMA, pltpu.SemaphoreType.DMA((2, GATHER_MESSAGES))],
        compiler_params=pltpu.CompilerParams(collective_id=2, has_side_effects=True),
    )(source, vec)


class Share(Spread):
    def __init__(self, place, blocks, pieces, sems):
        super().__init__(place, sems)
        self.blocks, self.pieces = blocks, pieces

    def run(self, own_sem, out, out_sem):
        place, pieces = self.place, self.pieces
        at = place.at
        c, x, y, z = at["c"], at["x"], at["y"], at["z"]
        own = pltpu.make_async_copy(self.blocks.at[y], pieces.at[c, z, x, y], own_sem)
        own.start()
        for step in (1, 2, 3):
            self.send(step - 1, self.blocks.at[place.index("y", step)], pieces.at[c, z, x, y], place.go("y", step))
        own.wait()
        for step in (1, 2, 3):
            self.wait(step - 1, pieces.at[c, z, x, place.index("y", 4 - step)])
        low, high = pl.ds(0, 2), pl.ds(2, 2)
        for step in (1, 2, 3):
            self.send(2 + step, pieces.at[c, z, x, low], pieces.at[c, z, x, low], place.go("x", step))
            self.send(5 + step, pieces.at[c, z, x, high], pieces.at[c, z, x, high], place.go("z", step))
        for step in (1, 2, 3):
            self.wait(2 + step, pieces.at[c, z, place.index("x", 4 - step), low])
            self.wait(5 + step, pieces.at[c, place.index("z", 4 - step), x, high])
        row, column = pieces.at[c, z, :, low], pieces.at[c, :, x, high]
        for step in (1, 3, 2):
            self.send(8 + step, row, row, place.go("z", step))
            self.send(11 + step, column, column, place.go("x", step))
        self.send(15, row, row, place.go("c", 1))
        self.send(16, column, column, place.go("c", 1))
        for step in (1, 3, 2):
            row = pieces.at[c, place.index("z", 4 - step), :, low]
            self.wait(8 + step, row)
            self.send(16 + step, row, row, place.go("c", 1))
            column = pieces.at[c, :, place.index("x", 4 - step), high]
            self.wait(11 + step, column)
            self.send(19 + step, column, column, place.go("c", 1))
        first = pltpu.make_async_copy(pieces.at[c], out.at[c], out_sem)
        first.start()
        self.wait(15, pieces.at[1 - c, z, :, low])
        self.wait(16, pieces.at[1 - c, :, x, high])
        for step in (1, 3, 2):
            self.wait(16 + step, pieces.at[1 - c, place.index("z", 4 - step), :, low])
            self.wait(19 + step, pieces.at[1 - c, :, place.index("x", 4 - step), high])
        first.wait()
        rest = pltpu.make_async_copy(pieces.at[1 - c], out.at[1 - c], out_sem)
        rest.start()
        rest.wait()
        self.drain()


def share_kernel(blocks, out, pieces, own_sem, out_sem, sems):
    place = Place()
    meet(place)
    Share(place, blocks, pieces, sems).run(own_sem, out, out_sem)


def assemble_kernel(first, second, third, out):
    for route, ref in enumerate((first, second, third)):
        for c in range(2):
            for a3 in range(4):
                if route == 0:
                    piece = ref[c, a3, 0, 0, 0]
                elif route == 1:
                    piece = ref[c, 0, a3, 0, 0]
                else:
                    piece = ref[c, 0, 0, a3, 0]
                left = (c * 4 + a3) * 384
                out[16 * route : 16 * route + 16, left : left + 384] = piece.astype(F32)


def share_all(blocks):
    hbm = pl.BlockSpec(memory_space=pl.ANY)
    vm = pl.BlockSpec(memory_space=pltpu.VMEM)
    pieces = pl.pallas_call(
        share_kernel,
        out_shape=jax.ShapeDtypeStruct((2, 4, 4, 4, 3, 16, 384), BF16),
        in_specs=[vm],
        out_specs=hbm,
        scratch_shapes=[
            pltpu.VMEM((2, 4, 4, 4, 3, 16, 384), BF16), pltpu.SemaphoreType.DMA, pltpu.SemaphoreType.DMA,
            pltpu.SemaphoreType.DMA((2, 23)),
        ],
        compiler_params=pltpu.CompilerParams(collective_id=3, has_side_effects=True),
    )(blocks)
    return pl.pallas_call(
        assemble_kernel,
        grid=(16,),
        out_shape=jax.ShapeDtypeStruct((D, FF), F32),
        in_specs=[
            pl.BlockSpec((2, 4, 1, 1, 1, 16, 384), lambda b: (0, 0, b // 4, b % 4, 0, 0, 0)),
            pl.BlockSpec((2, 1, 4, 1, 1, 16, 384), lambda b: (0, b % 4, 0, b // 4, 1, 0, 0)),
            pl.BlockSpec((2, 1, 1, 4, 1, 16, 384), lambda b: (0, b // 4, b % 4, 0, 2, 0, 0)),
        ],
        out_specs=pl.BlockSpec((48, FF), lambda b: (b, 0)),
    )(pieces, pieces, pieces)


def on_device(
    tokens, masked, live_images, mask_token, norm_gain, norm_shift, w_first, w_second, layer_scale, rel_table, cotangent
):
    here = masked[0] == 1
    valid = (lax.axis_index("section") < live_images[lax.axis_index("dp")]).astype(F32)

    def pad(array):
        return jnp.pad(array, ((0, ROWS - array.shape[0]), (0, 0)))

    h0 = pad(jnp.where(here[:, None], mask_token[None, :], tokens[0]))
    mask = jnp.broadcast_to(pad(here.astype(F32)[:, None]), (ROWS, 128))
    vec = jnp.concatenate([norm_gain, norm_shift, layer_scale, jnp.zeros((5, D), F32)], axis=0)
    w_all, vecs = gather_all(w_first[0], vec)
    table = jnp.transpose(rel_table, (0, 2, 1)).reshape(2 * HEADS, -1)
    turned = jnp.pad(table[:, : SPAN * SPAN][:, ::-1], ((0, 0), (0, 768 - SPAN * SPAN)))
    corner = jnp.pad(table[:, SPAN * SPAN :], ((0, 0), (0, 125)))
    block_out, tokens_grad, grads, small = layers(
        h0, pad(cotangent[0]), mask, jnp.full((8, 128), valid), w_all, w_second,
        vecs[:, 0], vecs[:, 1], vecs[:, 2], turned, corner,
    )
    first, second, totals = reduce_all(grads, small.reshape(2, 24, D))
    first_grad = share_all(first)
    totals = totals.reshape(48, D)
    count = jnp.sum(live_images).astype(F32) * (SEQ * D)
    rms = jnp.sqrt(jnp.sum(totals[:8], axis=1) / count).reshape(4, 2)
    own = lax.dynamic_slice(totals, (8 + 3 * lax.axis_index("section"), 0), (3, D))
    table_grad = jnp.transpose(totals[24:].reshape(2, HEADS, D)[:, :, :732], (0, 2, 1))
    return (
        block_out[None, :SEQ], tokens_grad[None, :SEQ], first_grad[None], second,
        own[1:2], own[2:3], own[0:1], table_grad, totals[20], rms,
    )


def solution(mesh):
    both = P(("dp", "section"), None, None)
    part = P("section", None)
    return jax.shard_map(
        on_device,
        mesh=mesh,
        in_specs=(both, P(("dp", "section"), None), P(), P(), part, part, P("section", None, None), P(), part, P(), both),
        out_specs=(
            both, both, P("section", None, None), P(None, ("dp", "section"), None), part, part, part, P(), P(), P(),
        ),
        check_vma=False,
    )
```

```python
import functools
import math

import jax
import jax.numpy as jnp
import numpy as np
from jax import lax
from jax.experimental import pallas as pl
from jax.experimental.pallas import tpu as pltpu
from jax.sharding import PartitionSpec as P

SEQ, ROWS, KEYS = 197, 208, 256
D, FF, HEADS, GRID = 768, 3072, 12, 14
SPAN = 2 * GRID - 1
EPSILON = 1e-06
INV_ROOT = 0.125
INV_ROOT_TWO_PI = 0.3989422804014327
F32, BF16 = jnp.float32, jnp.bfloat16
HALF = (3, 4, 4, 4, 16, 384)


def mm(a, b):
    return lax.dot_general(a, b, (((1,), (0,)), ((), ())), preferred_element_type=F32)


def mm_nt(a, b):
    return lax.dot_general(a, b, (((1,), (1,)), ((), ())), preferred_element_type=F32)


def mm_tn(a, b):
    return lax.dot_general(a, b, (((0,), (0,)), ((), ())), preferred_element_type=F32)


def lanes(start, size):
    return pl.ds(pl.multiple_of(start, 128), size)


def token_offsets():
    patch = np.arange(SEQ - 1)
    return (patch // GRID) * SPAN + patch % GRID


def selectors():
    forward = np.zeros((384, KEYS), np.float32)
    backward = np.zeros((KEYS, 384), np.float32)
    offsets = token_offsets()
    forward[offsets, np.arange(1, SEQ)] = 1.0
    backward[np.arange(1, SEQ), offsets[-1] - offsets] = 1.0
    return jnp.asarray(forward, BF16), jnp.asarray(backward, BF16)


def centre(h):
    average = jnp.mean(h, axis=-1, keepdims=True)
    centred = h - average
    inv_std = lax.rsqrt(jnp.mean(centred * centred, axis=-1, keepdims=True) + EPSILON)
    return centred * inv_std, inv_std


def gelu_pair(u):
    size = jnp.abs(u)
    t = 1.0 / (1.0 + 0.23164189 * size)
    bell = jnp.exp(-0.5 * u * u)
    poly = t * (
        0.127414796
        + t * (-0.142248368 + t * (0.7107068705 + t * (-0.7265760135 + t * 0.5307027145)))
    )
    tail = poly * bell
    phi = jnp.where(u >= 0.0, 1.0 - tail, tail)
    return u * phi, phi + u * bell * INV_ROOT_TWO_PI


def half_mask(rows, parity):
    lane = lax.broadcasted_iota(jnp.int32, (rows, 128), 1)
    return (lane < 64) if parity == 0 else (lane >= 64)


def keep_half(block, parity):
    return jnp.where(half_mask(block.shape[0], parity), block, jnp.zeros_like(block))


class Body:
    def __init__(self, **refs):
        self.__dict__.update(refs)

    def expand_bias(self, layer):
        def head(index, _):
            base = jnp.broadcast_to(self.table[pl.ds(layer * HEADS + index, 1), :], (16, 768))
            base = pltpu.roll(base, 404, 1, stride=1, stride_axis=0)
            for yi in range(GRID):
                turned = pltpu.roll(base, SPAN * yi, 1) if yi else base
                self.fold[1 + GRID * yi : 1 + GRID * (yi + 1), :384] = turned[:GRID, :384]
            spread = self.fold[:, :384]
            high = spread.astype(BF16)
            low = (spread - high.astype(F32)).astype(BF16)
            select = self.select_forward[...]
            grid = mm(high, select) + mm(low, select)
            row = lax.broadcasted_iota(jnp.int32, (ROWS, KEYS), 0)
            column = lax.broadcasted_iota(jnp.int32, (ROWS, KEYS), 1)
            corner = self.corner[pl.ds(layer * HEADS + index, 1), :]
            grid = jnp.where(row == 0, corner[:, 0:1], grid)
            grid = jnp.where(column == 0, corner[:, 1:2], grid)
            grid = jnp.where((row == 0) & (column == 0), corner[:, 2:3], grid)
            self.bias[index] = jnp.where(column >= SEQ, -1e30, grid)
            return 0

        lax.fori_loop(0, HEADS, head, 0)

    def normed(self, s):
        scaled, _ = centre(self.h[s].astype(F32))
        gain = self.vecs[s, 0:1, :]
        shift = self.vecs[s, 1:2, :]
        self.n[0] = (scaled * gain + shift).astype(BF16)

    def finish(self, s, left, right_of):
        real = (lax.broadcasted_iota(jnp.int32, (ROWS, 1), 0) < SEQ).astype(F32) * self.valid

        def block(j, _):
            columns = lanes(j * 256, 256)
            projected = mm(left[...], right_of(columns))
            branch = self.vecs[s, 2:3, columns] * projected
            result = self.h[s, :, columns].astype(F32) + branch
            self.p[s, :, columns] = projected.astype(BF16)
            self.small[2 * s : 2 * s + 1, columns] = jnp.sum(branch * branch * real, axis=0, keepdims=True)
            self.small[2 * s + 1 : 2 * s + 2, columns] = jnp.sum(result * result * real, axis=0, keepdims=True)
            if s < 3:
                self.h[s + 1, :, columns] = result.astype(BF16)
            else:
                self.block_out[0, :, columns] = (result[:SEQ] * self.valid).astype(BF16)
            return 0

        lax.fori_loop(0, 3, block, 0)

    def attend_forward(self, s):
        layer = s // 2
        self.normed(s)

        def project(j, _):
            columns = lanes(j * 256, 256)
            self.qkv[layer, :ROWS, columns] = mm(self.n[0], self.w[s, :, columns]).astype(BF16)
            return 0

        lax.fori_loop(0, 9, project, 0)
        self.qkv[layer, ROWS:, :] = jnp.zeros((KEYS - ROWS, 2304), BF16)

        def pair(j, _):
            q = self.qkv[layer, :ROWS, lanes(j * 128, 128)]
            k = self.qkv[layer, :, lanes(768 + j * 128, 128)]
            v = self.qkv[layer, :, lanes(1536 + j * 128, 128)]
            mixed = jnp.zeros((ROWS, 128), F32)
            for parity in range(2):
                scores = mm_nt(keep_half(q, parity), k) * INV_ROOT + self.bias[2 * j + parity]
                peak = jnp.max(scores, axis=-1, keepdims=True)
                exps = jnp.exp(scores - peak)
                total = jnp.sum(exps, axis=-1, keepdims=True)
                probs = (exps * (1.0 / total)).astype(BF16)
                self.probs[layer, 2 * j + parity] = probs
                mixed = mixed + mm(probs, keep_half(v, parity))
            self.o[layer, :, lanes(j * 128, 128)] = mixed.astype(BF16)
            return 0

        lax.fori_loop(0, HEADS // 2, pair, 0)
        self.finish(s, self.o.at[layer], lambda c: self.w[s, :, pl.ds(pl.multiple_of(2304 + c.start, 128), 256)])

    def dense_forward(self, s):
        layer = s // 2
        self.normed(s)

        def up(j, _):
            columns = lanes(j * 256, 256)
            u = mm(self.n[0], self.w[s, :, columns])
            act, slope = gelu_pair(u)
            self.a[layer, :, columns] = act.astype(BF16)
            self.slope[layer, :, columns] = slope.astype(BF16)
            return 0

        lax.fori_loop(0, 12, up, 0)
        self.finish(s, self.a.at[layer], lambda c: self.w2[:, c])

    def enter(self, s):
        g = self.g[...].astype(F32)
        row = 8 + 3 * s
        self.small[row : row + 1, :] = jnp.sum(g * self.p[s].astype(F32), axis=0, keepdims=True)
        dp = (g * self.vecs[s, 2:3, :]).astype(BF16)
        self.dp[...] = dp
        self.normed(s)
        if s % 2 == 0:
            self.n[1] = self.o[s // 2]
            self.du[:, 2304:] = dp

    def leave(self, s):
        width = 2304 if s % 2 == 0 else FF

        def block(j, _):
            rows = pl.ds(pl.multiple_of(j * 256, 256), 256)
            self.bias[j] = mm_nt(self.du[:, :width], self.w[s, rows, :width])
            return 0

        lax.fori_loop(0, 3, block, 0)
        scaled, inv_std = centre(self.h[s].astype(F32))
        dn = jnp.concatenate([self.bias[0], self.bias[1], self.bias[2]], axis=1)
        row = 8 + 3 * s
        self.small[row + 1 : row + 2, :] = jnp.sum(dn * scaled, axis=0, keepdims=True)
        self.small[row + 2 : row + 3, :] = jnp.sum(dn, axis=0, keepdims=True)
        e = dn * self.vecs[s, 0:1, :]
        mean_e = jnp.mean(e, axis=-1, keepdims=True)
        mean_ex = jnp.mean(e * scaled, axis=-1, keepdims=True)
        g = self.g[...].astype(F32) + inv_std * (e - mean_e - scaled * mean_ex)
        self.g[...] = g.astype(BF16)

    def put(self, k, mine, route, a1, a2, a3, piece):
        if mine:
            pair = self.pair.at[k % 2, route, a1, a2, a3]
            pair[...] = (piece + pair[...].astype(F32)).astype(BF16)
        else:
            self.stage[k % 2, route, a1, a2, a3] = piece.astype(BF16)

    def first_half(self, k, mine):
        half = self.core if mine else 1 - self.core

        def block(a3, _):
            j = half * 4 + a3
            left = jnp.where(j >= self.switch, 1, 0)
            grad = mm_tn(self.n[left], self.du[:, lanes(j * 384, 384)])
            for rb in range(16):
                for route in range(3):
                    top = rb * 48 + route * 16
                    self.put(k, mine, route, rb // 4, rb % 4, a3, grad[top : top + 16, :])
            return 0

        lax.fori_loop(0, 4, block, 0)

    def second_half(self, k, mine, layer):
        half = self.core if mine else 1 - self.core

        def block(q, _):
            z, x_high = q // 2, q % 2
            grad = mm_tn(self.a[layer, :, lanes(q * 384, 384)], self.dp[:, lanes(half * 384, 384)])
            for x_low in range(2):
                x = 2 * x_high + x_low
                for y in range(4):
                    top = x_low * 192 + y * 24
                    part = jnp.concatenate([grad[top : top + 24], grad[top + 96 : top + 120]], axis=0)
                    self.put(k, mine, 0, x, y, z, part[0:16])
                    self.put(k, mine, 1, y, z, x, part[16:32])
                    self.put(k, mine, 2, z, x, y, part[32:48])
            return 0

        lax.fori_loop(0, 8, block, 0)

    def down(self, s):
        layer = s // 2

        def block(j, _):
            columns = lanes(j * 256, 256)
            rows = pl.ds(pl.multiple_of(j * 256, 256), 256)
            da = mm_nt(self.dp[...], self.w2[rows, :])
            self.du[:, columns] = (da * self.slope[layer, :, columns].astype(F32)).astype(BF16)
            return 0

        lax.fori_loop(0, 12, block, 0)

    def back_out(self, s):
        def block(j, _):
            rows = pl.ds(pl.multiple_of(j * 256, 256), 256)
            self.do[:, lanes(j * 256, 256)] = mm_nt(self.dp[...], self.w[s, rows, 2304:]).astype(BF16)
            return 0

        lax.fori_loop(0, 3, block, 0)

    def pairs(self, s, lo, hi):
        layer = s // 2

        def pair(j, _):
            q = self.qkv[layer, :ROWS, lanes(j * 128, 128)]
            k = self.qkv[layer, :, lanes(768 + j * 128, 128)]
            v = self.qkv[layer, :, lanes(1536 + j * 128, 128)]
            do = self.do[:, lanes(j * 128, 128)]
            dq = jnp.zeros((ROWS, 128), F32)
            dk = jnp.zeros((KEYS, 128), F32)
            dv = jnp.zeros((KEYS, 128), F32)
            for parity in range(2):
                do_half = keep_half(do, parity)
                probs = self.probs[layer, 2 * j + parity]
                wide = probs.astype(F32)
                d_probs = mm_nt(do_half, v)
                inner = jnp.sum(d_probs * wide, axis=-1, keepdims=True)
                d_scores = (wide * (d_probs - inner)).astype(BF16)
                dv = dv + mm_tn(probs, do_half)
                dq = dq + mm(d_scores, keep_half(k, parity))
                dk = dk + mm_tn(d_scores, keep_half(q, parity))
                self.fold_bias(layer, 2 * j + parity, d_scores)
            self.du[:, lanes(j * 128, 128)] = (dq * INV_ROOT).astype(BF16)
            self.du[:, lanes(768 + j * 128, 128)] = (dk[:ROWS] * INV_ROOT).astype(BF16)
            self.du[:, lanes(1536 + j * 128, 128)] = dv[:ROWS].astype(BF16)
            return 0

        lax.fori_loop(lo, hi, pair, 0)

    def fold_bias(self, layer, head, d_scores):
        self.fold[:, :384] = mm(d_scores, self.select_backward[...])
        total = self.fold[1:17, :]
        for yi in range(1, GRID):
            total = total + pltpu.roll(self.fold[1 + GRID * yi : 17 + GRID * yi, :], SPAN * yi, 1)
        row = lax.broadcasted_iota(jnp.int32, (16, 768), 0)
        total = jnp.where(row < GRID, total, 0.0)
        total = pltpu.roll(total, 0, 1, stride=1, stride_axis=0)
        total = jnp.sum(total, axis=0, keepdims=True)
        wide = d_scores.astype(F32)
        corner = wide[0:1, 0:1]
        top = jnp.sum(wide[0:1, :], axis=1, keepdims=True) - corner
        side = jnp.sum(wide[:, 0:1], axis=0, keepdims=True) - corner
        lane = lax.broadcasted_iota(jnp.int32, (1, 768), 1)
        total = jnp.where(lane == 729, top, total)
        total = jnp.where(lane == 730, side, total)
        total = jnp.where(lane == 731, corner, total)
        self.small[pl.ds(24 + layer * HEADS + head, 1), :] = total


MESH = pl.DeviceIdType.MESH
AXES = ("x", "y", "z")
ROUTES = (("x", "y", "z"), ("y", "z", "x"), ("z", "x", "y"))
ORDER = (5, 3, 2, 4, 1, 0)


class Place:
    def __init__(self):
        dp = lax.axis_index("dp")
        self.at = {"z": dp // 8, "x": (dp // 2) % 4, "c": dp % 2, "y": lax.axis_index("section")}

    def go(self, axis, step):
        at = dict(self.at)
        at[axis] = (at[axis] + step) % (2 if axis == "c" else 4)
        return ((at["z"] * 4 + at["x"]) * 2 + at["c"], at["y"])

    def index(self, axis, step=0):
        return (self.at[axis] + step) % 4


def meet(place):
    barrier = pltpu.get_barrier_semaphore()
    count = 0
    for axis in AXES:
        for step in (1, 2, 3):
            pl.semaphore_signal(barrier, inc=1, device_id=place.go(axis, step), device_id_type=MESH)
            count += 1
    pl.semaphore_signal(barrier, inc=1, device_id=place.go("c", 1), device_id_type=MESH)
    pl.semaphore_wait(barrier, count + 1)


class Reduce:
    def __init__(self, place, **refs):
        self.place = place
        self.__dict__.update(refs)
        self.flying = {}

    def send(self, key, src, dst, number, device):
        k = key[1]
        copy = pltpu.make_async_remote_copy(
            src_ref=src, dst_ref=dst, send_sem=self.sems.at[0, k, number], recv_sem=self.sems.at[1, k, number],
            device_id=device, device_id_type=MESH,
        )
        copy.start()
        self.flying[key] = copy

    def sent(self, k, names):
        for name in names:
            for r in range(3):
                self.flying[(name, k, r)].wait_send()

    def reuse_stage(self, k):
        if k >= 2:
            self.sent(k - 2, ("c",))

    def swap(self, k):
        if k >= 2:
            pl.semaphore_wait(self.pair_credit, 1)
        for r in range(3):
            self.send(("c", k, r), self.stage.at[k % 2, r], self.pair.at[k % 2, r], r, self.place.go("c", 1))

    def swapped(self, k):
        for r in range(3):
            self.flying[("c", k, r)].wait_recv()

    def first(self, k):
        place = self.place
        for r, (axis, _, _) in enumerate(ROUTES):
            own, far = self.pair.at[k % 2, r], self.far.at[k % 2, r]
            across, ahead, behind = place.index(axis, 2), place.index(axis, 1), place.index(axis, 3)
            up, down = place.go(axis, 1), place.go(axis, 3)
            base = 3 + 6 * r
            if k >= 2:
                pl.semaphore_wait(self.far_credit.at[r, 0], 1)
                pl.semaphore_wait(self.far_credit.at[r, 1], 1)
            self.send(("fa", k, r), own.at[across, 0:2], far.at[0], base, up)
            self.send(("fb", k, r), own.at[across, 2:4], far.at[1], base + 1, down)
            self.send(("db", k, r), own.at[ahead, 2:4], far.at[2], base + 2, up)
            self.send(("da", k, r), own.at[behind, 0:2], far.at[3], base + 3, down)

    def merge(self, k):
        place = self.place
        for r, (axis, _, _) in enumerate(ROUTES):
            own, far = self.pair.at[k % 2, r], self.far.at[k % 2, r]
            ahead, behind = place.index(axis, 1), place.index(axis, 3)
            base = 3 + 6 * r
            self.flying[("fa", k, r)].wait_recv()
            far[0] = (far[0].astype(F32) + own[ahead, 0:2].astype(F32)).astype(BF16)
            self.send(("ma", k, r), far.at[0], far.at[4], base + 4, place.go(axis, 1))
            self.flying[("fb", k, r)].wait_recv()
            far[1] = (far[1].astype(F32) + own[behind, 2:4].astype(F32)).astype(BF16)
            self.send(("mb", k, r), far.at[1], far.at[5], base + 5, place.go(axis, 3))

    def second(self, k):
        place = self.place
        for r, (axis, nxt, _) in enumerate(ROUTES):
            for name in ("db", "da", "ma", "mb"):
                self.flying[(name, k, r)].wait_recv()
            own, far = self.pair.at[k % 2, r], self.far.at[k % 2, r]
            me = place.index(axis)
            low = own[me, 0:2].astype(F32) + far[4].astype(F32) + far[3].astype(F32)
            high = own[me, 2:4].astype(F32) + far[2].astype(F32) + far[5].astype(F32)
            line, line_in = self.line.at[k % 2, r], self.line_in.at[k, r]
            line[0:2] = low.astype(BF16)
            line[2:4] = high.astype(BF16)
            for step in (1, 2, 3):
                self.send(
                    (("s", step), k, r), line.at[place.index(nxt, step)], line_in.at[step - 1],
                    21 + 3 * r + step - 1, place.go(nxt, step),
                )
        self.sent(k, ("fa", "fb", "db", "da", "ma", "mb"))
        if k + 2 < 6:
            pl.semaphore_signal(self.pair_credit, inc=1, device_id=place.go("c", 1), device_id_type=MESH)
            for r, (axis, _, _) in enumerate(ROUTES):
                pl.semaphore_signal(self.far_credit.at[r, 0], inc=1, device_id=place.go(axis, 1), device_id_type=MESH)
                pl.semaphore_signal(self.far_credit.at[r, 1], inc=1, device_id=place.go(axis, 3), device_id_type=MESH)

    def third(self, k):
        place = self.place
        for r, (_, axis, nxt) in enumerate(ROUTES):
            line, line_in, spot, spot_in = self.line.at[k % 2, r], self.line_in.at[k, r], self.spot.at[k % 2, r], self.spot_in.at[k, r]
            total = line[place.index(axis)].astype(F32)
            for step in (1, 2, 3):
                self.flying[(("s", step), k, r)].wait_recv()
                total = total + line_in[step - 1].astype(F32)
            spot[...] = total.astype(BF16)
            for step in (1, 2, 3):
                self.send(
                    (("t", step), k, r), spot.at[place.index(nxt, step)], spot_in.at[step - 1],
                    30 + 3 * r + step - 1, place.go(nxt, step),
                )
        self.sent(k, (("s", 1), ("s", 2), ("s", 3)))

    def close(self, k):
        place, tensor = self.place, ORDER[k]
        for r, (_, _, axis) in enumerate(ROUTES):
            spot, spot_in = self.spot.at[k % 2, r], self.spot_in.at[k, r]
            total = spot[place.index(axis)].astype(F32)
            for step in (1, 2, 3):
                self.flying[(("t", step), k, r)].wait_recv()
                total = total + spot_in[step - 1].astype(F32)
            if tensor < 4:
                self.first_out[tensor, r] = total.astype(BF16)
            else:
                rows = self.rows.at[tensor - 4]
                if r == 0:
                    rows[0, 0:16] = total
                elif r == 1:
                    rows[0, 16:24] = total[0:8]
                    rows[1, 0:8] = total[8:16]
                else:
                    rows[1, 8:24] = total
        self.sent(k, (("t", 1), ("t", 2), ("t", 3)))
        if tensor >= 4:
            layer, me = tensor - 4, place.at["c"]
            self.send(("r", k, 0), self.rows.at[layer, 1 - me], self.rows_in.at[layer], 39, place.go("c", 1))

    def finish(self):
        me = self.place.at["c"]
        for k, tensor in enumerate(ORDER):
            if tensor >= 4:
                self.flying[("r", k, 0)].wait()
                layer = tensor - 4
                self.second_out[layer, :, lanes(me * 384, 384)] = self.rows[layer, me]
                self.second_out[layer, :, lanes((1 - me) * 384, 384)] = self.rows_in[layer]
        for k in (4, 5):
            self.sent(k, ("c",))


class Totals:
    def __init__(self, place, part, bufs, sems):
        self.place, self.part, self.bufs, self.sems = place, part, bufs, sems
        self.copies = []

    def send(self, src, dst, number, device):
        copy = pltpu.make_async_remote_copy(
            src_ref=src, dst_ref=dst, send_sem=self.sems.at[0, number], recv_sem=self.sems.at[1, number],
            device_id=device, device_id_type=MESH,
        )
        copy.start()
        self.copies.append(copy)
        return copy

    @staticmethod
    def half(core):
        return pl.ds(pl.multiple_of(core * 24, 8), 24)

    def start(self, small):
        me = self.place.at["c"]
        self.small = small
        self.now = [self.send(small.at[self.half(1 - me)], self.bufs.at[0, 0], 0, self.place.go("c", 1))]

    def step(self, number):
        place, me = self.place, self.place.at["c"]
        for copy in self.now:
            copy.wait_recv()
        if number == 0:
            self.part[...] = self.small[self.half(me), :] + self.bufs[0, 0]
        else:
            axis = AXES[number - 1]
            self.bufs[number, place.at[axis]] = self.part[...]
            self.part[...] = (self.bufs[number, 0] + self.bufs[number, 1]) + (self.bufs[number, 2] + self.bufs[number, 3])
        if number < 3:
            axis = AXES[number]
            self.now = [
                self.send(self.part, self.bufs.at[number + 1, place.at[axis]], 1 + 3 * number + step - 1, place.go(axis, step))
                for step in (1, 2, 3)
            ]
            for copy in self.now:
                copy.wait_send()
        else:
            self.now = [self.send(self.part, self.bufs.at[0, 1], 10, place.go("c", 1))]

    def close(self, out):
        me = self.place.at["c"]
        for copy in self.now:
            copy.wait_recv()
        out[self.half(me), :] = self.part[...]
        out[self.half(1 - me), :] = self.bufs[0, 1]
        self.copies[0].wait_send()
        self.copies[-1].wait_send()


class Spread:
    def __init__(self, place, sems):
        self.place, self.sems = place, sems
        self.sent = []

    def send(self, number, src, dst, device):
        copy = pltpu.make_async_remote_copy(
            src_ref=src, dst_ref=dst, send_sem=self.sems.at[0, number], recv_sem=self.sems.at[1, number],
            device_id=device, device_id_type=MESH,
        )
        copy.start()
        self.sent.append(copy)

    def wait(self, number, ref):
        pltpu.make_async_remote_copy(
            src_ref=ref, dst_ref=ref, send_sem=self.sems.at[0, number], recv_sem=self.sems.at[1, number],
            device_id=self.place.go("c", 1), device_id_type=MESH,
        ).wait_recv()

    def drain(self):
        for copy in self.sent:
            copy.wait_send()


GATHER_MESSAGES = 99


class Gather(Spread):
    def __init__(self, place, source, full, sems):
        super().__init__(place, sems)
        self.source, self.full = source, full

    def rows(self, route, step, sub=None):
        top = (0 if route == "x" else 384) + self.place.index(route, step) * 96 + self.place.at["c"] * 48
        if sub is None:
            return pl.ds(pl.multiple_of(top, 16), 48)
        return pl.ds(pl.multiple_of(top + 16 * sub, 16), 16)

    def ref(self, rel, route, step, sub=None):
        return self.full.at[self.place.index("y", rel), self.rows(route, step, sub)]

    @staticmethod
    def along_y(rel, route, sub):
        return 3 * (2 * (rel - 1) + (route == "z")) + sub

    @staticmethod
    def in_plane(rel, route, kind, sub):
        return 18 + 9 * (2 * (rel - 1) + (route == "z")) + 3 * kind + sub

    @staticmethod
    def across(rel, route, step):
        return 72 + 4 * (2 * (rel - 1) + (route == "z")) + step

    def begin(self, up, down):
        for sub in range(3):
            for route, step in ((up, 1), (down, 3)):
                mine = self.source.at[self.rows(route, 0, sub)]
                self.send(self.along_y(4 - step, route, sub), mine, self.ref(0, route, 0, sub), self.place.go("y", step))

    def arrive(self, *pieces):
        for sub in range(3):
            for rel, route in pieces:
                piece = self.ref(rel, route, 0, sub)
                self.wait(self.along_y(rel, route, sub), piece)
                if (rel, route) == (3, "x"):
                    self.send(self.along_y(2, route, sub), piece, piece, self.place.go("y", 1))
                if (rel, route) == (1, "z"):
                    self.send(self.along_y(2, route, sub), piece, piece, self.place.go("y", 3))
                for kind, step in ((0, 1), (1, 3)):
                    self.send(self.in_plane(rel, route, kind, sub), piece, piece, self.place.go(route, step))
        for rel, route in pieces:
            piece = self.ref(rel, route, 0)
            self.send(self.across(rel, route, 0), piece, piece, self.place.go("c", 1))

    def turn(self, *pieces):
        place = self.place
        clockwise = 1 - 2 * place.at["c"]
        for sub, way in ((0, 1), (1, clockwise), (2, -1)):
            for rel, route in pieces:
                for kind, step in ((0, 3), (1, 1)):
                    self.wait(self.in_plane(rel, route, kind, sub), self.ref(rel, route, step, sub))
                piece = self.ref(rel, route, 4 - way, sub)
                self.send(self.in_plane(rel, route, 2, sub), piece, piece, place.go(route, 4 + way))
        for rel, route in pieces:
            for step in (3, 1):
                piece = self.ref(rel, route, step)
                self.send(self.across(rel, route, step), piece, piece, place.go("c", 1))

    def end(self, *pieces):
        for rel, route in pieces:
            for sub in range(3):
                self.wait(self.in_plane(rel, route, 2, sub), self.ref(rel, route, 2, sub))
            piece = self.ref(rel, route, 2)
            self.send(self.across(rel, route, 2), piece, piece, self.place.go("c", 1))

    def settle(self, rel):
        other = 1 - self.place.at["c"]
        for route in ("x", "z"):
            for step in range(4):
                top = (0 if route == "x" else 384) + self.place.index(route, step) * 96 + other * 48
                self.wait(self.across(rel, route, step), self.full.at[self.place.index("y", rel), pl.ds(pl.multiple_of(top, 16), 48)])


def layers_kernel(
    tokens, masked, cotangent, live, mask_token, norm_gain, norm_shift, layer_scale, w_own, w2_hbm,
    table, corner, select_f, select_b,
    block_out, tokens_grad, first_out, second_out, totals,
    w, w2, h, qkv, probs, o, a, slope, p, n, bias, fold, du, dp, do, g, vec, vecs, small,
    stage, pair, far, line, line_in, spot, spot_in, rows, rows_in, part, bufs,
    load_sem, w2_sem, gather_sems, sems, small_sems, pair_credit, far_credit,
):
    place = Place()
    vec[0:1] = norm_gain[...]
    vec[1:2] = norm_shift[...]
    vec[2:3] = layer_scale[...]
    vec[3:8] = jnp.zeros((5, D), F32)
    meet(place)
    y = place.at["y"]
    own = pltpu.make_async_copy(w_own.at[0], w.at[y], load_sem)
    own.start()
    w2_load = pltpu.make_async_copy(w2_hbm.at[0], w2, w2_sem)
    w2_load.start()
    gather = Gather(place, w_own.at[0], w, gather_sems)
    gather.begin("x", "z")
    vecs[y] = vec[...]
    for step in (1, 2, 3):
        gather.send(95 + step, vec, vecs.at[y], place.go("y", step))
    valid = jnp.where(y < live[lax.axis_index("dp")], 1.0, 0.0)
    body = Body(
        valid=valid, core=place.at["c"], vecs=vecs, table=table, corner=corner,
        select_forward=select_f, select_backward=select_b, block_out=block_out, small=small,
        w=w, w2=w2, h=h, qkv=qkv, probs=probs, o=o, a=a, slope=slope, p=p, n=n, bias=bias,
        fold=fold, du=du, dp=dp, do=do, g=g, stage=stage, pair=pair,
    )
    reduce = Reduce(
        place, stage=stage, pair=pair, far=far, line=line, line_in=line_in, spot=spot, spot_in=spot_in,
        rows=rows, rows_in=rows_in, first_out=first_out, second_out=second_out, sems=sems,
        pair_credit=pair_credit, far_credit=far_credit,
    )
    sums = Totals(place, part, bufs, small_sems)

    gather.arrive((3, "x"), (1, "z"))
    gather.begin("z", "x")
    fold[...] = jnp.zeros_like(fold)
    square = (ROWS, KEYS)
    diagonal = lax.broadcasted_iota(jnp.int32, square, 0) == lax.broadcasted_iota(jnp.int32, square, 1)
    flags = jnp.concatenate([masked[...].astype(F32), jnp.zeros((1, KEYS - SEQ), F32)], axis=1)
    here = jnp.sum(jnp.where(diagonal, flags, 0.0), axis=1, keepdims=True)
    h[0, 192:] = jnp.zeros((16, D), BF16)
    start = tokens[0].astype(F32)
    h[0, :SEQ] = (start + here[:SEQ] * (mask_token[...].astype(F32) - start)).astype(BF16)
    g[192:] = jnp.zeros((16, D), BF16)
    g[:SEQ] = (cotangent[0].astype(F32) * valid).astype(BF16)
    body.expand_bias(0)
    gather.arrive((2, "x"), (2, "z"))
    gather.turn((3, "x"), (1, "z"))
    gather.arrive((1, "x"), (3, "z"))
    gather.turn((2, "x"), (2, "z"))
    gather.end((3, "x"), (1, "z"))
    gather.turn((1, "x"), (3, "z"))
    gather.end((2, "x"), (2, "z"), (1, "x"), (3, "z"))
    for rel in (3, 1, 2):
        gather.settle(rel)
    for step in (1, 2, 3):
        gather.wait(95 + step, vecs.at[place.index("y", 4 - step)])
    own.wait()
    body.attend_forward(0)
    w2_load.wait()
    body.dense_forward(1)
    w2_load = pltpu.make_async_copy(w2_hbm.at[1], w2, w2_sem)
    w2_load.start()
    body.expand_bias(1)
    body.attend_forward(2)
    w2_load.wait()
    body.dense_forward(3)
    gather.drain()

    body.switch = 8
    body.enter(3)
    body.second_half(0, False, 1)
    reduce.swap(0)
    body.down(3)
    w2_load = pltpu.make_async_copy(w2_hbm.at[0], w2, w2_sem)
    w2_load.start()
    reduce.swapped(0)
    body.second_half(0, True, 1)
    reduce.first(0)
    body.first_half(1, False)
    reduce.swap(1)
    body.leave(3)
    reduce.merge(0)
    reduce.swapped(1)
    body.first_half(1, True)
    reduce.first(1)
    body.switch = 6
    body.enter(2)
    body.back_out(2)
    reduce.second(0)
    body.pairs(2, 0, 3)
    reduce.merge(1)
    body.pairs(2, 3, 6)
    reduce.third(0)
    reduce.reuse_stage(2)
    body.first_half(2, False)
    reduce.swap(2)
    body.leave(2)
    reduce.second(1)
    reduce.swapped(2)
    body.first_half(2, True)
    reduce.first(2)
    reduce.close(0)
    body.switch = 8
    body.enter(1)
    reduce.reuse_stage(3)
    body.second_half(3, False, 0)
    reduce.swap(3)
    reduce.third(1)
    w2_load.wait()
    body.down(1)
    reduce.merge(2)
    reduce.swapped(3)
    body.second_half(3, True, 0)
    reduce.first(3)
    reduce.reuse_stage(4)
    body.first_half(4, False)
    reduce.second(2)
    reduce.swap(4)
    reduce.close(1)
    body.leave(1)
    reduce.merge(3)
    reduce.swapped(4)
    body.first_half(4, True)
    reduce.first(4)
    body.switch = 6
    body.enter(0)
    body.back_out(0)
    reduce.third(2)
    reduce.second(3)
    body.pairs(0, 0, 3)
    reduce.merge(4)
    reduce.close(2)
    body.pairs(0, 3, 6)
    reduce.third(3)
    reduce.reuse_stage(5)
    body.first_half(5, False)
    reduce.swap(5)
    body.leave(0)
    grad = g[...].astype(F32)
    tokens_grad[0] = (grad * (1.0 - here)).astype(BF16)[:SEQ]
    small[20:21, :] = jnp.sum(grad * here, axis=0, keepdims=True)
    small[21:24, :] = jnp.zeros((3, D), F32)
    sums.start(small)
    reduce.second(4)
    reduce.swapped(5)
    body.first_half(5, True)
    reduce.first(5)
    reduce.close(3)
    sums.step(0)
    reduce.third(4)
    reduce.merge(5)
    sums.step(1)
    reduce.close(4)
    reduce.second(5)
    sums.step(2)
    reduce.third(5)
    sums.step(3)
    reduce.close(5)
    sums.close(totals)
    reduce.finish()


def layers(tokens, masked, cotangent, live, mask_token, norm_gain, norm_shift, layer_scale, w_own, w2, table, corner):
    select_f, select_b = selectors()
    vm = pl.BlockSpec(memory_space=pltpu.VMEM)
    hbm = pl.BlockSpec(memory_space=pl.ANY)
    sm = pl.BlockSpec(memory_space=pltpu.SMEM)
    V, DMA, REGULAR = pltpu.VMEM, pltpu.SemaphoreType.DMA, pltpu.SemaphoreType.REGULAR
    return pl.pallas_call(
        layers_kernel,
        out_shape=(
            jax.ShapeDtypeStruct((1, SEQ, D), BF16),
            jax.ShapeDtypeStruct((1, SEQ, D), BF16),
            jax.ShapeDtypeStruct((4, 3, 16, 384), BF16),
            jax.ShapeDtypeStruct((2, 24, D), F32),
            jax.ShapeDtypeStruct((48, D), F32),
        ),
        in_specs=[vm, vm, vm, sm, vm, vm, vm, vm, hbm, hbm, vm, vm, vm, vm],
        out_specs=(vm,) * 5,
        scratch_shapes=[
            V((4, D, FF), BF16), V((FF, D), BF16), V((4, ROWS, D), BF16), V((2, KEYS, 2304), BF16),
            V((2, HEADS, ROWS, KEYS), BF16), V((2, ROWS, D), BF16), V((2, ROWS, FF), BF16), V((2, ROWS, FF), BF16),
            V((4, ROWS, D), BF16), V((2, ROWS, D), BF16), V((HEADS, ROWS, KEYS), F32),
            V((ROWS, D), F32), V((ROWS, FF), BF16), V((ROWS, D), BF16), V((ROWS, D), BF16), V((ROWS, D), BF16),
            V((8, D), F32), V((4, 8, D), F32), V((48, D), F32),
            V((2,) + HALF, BF16), V((2,) + HALF, BF16), V((2, 3, 6, 2, 4, 16, 384), BF16),
            V((2, 3, 4, 4, 16, 384), BF16), V((6, 3, 3, 4, 16, 384), BF16),
            V((2, 3, 4, 16, 384), BF16), V((6, 3, 3, 16, 384), BF16),
            V((2, 2, 24, 384), F32), V((2, 24, 384), F32), V((24, D), F32), V((4, 4, 24, D), F32),
            DMA, DMA, DMA((2, GATHER_MESSAGES)), DMA((2, 6, 40)), DMA((2, 11)), REGULAR, REGULAR((3, 2)),
        ],
        compiler_params=pltpu.CompilerParams(
            collective_id=1, has_side_effects=True, vmem_limit_bytes=64 * 2**20
        ),
    )(tokens, masked, cotangent, live, mask_token, norm_gain, norm_shift, layer_scale, w_own, w2, table, corner, select_f, select_b)


class Share(Spread):
    def __init__(self, place, blocks, pieces, sems):
        super().__init__(place, sems)
        self.blocks, self.pieces = blocks, pieces

    def run(self, own_sem, out, out_sem):
        place, pieces = self.place, self.pieces
        at = place.at
        c, x, y, z = at["c"], at["x"], at["y"], at["z"]
        own = pltpu.make_async_copy(self.blocks.at[y], pieces.at[c, z, x, y], own_sem)
        own.start()
        for step in (1, 2, 3):
            self.send(step - 1, self.blocks.at[place.index("y", step)], pieces.at[c, z, x, y], place.go("y", step))
        own.wait()
        for step in (1, 2, 3):
            self.wait(step - 1, pieces.at[c, z, x, place.index("y", 4 - step)])
        low, high = pl.ds(0, 2), pl.ds(2, 2)
        for step in (1, 2, 3):
            self.send(2 + step, pieces.at[c, z, x, low], pieces.at[c, z, x, low], place.go("x", step))
            self.send(5 + step, pieces.at[c, z, x, high], pieces.at[c, z, x, high], place.go("z", step))
        for step in (1, 2, 3):
            self.wait(2 + step, pieces.at[c, z, place.index("x", 4 - step), low])
            self.wait(5 + step, pieces.at[c, place.index("z", 4 - step), x, high])
        row, column = pieces.at[c, z, :, low], pieces.at[c, :, x, high]
        for step in (1, 3, 2):
            self.send(8 + step, row, row, place.go("z", step))
            self.send(11 + step, column, column, place.go("x", step))
        self.send(15, row, row, place.go("c", 1))
        self.send(16, column, column, place.go("c", 1))
        for step in (1, 3, 2):
            row = pieces.at[c, place.index("z", 4 - step), :, low]
            self.wait(8 + step, row)
            self.send(16 + step, row, row, place.go("c", 1))
            column = pieces.at[c, :, place.index("x", 4 - step), high]
            self.wait(11 + step, column)
            self.send(19 + step, column, column, place.go("c", 1))
        first = pltpu.make_async_copy(pieces.at[c], out.at[c], out_sem)
        first.start()
        self.wait(15, pieces.at[1 - c, z, :, low])
        self.wait(16, pieces.at[1 - c, :, x, high])
        for step in (1, 3, 2):
            self.wait(16 + step, pieces.at[1 - c, place.index("z", 4 - step), :, low])
            self.wait(19 + step, pieces.at[1 - c, :, place.index("x", 4 - step), high])
        first.wait()
        rest = pltpu.make_async_copy(pieces.at[1 - c], out.at[1 - c], out_sem)
        rest.start()
        rest.wait()
        self.drain()


def share_kernel(blocks, out, pieces, own_sem, out_sem, sems):
    place = Place()
    meet(place)
    Share(place, blocks, pieces, sems).run(own_sem, out, out_sem)


def assemble_kernel(first, second, third, out):
    for route, ref in enumerate((first, second, third)):
        for c in range(2):
            for a3 in range(4):
                if route == 0:
                    piece = ref[c, a3, 0, 0, 0]
                elif route == 1:
                    piece = ref[c, 0, a3, 0, 0]
                else:
                    piece = ref[c, 0, 0, a3, 0]
                left = (c * 4 + a3) * 384
                out[16 * route : 16 * route + 16, left : left + 384] = piece.astype(F32)


def share_all(blocks):
    hbm = pl.BlockSpec(memory_space=pl.ANY)
    vm = pl.BlockSpec(memory_space=pltpu.VMEM)
    pieces = pl.pallas_call(
        share_kernel,
        out_shape=jax.ShapeDtypeStruct((2, 4, 4, 4, 3, 16, 384), BF16),
        in_specs=[vm],
        out_specs=hbm,
        scratch_shapes=[
            pltpu.VMEM((2, 4, 4, 4, 3, 16, 384), BF16), pltpu.SemaphoreType.DMA, pltpu.SemaphoreType.DMA,
            pltpu.SemaphoreType.DMA((2, 23)),
        ],
        compiler_params=pltpu.CompilerParams(collective_id=3, has_side_effects=True),
    )(blocks)
    return pl.pallas_call(
        assemble_kernel,
        grid=(16,),
        out_shape=jax.ShapeDtypeStruct((D, FF), F32),
        in_specs=[
            pl.BlockSpec((2, 4, 1, 1, 1, 16, 384), lambda b: (0, 0, b // 4, b % 4, 0, 0, 0)),
            pl.BlockSpec((2, 1, 4, 1, 1, 16, 384), lambda b: (0, b % 4, 0, b // 4, 1, 0, 0)),
            pl.BlockSpec((2, 1, 1, 4, 1, 16, 384), lambda b: (0, b // 4, b % 4, 0, 2, 0, 0)),
        ],
        out_specs=pl.BlockSpec((48, FF), lambda b: (b, 0)),
    )(pieces, pieces, pieces)


def on_device(
    tokens, masked, live_images, mask_token, norm_gain, norm_shift, w_first, w_second, layer_scale, rel_table, cotangent
):
    table = jnp.transpose(rel_table, (0, 2, 1)).reshape(2 * HEADS, -1)
    turned = jnp.pad(table[:, : SPAN * SPAN][:, ::-1], ((0, 0), (0, 768 - SPAN * SPAN)))
    corner = jnp.pad(table[:, SPAN * SPAN :], ((0, 0), (0, 125)))
    block_out, tokens_grad, first, second, totals = layers(
        tokens, masked, cotangent, live_images, mask_token.reshape(1, D), norm_gain, norm_shift, layer_scale,
        w_first, w_second, turned, corner,
    )
    first_grad = share_all(first)
    count = jnp.sum(live_images).astype(F32) * (SEQ * D)
    rms = jnp.sqrt(jnp.sum(totals[:8], axis=1) / count).reshape(4, 2)
    own = lax.dynamic_slice(totals, (8 + 3 * lax.axis_index("section"), 0), (3, D))
    table_grad = jnp.transpose(totals[24:].reshape(2, HEADS, D)[:, :, :732], (0, 2, 1))
    return (
        block_out, tokens_grad, first_grad[None], second,
        own[1:2], own[2:3], own[0:1], table_grad, totals[20], rms,
    )


def solution(mesh):
    both = P(("dp", "section"), None, None)
    part = P("section", None)
    return jax.shard_map(
        on_device,
        mesh=mesh,
        in_specs=(both, P(("dp", "section"), None), P(), P(), part, part, P("section", None, None), P(), part, P(), both),
        out_specs=(
            both, both, P("section", None, None), P(None, ("dp", "section"), None), part, part, part, P(), P(), P(),
        ),
        check_vma=False,
    )
```

```python
import functools
import math

import jax
import jax.numpy as jnp
import numpy as np
from jax import lax
from jax.experimental import pallas as pl
from jax.experimental.pallas import tpu as pltpu
from jax.sharding import PartitionSpec as P

SEQ, ROWS, KEYS = 197, 208, 256
D, FF, HEADS, GRID = 768, 3072, 12, 14
SPAN = 2 * GRID - 1
EPSILON = 1e-06
INV_ROOT = 0.125
INV_ROOT_TWO_PI = 0.3989422804014327
F32, BF16 = jnp.float32, jnp.bfloat16
HALF = (3, 4, 4, 4, 16, 384)


def mm(a, b):
    return lax.dot_general(a, b, (((1,), (0,)), ((), ())), preferred_element_type=F32)


def mm_nt(a, b):
    return lax.dot_general(a, b, (((1,), (1,)), ((), ())), preferred_element_type=F32)


def mm_tn(a, b):
    return lax.dot_general(a, b, (((0,), (0,)), ((), ())), preferred_element_type=F32)


def lanes(start, size):
    return pl.ds(pl.multiple_of(start, 128), size)


def token_offsets():
    patch = np.arange(SEQ - 1)
    return (patch // GRID) * SPAN + patch % GRID


def selectors():
    forward = np.zeros((384, KEYS), np.float32)
    forward[token_offsets(), np.arange(1, SEQ)] = 1.0
    rows = np.zeros((16 * GRID, ROWS), np.float32)
    patch = np.arange(SEQ - 1)
    rows[(patch % GRID) * 16 + patch // GRID, patch + 1] = 1.0
    rows[GRID, 0] = 1.0
    return jnp.asarray(forward, BF16), jnp.asarray(rows, BF16)


def centre(h):
    average = jnp.mean(h, axis=-1, keepdims=True)
    centred = h - average
    inv_std = lax.rsqrt(jnp.mean(centred * centred, axis=-1, keepdims=True) + EPSILON)
    return centred * inv_std, inv_std


def gelu_pair(u):
    size = jnp.abs(u)
    t = 1.0 / (1.0 + 0.23164189 * size)
    bell = jnp.exp(-0.5 * u * u)
    poly = t * (
        0.127414796
        + t * (-0.142248368 + t * (0.7107068705 + t * (-0.7265760135 + t * 0.5307027145)))
    )
    tail = poly * bell
    phi = jnp.where(u >= 0.0, 1.0 - tail, tail)
    return u * phi, phi + u * bell * INV_ROOT_TWO_PI


def half_mask(rows, parity):
    lane = lax.broadcasted_iota(jnp.int32, (rows, 128), 1)
    return (lane < 64) if parity == 0 else (lane >= 64)


def keep_half(block, parity):
    return jnp.where(half_mask(block.shape[0], parity), block, jnp.zeros_like(block))


class Body:
    def __init__(self, **refs):
        self.__dict__.update(refs)

    def expand_bias(self, layer, lo, hi):
        def head(index, _):
            base = jnp.broadcast_to(self.table[pl.ds(layer * HEADS + index, 1), :], (16, 768))
            base = pltpu.roll(base, 404, 1, stride=1, stride_axis=0)
            for yi in range(GRID):
                turned = pltpu.roll(base, SPAN * yi, 1) if yi else base
                self.fold[1 + GRID * yi : 1 + GRID * (yi + 1), :] = turned[:GRID, :384]
            spread = self.fold[...]
            grid = mm(spread.astype(BF16), self.select_forward[...])
            row = lax.broadcasted_iota(jnp.int32, (ROWS, KEYS), 0)
            column = lax.broadcasted_iota(jnp.int32, (ROWS, KEYS), 1)
            corner = self.corner[pl.ds(layer * HEADS + index, 1), :]
            grid = jnp.where(row == 0, corner[:, 0:1], grid)
            grid = jnp.where(column == 0, corner[:, 1:2], grid)
            grid = jnp.where((row == 0) & (column == 0), corner[:, 2:3], grid)
            self.bias[layer, index] = jnp.where(column >= SEQ, -1e30, grid).astype(BF16)
            return 0

        lax.fori_loop(lo, hi, head, 0)

    def normed(self, s):
        scaled, _ = centre(self.h[s].astype(F32))
        gain = self.vecs[s, 0:1, :]
        shift = self.vecs[s, 1:2, :]
        self.n[0] = (scaled * gain + shift).astype(BF16)

    def finish(self, s, left, right):
        real = (lax.broadcasted_iota(jnp.int32, (ROWS, 1), 0) < SEQ).astype(F32) * self.valid

        projected = mm(left[...], right)
        branch = self.vecs[s, 2:3, :] * projected
        result = self.h[s].astype(F32) + branch
        self.p[s] = projected.astype(BF16)
        self.small[2 * s : 2 * s + 1, :] = jnp.sum(branch * branch * real, axis=0, keepdims=True)
        self.small[2 * s + 1 : 2 * s + 2, :] = jnp.sum(result * result * real, axis=0, keepdims=True)
        if s < 3:
            self.h[s + 1] = result.astype(BF16)
        else:
            self.block_out[0] = (result[:SEQ] * self.valid).astype(BF16)

    def attend_forward(self, s):
        layer = s // 2
        self.normed(s)

        def project(j, _):
            columns = lanes(j * 1152, 1152)
            weights = self.w[s, :, :, :, columns].reshape(D, 1152)
            self.qkv[layer, :ROWS, columns] = mm(self.n[0], weights).astype(BF16)
            return 0

        lax.fori_loop(0, 2, project, 0)
        self.qkv[layer, ROWS:, :] = jnp.zeros((KEYS - ROWS, 2304), BF16)

        def pair(j):
            q = self.qkv[layer, :ROWS, lanes(j * 128, 128)]
            k = self.qkv[layer, :, lanes(768 + j * 128, 128)]
            v = self.qkv[layer, :, lanes(1536 + j * 128, 128)]
            mixed = jnp.zeros((ROWS, 128), F32)
            for parity in range(2):
                scores = mm_nt(keep_half(q, parity), k) * INV_ROOT + self.bias[layer, 2 * j + parity].astype(F32)
                peak = jnp.max(scores, axis=-1, keepdims=True)
                exps = jnp.exp(scores - peak)
                total = jnp.sum(exps, axis=-1, keepdims=True)
                probs = (exps * (1.0 / total)).astype(BF16)
                self.probs[layer, 2 * j + parity, :ROWS] = probs
                mixed = mixed + mm(probs, keep_half(v, parity))
            self.o[layer, :, lanes(j * 128, 128)] = mixed.astype(BF16)

        def pairs(i, _):
            for j in range(3):
                pair(3 * i + j)
            return 0

        lax.fori_loop(0, 2, pairs, 0)
        self.finish(s, self.o.at[layer], self.w[s, :, :, :, 2304:].reshape(D, D))

    def dense_forward(self, s):
        layer = s // 2
        self.normed(s)

        def up(j, _):
            columns = lanes(j * 1024, 1024)
            u = mm(self.n[0], self.w[s, :, :, :, columns].reshape(D, 1024))
            act, slope = gelu_pair(u)
            self.a[layer, :, columns] = act.astype(BF16)
            self.slope[layer, :, columns] = slope.astype(BF16)
            return 0

        lax.fori_loop(0, 3, up, 0)
        self.finish(s, self.a.at[layer], self.w2[...])

    def enter(self, s):
        g = self.g[...].astype(F32)
        row = 8 + 3 * s
        self.small[row : row + 1, :] = jnp.sum(g * self.p[s].astype(F32), axis=0, keepdims=True)
        dp = (g * self.vecs[s, 2:3, :]).astype(BF16)
        self.dp[...] = dp
        self.normed(s)
        if s % 2 == 0:
            self.n[1] = self.o[s // 2]
            self.du[:, 2304:] = dp

    def leave(self, s):
        width = 2304 if s % 2 == 0 else FF
        dn = mm_nt(self.du[:, :width], self.w[s, :, :, :, :width].reshape(D, width))
        scaled, inv_std = centre(self.h[s].astype(F32))
        row = 8 + 3 * s
        self.small[row + 1 : row + 2, :] = jnp.sum(dn * scaled, axis=0, keepdims=True)
        self.small[row + 2 : row + 3, :] = jnp.sum(dn, axis=0, keepdims=True)
        e = dn * self.vecs[s, 0:1, :]
        mean_e = jnp.mean(e, axis=-1, keepdims=True)
        mean_ex = jnp.mean(e * scaled, axis=-1, keepdims=True)
        g = self.g[...].astype(F32) + inv_std * (e - mean_e - scaled * mean_ex)
        self.g[...] = g.astype(BF16)

    def put(self, k, mine, route, a1, a2, a3, piece):
        if mine:
            pair = self.pair.at[k % 2, route, a1, a2, a3]
            pair[...] = (piece + pair[...].astype(F32)).astype(BF16)
        else:
            self.stage[k % 2, route, a1, a2, a3] = piece.astype(BF16)

    def first_half(self, k, mine):
        half = self.core if mine else 1 - self.core

        def block(i, _):
            if mine:
                self.reduce.swapped(k, i)
            j = half * 2 + i
            left = jnp.where(j >= self.switch, 1, 0)
            grad = mm_tn(self.n[left], self.du[:, lanes(j * 768, 768)])
            for side in range(2):
                for rb in range(16):
                    for route in range(3):
                        top = rb * 48 + route * 16
                        self.put(
                            k, mine, route, rb // 4, rb % 4, 2 * i + side,
                            grad[top : top + 16, 384 * side : 384 * side + 384],
                        )
            if not mine:
                self.reduce.swap(k, i)
            return 0

        lax.fori_loop(0, 2, block, 0)

    def second_half(self, k, mine, layer):
        half = self.core if mine else 1 - self.core

        def block(i, _):
            if mine:
                self.reduce.swapped(k, i)
            grad = mm_tn(self.a[layer, :, lanes(i * 1536, 1536)], self.dp[:, lanes(half * 384, 384)])
            for z_low in range(2):
                z = 2 * i + z_low
                for x in range(4):
                    for y in range(4):
                        top = (z_low * 4 + x) * 192 + y * 24
                        part = jnp.concatenate([grad[top : top + 24], grad[top + 96 : top + 120]], axis=0)
                        self.put(k, mine, 0, x, y, z, part[0:16])
                        self.put(k, mine, 1, y, z, x, part[16:32])
                        self.put(k, mine, 2, z, x, y, part[32:48])
            if not mine:
                self.reduce.swap(k, i)
            return 0

        lax.fori_loop(0, 2, block, 0)

    def down(self, s):
        layer = s // 2

        def block(j, _):
            columns = lanes(j * 1536, 1536)
            rows = pl.ds(pl.multiple_of(j * 1536, 256), 1536)
            da = mm_nt(self.dp[...], self.w2[rows, :])
            self.du[:, columns] = (da * self.slope[layer, :, columns].astype(F32)).astype(BF16)
            return 0

        lax.fori_loop(0, 2, block, 0)

    def back_out(self, s):
        weights = self.w[s, :, :, :, 2304:].reshape(D, D)
        self.dp[...] = mm_nt(self.du[:, 2304:], weights).astype(BF16)

    def pairs(self, s, third):
        layer = s // 2

        def pair(j):
            q = self.qkv[layer, :ROWS, lanes(j * 128, 128)]
            k = self.qkv[layer, :, lanes(768 + j * 128, 128)]
            v = self.qkv[layer, :, lanes(1536 + j * 128, 128)]
            do = self.dp[:, lanes(j * 128, 128)]
            dq = jnp.zeros((ROWS, 128), F32)
            dk = jnp.zeros((KEYS, 128), F32)
            dv = jnp.zeros((KEYS, 128), F32)
            for parity in range(2):
                do_half = keep_half(do, parity)
                probs = self.probs[layer, 2 * j + parity, :ROWS]
                wide = probs.astype(F32)
                d_probs = mm_nt(do_half, v)
                inner = jnp.sum(d_probs * wide, axis=-1, keepdims=True)
                d_scores = (wide * (d_probs - inner)).astype(BF16)
                dv = dv + mm_tn(probs, do_half)
                dq = dq + mm(d_scores, keep_half(k, parity))
                dk = dk + mm_tn(d_scores, keep_half(q, parity))
                self.probs[layer, 2 * j + parity] = mm(self.by_x[...], d_scores).astype(BF16)
            self.du[:, lanes(j * 128, 128)] = (dq * INV_ROOT).astype(BF16)
            self.du[:, lanes(768 + j * 128, 128)] = (dk[:ROWS] * INV_ROOT).astype(BF16)
            self.du[:, lanes(1536 + j * 128, 128)] = dv[:ROWS].astype(BF16)

        def trio(i, _):
            for j in range(3):
                pair(3 * i + j)
            return 0

        lax.fori_loop(third, third + 1, trio, 0)

    def fold_bias(self, s):
        layer = s // 2
        shape = (KEYS, 384)
        token = lax.broadcasted_iota(jnp.int32, shape, 0)
        lane = lax.broadcasted_iota(jnp.int32, shape, 1)
        patch = token - 1
        offset = patch + (SPAN - GRID) * ((patch * 4682) >> 16)
        target = jnp.where(token >= SEQ, -1000, (SPAN + 1) * (GRID - 1) - offset)
        self.sums[...] = jnp.zeros((3, 192, 128), F32)

        def two(i, _):
            lefts, rights = [], []
            for odd in range(2):
                x = 2 * i + odd
                rows = pl.ds(pl.multiple_of(16 * x, 16), 16)
                lefts.append(self.probs[layer, :, rows, :].reshape(192, KEYS))
                here = jnp.where(token == 0, 383, target + x)
                rights.append(jnp.where(lane == here, 1.0, 0.0).astype(BF16))
            more = mm(jnp.concatenate(lefts, axis=1), jnp.concatenate(rights, axis=0))
            for t in range(3):
                self.sums[t] += more[:, 128 * t : 128 * t + 128]
            return 0

        lax.fori_loop(0, GRID // 2, two, 0)
        last = lax.broadcasted_iota(jnp.int32, (HEADS, 384), 1) == 383
        total = jnp.zeros((HEADS, D), F32)
        side = jnp.zeros((HEADS, 1), F32)
        for y in range(GRID + 1):
            rows = jnp.concatenate([self.sums[t, pl.ds(y, HEADS, stride=16), :] for t in range(3)], axis=1)
            plain = jnp.where(last, 0.0, rows)
            if y < GRID:
                side = side + jnp.sum(rows - plain, axis=1, keepdims=True)
                wide = jnp.concatenate([plain, jnp.zeros((HEADS, 384), F32)], axis=1)
                total = total + (pltpu.roll(wide, SPAN * y, 1) if y else wide)
            else:
                top = jnp.sum(plain, axis=1, keepdims=True)
                corner = jnp.sum(rows - plain, axis=1, keepdims=True)
        entry = lax.broadcasted_iota(jnp.int32, (HEADS, D), 1)
        total = jnp.where(entry == 729, top, total)
        total = jnp.where(entry == 730, side, total)
        total = jnp.where(entry == 731, corner, total)
        self.small[24 + layer * HEADS : 24 + (layer + 1) * HEADS, :] = total


MESH = pl.DeviceIdType.MESH
AXES = ("x", "y", "z")
ROUTES = (("x", "y", "z"), ("y", "z", "x"), ("z", "x", "y"))
ORDER = (5, 3, 2, 4, 1, 0)


class Place:
    def __init__(self):
        dp = lax.axis_index("dp")
        self.at = {"z": dp // 8, "x": (dp // 2) % 4, "c": dp % 2, "y": lax.axis_index("section")}

    def go(self, axis, step):
        at = dict(self.at)
        at[axis] = (at[axis] + step) % (2 if axis == "c" else 4)
        return ((at["z"] * 4 + at["x"]) * 2 + at["c"], at["y"])

    def index(self, axis, step=0):
        return (self.at[axis] + step) % 4


def meet(place):
    barrier = pltpu.get_barrier_semaphore()
    count = 0
    for axis in AXES:
        for step in (1, 2, 3):
            pl.semaphore_signal(barrier, inc=1, device_id=place.go(axis, step), device_id_type=MESH)
            count += 1
    pl.semaphore_signal(barrier, inc=1, device_id=place.go("c", 1), device_id_type=MESH)
    pl.semaphore_wait(barrier, count + 1)


class Reduce:
    def __init__(self, place, **refs):
        self.place = place
        self.__dict__.update(refs)
        self.flying = {}

    def send(self, key, src, dst, number, device):
        k = key[1]
        copy = pltpu.make_async_remote_copy(
            src_ref=src, dst_ref=dst, send_sem=self.sems.at[0, k, number], recv_sem=self.sems.at[1, k, number],
            device_id=device, device_id_type=MESH,
        )
        copy.start()
        self.flying[key] = copy

    def sent(self, k, names):
        for name in names:
            for r in range(3):
                self.flying[(name, k, r)].wait_send()

    def part(self, buffer, k, i):
        pair = pl.ds(2 * i, 2)
        if ORDER[k] < 4:
            return [(3 * i, buffer.at[k % 2, :, :, :, pair])]
        return [
            (3 * i, buffer.at[k % 2, 0, :, :, pair]),
            (3 * i + 1, buffer.at[k % 2, 1, :, pair]),
            (3 * i + 2, buffer.at[k % 2, 2, pair]),
        ]

    def across(self, k, i):
        for (number, source), (_, target) in zip(self.part(self.stage, k, i), self.part(self.pair, k, i)):
            yield pltpu.make_async_remote_copy(
                src_ref=source, dst_ref=target, send_sem=self.sems.at[0, k, number],
                recv_sem=self.sems.at[1, k, number], device_id=self.place.go("c", 1), device_id_type=MESH,
            )

    def prepare(self, k):
        if k >= 2:
            self.swap_sent(k - 2)
            pl.semaphore_wait(self.pair_credit, 1)

    def swap(self, k, i):
        for copy in self.across(k, i):
            copy.start()

    def swapped(self, k, i):
        for copy in self.across(k, i):
            copy.wait_recv()

    def swap_sent(self, k):
        for i in range(2):
            for copy in self.across(k, i):
                copy.wait_send()

    def first(self, k):
        place = self.place
        for r, (axis, _, _) in enumerate(ROUTES):
            own, far = self.pair.at[k % 2, r], self.far.at[k % 2, r]
            across, ahead, behind = place.index(axis, 2), place.index(axis, 1), place.index(axis, 3)
            up, down = place.go(axis, 1), place.go(axis, 3)
            base = 6 + 6 * r
            if k >= 2:
                pl.semaphore_wait(self.far_credit.at[r, 0], 1)
                pl.semaphore_wait(self.far_credit.at[r, 1], 1)
            self.send(("fa", k, r), own.at[across, 0:2], far.at[0], base, up)
            self.send(("fb", k, r), own.at[across, 2:4], far.at[1], base + 1, down)
            self.send(("db", k, r), own.at[ahead, 2:4], far.at[2], base + 2, up)
            self.send(("da", k, r), own.at[behind, 0:2], far.at[3], base + 3, down)

    def merge(self, k):
        place = self.place
        for r, (axis, _, _) in enumerate(ROUTES):
            own, far = self.pair.at[k % 2, r], self.far.at[k % 2, r]
            ahead, behind = place.index(axis, 1), place.index(axis, 3)
            base = 6 + 6 * r
            self.flying[("fa", k, r)].wait_recv()
            far[0] = (far[0].astype(F32) + own[ahead, 0:2].astype(F32)).astype(BF16)
            self.send(("ma", k, r), far.at[0], far.at[4], base + 4, place.go(axis, 1))
            self.flying[("fb", k, r)].wait_recv()
            far[1] = (far[1].astype(F32) + own[behind, 2:4].astype(F32)).astype(BF16)
            self.send(("mb", k, r), far.at[1], far.at[5], base + 5, place.go(axis, 3))

    def second(self, k):
        place = self.place
        for r, (axis, nxt, _) in enumerate(ROUTES):
            for name in ("db", "da", "ma", "mb"):
                self.flying[(name, k, r)].wait_recv()
            own, far = self.pair.at[k % 2, r], self.far.at[k % 2, r]
            me = place.index(axis)
            low = own[me, 0:2].astype(F32) + far[4].astype(F32) + far[3].astype(F32)
            high = own[me, 2:4].astype(F32) + far[2].astype(F32) + far[5].astype(F32)
            line, line_in = self.line.at[k % 2, r], self.line_in.at[k, r]
            line[0:2] = low.astype(BF16)
            line[2:4] = high.astype(BF16)
            for step in (1, 2, 3):
                self.send(
                    (("s", step), k, r), line.at[place.index(nxt, step)], line_in.at[step - 1],
                    24 + 3 * r + step - 1, place.go(nxt, step),
                )
        self.sent(k, ("fa", "fb", "db", "da", "ma", "mb"))
        if k + 2 < 6:
            pl.semaphore_signal(self.pair_credit, inc=1, device_id=place.go("c", 1), device_id_type=MESH)
            for r, (axis, _, _) in enumerate(ROUTES):
                pl.semaphore_signal(self.far_credit.at[r, 0], inc=1, device_id=place.go(axis, 1), device_id_type=MESH)
                pl.semaphore_signal(self.far_credit.at[r, 1], inc=1, device_id=place.go(axis, 3), device_id_type=MESH)

    def third(self, k):
        place = self.place
        for r, (_, axis, nxt) in enumerate(ROUTES):
            line, line_in, spot, spot_in = self.line.at[k % 2, r], self.line_in.at[k, r], self.spot.at[k % 2, r], self.spot_in.at[k, r]
            total = line[place.index(axis)].astype(F32)
            for step in (1, 2, 3):
                self.flying[(("s", step), k, r)].wait_recv()
                total = total + line_in[step - 1].astype(F32)
            spot[...] = total.astype(BF16)
            for step in (1, 2, 3):
                self.send(
                    (("t", step), k, r), spot.at[place.index(nxt, step)], spot_in.at[step - 1],
                    33 + 3 * r + step - 1, place.go(nxt, step),
                )
        self.sent(k, (("s", 1), ("s", 2), ("s", 3)))

    def close(self, k):
        place, tensor = self.place, ORDER[k]
        for r, (_, _, axis) in enumerate(ROUTES):
            spot, spot_in = self.spot.at[k % 2, r], self.spot_in.at[k, r]
            total = spot[place.index(axis)].astype(F32)
            for step in (1, 2, 3):
                self.flying[(("t", step), k, r)].wait_recv()
                total = total + spot_in[step - 1].astype(F32)
            if tensor < 4:
                self.first_out[tensor, 0, 0, r] = total.astype(BF16)
            else:
                rows = self.rows.at[tensor - 4]
                if r == 0:
                    rows[0, 0:16] = total
                elif r == 1:
                    rows[0, 16:24] = total[0:8]
                    rows[1, 0:8] = total[8:16]
                else:
                    rows[1, 8:24] = total
        self.sent(k, (("t", 1), ("t", 2), ("t", 3)))
        if tensor >= 4:
            layer, me = tensor - 4, place.at["c"]
            self.send(("r", k, 0), self.rows.at[layer, 1 - me], self.rows_in.at[layer], 42, place.go("c", 1))

    def finish(self):
        me = self.place.at["c"]
        for k, tensor in enumerate(ORDER):
            if tensor >= 4:
                self.flying[("r", k, 0)].wait()
                layer = tensor - 4
                self.second_out[layer, :, lanes(me * 384, 384)] = self.rows[layer, me]
                self.second_out[layer, :, lanes((1 - me) * 384, 384)] = self.rows_in[layer]
        for k in (4, 5):
            self.swap_sent(k)


class Totals:
    def __init__(self, place, part, bufs, sems):
        self.place, self.part, self.bufs, self.sems = place, part, bufs, sems
        self.copies = []

    def send(self, src, dst, number, device):
        copy = pltpu.make_async_remote_copy(
            src_ref=src, dst_ref=dst, send_sem=self.sems.at[0, number], recv_sem=self.sems.at[1, number],
            device_id=device, device_id_type=MESH,
        )
        copy.start()
        self.copies.append(copy)
        return copy

    @staticmethod
    def half(core):
        return pl.ds(pl.multiple_of(core * 24, 8), 24)

    def start(self, small):
        me = self.place.at["c"]
        self.small = small
        self.now = [self.send(small.at[self.half(1 - me)], self.bufs.at[0, 0], 0, self.place.go("c", 1))]

    def step(self, number):
        place, me = self.place, self.place.at["c"]
        for copy in self.now:
            copy.wait_recv()
        if number == 0:
            self.part[...] = self.small[self.half(me), :] + self.bufs[0, 0]
        else:
            axis = AXES[number - 1]
            self.bufs[number, place.at[axis]] = self.part[...]
            self.part[...] = (self.bufs[number, 0] + self.bufs[number, 1]) + (self.bufs[number, 2] + self.bufs[number, 3])
        if number < 3:
            axis = AXES[number]
            self.now = [
                self.send(self.part, self.bufs.at[number + 1, place.at[axis]], 1 + 3 * number + step - 1, place.go(axis, step))
                for step in (1, 2, 3)
            ]
            for copy in self.now:
                copy.wait_send()
        else:
            self.now = [self.send(self.part, self.bufs.at[0, 1], 10, place.go("c", 1))]

    def close(self, out):
        me = self.place.at["c"]
        for copy in self.now:
            copy.wait_recv()
        out[self.half(me), :] = self.part[...]
        out[self.half(1 - me), :] = self.bufs[0, 1]
        self.copies[0].wait_send()
        self.copies[-1].wait_send()


class Spread:
    def __init__(self, place, sems):
        self.place, self.sems = place, sems
        self.sent = []

    def make(self, number, src, dst, device):
        return pltpu.make_async_remote_copy(
            src_ref=src, dst_ref=dst, send_sem=self.sems.at[0, number], recv_sem=self.sems.at[1, number],
            device_id=device, device_id_type=MESH,
        )

    def send(self, number, src, dst, device):
        copy = self.make(number, src, dst, device)
        copy.start()
        self.sent.append(copy)

    def wait(self, number, ref):
        pltpu.make_async_remote_copy(
            src_ref=ref, dst_ref=ref, send_sem=self.sems.at[0, number], recv_sem=self.sems.at[1, number],
            device_id=self.place.go("c", 1), device_id_type=MESH,
        ).wait_recv()

    def drain(self):
        for copy in self.sent:
            copy.wait_send()


GATHER_MESSAGES = 99


class Gather(Spread):
    def __init__(self, place, full, sems):
        super().__init__(place, sems)
        self.full = full
        y = place.at["y"]
        self.first = {"x": 3, "z": 1}
        self.second = {"x": jnp.where(y == 3, 1, 2), "z": jnp.where(y == 1, 3, 2)}
        self.third = {"x": jnp.where(y == 3, 2, 1), "z": jnp.where(y == 1, 2, 3)}

    def rows(self, route, step, sub=None, core=None):
        core = self.place.at["c"] if core is None else core
        block = (0 if route == "x" else 8) + self.place.index(route, step) * 2 + core
        return (block // 4, block % 4, slice(None) if sub is None else slice(16 * sub, 16 * sub + 16))

    def ref(self, rel, route, step, sub=None):
        return self.full.at[(self.place.index("y", rel),) + self.rows(route, step, sub)]

    @staticmethod
    def along_y(rel, route, sub):
        return 3 * (2 * (rel - 1) + (route == "z")) + sub

    @staticmethod
    def in_plane(rel, route, kind, sub):
        return 18 + 9 * (2 * (rel - 1) + (route == "z")) + 3 * kind + sub

    @staticmethod
    def across(rel, route, step):
        return 72 + 4 * (2 * (rel - 1) + (route == "z")) + step

    def load(self, source, sems):
        at = self.place.at
        mine, rest = [], []
        for half, route in enumerate(("x", "z")):
            for block in range(8):
                number = 8 * half + (at[route] * 2 + at["c"] + block) % 8
                rows = pl.ds(pl.multiple_of(number * 48, 16), 48)
                copy = pltpu.make_async_copy(
                    source.at[rows], self.full.at[at["y"], number // 4, number % 4], sems.at[half, block]
                )
                (rest if block else mine).append(copy)
        for copy in mine + rest:
            copy.start()
        for copy in mine:
            copy.wait()
        return rest

    def own(self, up, down):
        copies = []
        for sub in range(3):
            for route, step in ((up, 1), (down, 3)):
                mine = self.ref(0, route, 0, sub)
                copies.append(self.make(self.along_y(4 - step, route, sub), mine, mine, self.place.go("y", step)))
        self.sent += copies
        return copies

    def arrive(self, rels):
        for sub in range(3):
            for route, rel in rels.items():
                piece = self.ref(rel, route, 0, sub)
                self.wait(self.along_y(rel, route, sub), piece)
                if rels is self.first:
                    self.send(self.along_y(2, route, sub), piece, piece, self.place.go("y", 4 - rel))
                for kind, step in ((0, 1), (1, 3)):
                    self.send(self.in_plane(rel, route, kind, sub), piece, piece, self.place.go(route, step))
        for route, rel in rels.items():
            piece = self.ref(rel, route, 0)
            self.send(self.across(rel, route, 0), piece, piece, self.place.go("c", 1))

    def turn(self, rels):
        place = self.place
        clockwise = 1 - 2 * place.at["c"]
        for sub, way in ((0, 1), (1, clockwise), (2, -1)):
            for route, rel in rels.items():
                for kind, step in ((0, 3), (1, 1)):
                    self.wait(self.in_plane(rel, route, kind, sub), self.ref(rel, route, step, sub))
                piece = self.ref(rel, route, 4 - way, sub)
                self.send(self.in_plane(rel, route, 2, sub), piece, piece, place.go(route, 4 + way))
        for route, rel in rels.items():
            for step in (3, 1):
                piece = self.ref(rel, route, step)
                self.send(self.across(rel, route, step), piece, piece, place.go("c", 1))

    def end(self, rels):
        for route, rel in rels.items():
            for sub in range(3):
                self.wait(self.in_plane(rel, route, 2, sub), self.ref(rel, route, 2, sub))
            piece = self.ref(rel, route, 2)
            self.send(self.across(rel, route, 2), piece, piece, self.place.go("c", 1))

    def settle(self, section):
        rel = (section - self.place.at["y"] + 4) % 4
        other = 1 - self.place.at["c"]

        def run():
            for route in ("x", "z"):
                for step in range(4):
                    self.wait(self.across(rel, route, step), self.full.at[(section,) + self.rows(route, step, core=other)])

        pl.when(rel > 0)(run)


def layers_kernel(
    tokens, masked, cotangent, live, mask_token, norm_gain, norm_shift, layer_scale, w_own, w2_hbm,
    table, corner, select_f, by_x,
    block_out, tokens_grad, first_grad, second_out, totals,
    w, w2, h, qkv, probs, o, a, slope, p, n, bias, fold, fold_sums, du, dp, g, vec, vecs, small,
    stage, pair, far, line, line_in, spot, spot_in, rows, rows_in, part, bufs, first_out,
    load_sems, w2_sems, gather_sems, sems, small_sems, share_sems, share_out_sems, pair_credit, far_credit,
):
    place = Place()
    vec[0:1] = norm_gain[...]
    vec[1:2] = norm_shift[...]
    vec[2:3] = layer_scale[...]
    vec[3:8] = jnp.zeros((5, D), F32)
    meet(place)
    y = place.at["y"]
    gather = Gather(place, w, gather_sems)
    own_rest = gather.load(w_own.at[0], load_sems)
    for copy in gather.own("x", "z"):
        copy.start()
    own_later = gather.own("z", "x")

    @pl.when(y == 0)
    def _():
        for copy in own_later:
            copy.start()

    def load_second(layer):
        copies = []
        for block in range(8):
            rows = pl.ds(block * 384, 384)
            copies.append(pltpu.make_async_copy(w2_hbm.at[layer, rows], w2.at[rows], w2_sems.at[block]))
            copies[-1].start()
        return copies

    def loaded(copies):
        for copy in copies:
            copy.wait()

    w2_load = load_second(0)
    vecs[y] = vec[...]
    for step in (1, 2, 3):
        gather.send(95 + step, vec, vecs.at[y], place.go("y", step))
    valid = jnp.where(y < live[lax.axis_index("dp")], 1.0, 0.0)
    body = Body(
        valid=valid, core=place.at["c"], vecs=vecs, table=table, corner=corner,
        select_forward=select_f, by_x=by_x, block_out=block_out, small=small,
        w=w, w2=w2, h=h, qkv=qkv, probs=probs, o=o, a=a, slope=slope, p=p, n=n, bias=bias,
        fold=fold, sums=fold_sums, du=du, dp=dp, g=g, stage=stage, pair=pair,
    )
    reduce = Reduce(
        place, stage=stage, pair=pair, far=far, line=line, line_in=line_in, spot=spot, spot_in=spot_in,
        rows=rows, rows_in=rows_in, first_out=first_out, second_out=second_out, sems=sems,
        pair_credit=pair_credit, far_credit=far_credit,
    )
    body.reduce = reduce
    sums = Totals(place, part, bufs, small_sems)

    gather.arrive(gather.first)

    @pl.when(y != 0)
    def _():
        for copy in own_later:
            copy.start()

    fold[...] = jnp.zeros_like(fold)
    square = (ROWS, KEYS)
    diagonal = lax.broadcasted_iota(jnp.int32, square, 0) == lax.broadcasted_iota(jnp.int32, square, 1)
    flags = jnp.concatenate([masked[...].astype(F32), jnp.zeros((1, KEYS - SEQ), F32)], axis=1)
    here = jnp.sum(jnp.where(diagonal, flags, 0.0), axis=1, keepdims=True)
    h[0, 192:] = jnp.zeros((16, D), BF16)
    start = tokens[0].astype(F32)
    h[0, :SEQ] = (start + here[:SEQ] * (mask_token[...].astype(F32) - start)).astype(BF16)
    g[192:] = jnp.zeros((16, D), BF16)
    g[:SEQ] = (cotangent[0].astype(F32) * valid).astype(BF16)
    body.expand_bias(0, 0, 6)
    gather.arrive(gather.second)
    body.expand_bias(0, 6, 12)
    gather.turn(gather.first)
    body.expand_bias(1, 0, 6)
    gather.arrive(gather.third)
    gather.turn(gather.second)
    body.expand_bias(1, 6, 12)
    gather.end(gather.first)
    gather.end(gather.second)
    for step in (1, 2, 3):
        gather.wait(95 + step, vecs.at[place.index("y", 4 - step)])
    loaded(own_rest)
    gather.turn(gather.third)
    gather.settle(0)
    body.attend_forward(0)
    gather.end(gather.third)
    gather.settle(1)
    loaded(w2_load)
    body.dense_forward(1)
    w2_load = load_second(1)
    gather.settle(2)
    body.attend_forward(2)
    gather.settle(3)
    loaded(w2_load)
    body.dense_forward(3)
    gather.drain()

    body.switch = 4
    body.enter(3)
    body.second_half(0, False, 1)
    body.down(3)
    w2_load = load_second(0)
    body.second_half(0, True, 1)
    reduce.first(0)
    body.first_half(1, False)
    body.leave(3)
    reduce.merge(0)
    body.first_half(1, True)
    reduce.first(1)
    body.switch = 3
    body.enter(2)
    body.back_out(2)
    body.pairs(2, 0)
    reduce.second(0)
    body.pairs(2, 1)
    reduce.merge(1)
    body.fold_bias(2)
    reduce.third(0)
    reduce.prepare(2)
    body.first_half(2, False)
    body.leave(2)
    reduce.second(1)
    body.first_half(2, True)
    reduce.first(2)
    reduce.close(0)
    body.switch = 4
    body.enter(1)
    reduce.prepare(3)
    body.second_half(3, False, 0)
    reduce.third(1)
    loaded(w2_load)
    body.down(1)
    reduce.merge(2)
    body.second_half(3, True, 0)
    reduce.first(3)
    reduce.second(2)
    reduce.prepare(4)
    body.first_half(4, False)
    reduce.close(1)
    body.leave(1)
    reduce.merge(3)
    body.first_half(4, True)
    reduce.first(4)
    body.switch = 3
    body.enter(0)
    body.back_out(0)
    reduce.third(2)
    body.pairs(0, 0)
    reduce.second(3)
    reduce.merge(4)
    body.pairs(0, 1)
    reduce.close(2)
    reduce.prepare(5)
    body.first_half(5, False)
    reduce.third(3)
    body.fold_bias(0)
    body.leave(0)
    grad = g[...].astype(F32)
    tokens_grad[0] = (grad * (1.0 - here)).astype(BF16)[:SEQ]
    small[20:21, :] = jnp.sum(grad * here, axis=0, keepdims=True)
    small[21:24, :] = jnp.zeros((3, D), F32)
    sums.start(small)
    reduce.second(4)
    body.first_half(5, True)
    reduce.first(5)
    reduce.close(3)
    sums.step(0)
    reduce.third(4)
    reduce.merge(5)
    sums.step(1)
    reduce.close(4)
    reduce.second(5)
    sums.step(2)
    reduce.third(5)
    sums.step(3)
    reduce.close(5)
    sums.close(totals)
    Share(place, first_out, w.at[3], share_sems).run(first_grad, share_out_sems)
    reduce.finish()


def layers(tokens, masked, cotangent, live, mask_token, norm_gain, norm_shift, layer_scale, w_own, w2, table, corner):
    select_f, by_x = selectors()
    vm = pl.BlockSpec(memory_space=pltpu.VMEM)
    hbm = pl.BlockSpec(memory_space=pl.ANY)
    sm = pl.BlockSpec(memory_space=pltpu.SMEM)
    V, DMA, REGULAR = pltpu.VMEM, pltpu.SemaphoreType.DMA, pltpu.SemaphoreType.REGULAR
    return pl.pallas_call(
        layers_kernel,
        out_shape=(
            jax.ShapeDtypeStruct((1, SEQ, D), BF16),
            jax.ShapeDtypeStruct((1, SEQ, D), BF16),
            jax.ShapeDtypeStruct((4, 4, 48, FF), BF16),
            jax.ShapeDtypeStruct((2, 24, D), F32),
            jax.ShapeDtypeStruct((48, D), F32),
        ),
        in_specs=[vm, vm, vm, sm, vm, vm, vm, vm, hbm, hbm, vm, vm, vm, vm],
        out_specs=(vm, vm, hbm, vm, vm),
        scratch_shapes=[
            V((4, 4, 4, 48, FF), BF16), V((FF, D), BF16), V((4, ROWS, D), BF16), V((2, KEYS, 2304), BF16),
            V((2, HEADS, 16 * GRID, KEYS), BF16), V((2, ROWS, D), BF16), V((2, ROWS, FF), BF16), V((2, ROWS, FF), BF16),
            V((4, ROWS, D), BF16), V((2, ROWS, D), BF16), V((2, HEADS, ROWS, KEYS), BF16),
            V((ROWS, 384), F32), V((3, 192, 128), F32), V((ROWS, FF), BF16), V((ROWS, D), BF16), V((ROWS, D), BF16),
            V((8, D), F32), V((4, 8, D), F32), V((48, D), F32),
            V((2,) + HALF, BF16), V((2,) + HALF, BF16), V((2, 3, 6, 2, 4, 16, 384), BF16),
            V((2, 3, 4, 4, 16, 384), BF16), V((6, 3, 3, 4, 16, 384), BF16),
            V((2, 3, 4, 16, 384), BF16), V((6, 3, 3, 16, 384), BF16),
            V((2, 2, 24, 384), F32), V((2, 24, 384), F32), V((24, D), F32), V((4, 4, 24, D), F32),
            V((4, 1, 1, 3, 16, 384), BF16),
            DMA((2, 8)), DMA((8,)), DMA((2, GATHER_MESSAGES)), DMA((2, 6, 43)), DMA((2, 11)), DMA((2, 69)), DMA((4,)), REGULAR, REGULAR((3, 2)),
        ],
        compiler_params=pltpu.CompilerParams(
            collective_id=1, has_side_effects=True, vmem_limit_bytes=64 * 2**20
        ),
    )(tokens, masked, cotangent, live, mask_token, norm_gain, norm_shift, layer_scale, w_own, w2, table, corner, select_f, by_x)


class Share(Spread):
    def __init__(self, place, blocks, full, sems):
        super().__init__(place, sems)
        self.blocks, self.full = blocks, full

    def regions(self, c, x, y, z):
        def columns(third):
            return pl.ds(pl.multiple_of((c * 4 + third[0]) * 384, 128), third[1] * 384)

        for route, (a1, a2, a3) in enumerate(((x, y, z), (y, z, x), (z, x, y))):
            yield route, self.full.at[
                pl.ds(*a1), pl.ds(*a2), slice(16 * route, 16 * route + 16), columns(a3)
            ]

    def pass_on(self, base, regions, device):
        for route, region in regions:
            self.send(base + route, region, region, device)

    def await_all(self, base, regions):
        for route, region in regions:
            self.wait(base + route, region)

    def run(self, out, out_sems):
        place = self.place
        at = place.at
        c, x, y, z = at["c"], (at["x"], 1), (at["y"], 1), (at["z"], 1)
        every = (0, 4)
        halves = ((0, 2), (2, 2))

        def near(axis, step):
            return (place.index(axis, step), 1)

        for route, region in self.regions(c, x, y, z):
            for step in (1, 2, 3):
                source = self.blocks.at[place.index("y", step), :, :, route]
                self.send(3 * (step - 1) + route, source, region, place.go("y", step))
            region[...] = self.blocks[at["y"], :, :, route]
        for step in (1, 2, 3):
            self.await_all(3 * (step - 1), self.regions(c, x, near("y", 4 - step), z))
        for step in (1, 3, 2):
            self.pass_on(9 + 3 * (step - 1), self.regions(c, x, halves[0], z), place.go("x", step))
            self.pass_on(18 + 3 * (step - 1), self.regions(c, x, halves[1], z), place.go("z", step))
        for step in (1, 3, 2):
            self.await_all(9 + 3 * (step - 1), self.regions(c, near("x", 4 - step), halves[0], z))
            self.await_all(18 + 3 * (step - 1), self.regions(c, x, halves[1], near("z", 4 - step)))
        for step in (1, 3, 2):
            self.pass_on(27 + 3 * (step - 1), self.regions(c, every, halves[0], z), place.go("z", step))
            self.pass_on(36 + 3 * (step - 1), self.regions(c, x, halves[1], every), place.go("x", step))
        self.pass_on(45, self.regions(c, every, halves[0], z), place.go("c", 1))
        self.pass_on(48, self.regions(c, x, halves[1], every), place.go("c", 1))
        for step in (1, 3, 2):
            got = list(self.regions(c, every, halves[0], near("z", 4 - step)))
            self.await_all(27 + 3 * (step - 1), got)
            self.pass_on(51 + 3 * (step - 1), got, place.go("c", 1))
            got = list(self.regions(c, near("x", 4 - step), halves[1], every))
            self.await_all(36 + 3 * (step - 1), got)
            self.pass_on(60 + 3 * (step - 1), got, place.go("c", 1))
        other = 1 - c
        self.await_all(45, self.regions(other, every, halves[0], z))
        self.await_all(48, self.regions(other, x, halves[1], every))
        for step in (1, 3, 2):
            self.await_all(51 + 3 * (step - 1), self.regions(other, every, halves[0], near("z", 4 - step)))
            self.await_all(60 + 3 * (step - 1), self.regions(other, near("x", 4 - step), halves[1], every))
        copies = [pltpu.make_async_copy(self.full.at[a], out.at[a], out_sems.at[a]) for a in range(4)]
        for copy in copies:
            copy.start()
        for copy in copies:
            copy.wait()
        self.drain()


def on_device(
    tokens, masked, live_images, mask_token, norm_gain, norm_shift, w_first, w_second, layer_scale, rel_table, cotangent
):
    table = jnp.transpose(rel_table, (0, 2, 1)).reshape(2 * HEADS, -1)
    turned = jnp.pad(table[:, : SPAN * SPAN][:, ::-1], ((0, 0), (0, 768 - SPAN * SPAN)))
    corner = jnp.pad(table[:, SPAN * SPAN :], ((0, 0), (0, 125)))
    block_out, tokens_grad, first, second, totals = layers(
        tokens, masked, cotangent, live_images, mask_token.reshape(1, D), norm_gain, norm_shift, layer_scale,
        w_first, w_second, turned, corner,
    )
    first_grad = first.reshape(D, FF).astype(F32)
    count = jnp.sum(live_images).astype(F32) * (SEQ * D)
    rms = jnp.sqrt(jnp.sum(totals[:8], axis=1) / count).reshape(4, 2)
    own = lax.dynamic_slice(totals, (8 + 3 * lax.axis_index("section"), 0), (3, D))
    table_grad = jnp.transpose(totals[24:].reshape(2, HEADS, D)[:, :, :732], (0, 2, 1))
    return (
        block_out, tokens_grad, first_grad[None], second,
        own[1:2], own[2:3], own[0:1], table_grad, totals[20], rms,
    )


def solution(mesh):
    both = P(("dp", "section"), None, None)
    part = P("section", None)
    return jax.shard_map(
        on_device,
        mesh=mesh,
        in_specs=(both, P(("dp", "section"), None), P(), P(), part, part, P("section", None, None), P(), part, P(), both),
        out_specs=(
            both, both, P("section", None, None), P(None, ("dp", "section"), None), part, part, part, P(), P(), P(),
        ),
        check_vma=False,
    )
```

```python
import functools
import math

import jax
import jax.numpy as jnp
from jax import lax
from jax.experimental import pallas as pl
from jax.experimental.pallas import tpu as pltpu
from jax.sharding import PartitionSpec as P

SEQ, ROWS, KEYS = 197, 208, 256
D, FF, HEADS, GRID = 768, 3072, 12, 14
SPAN = 2 * GRID - 1
EPSILON = 1e-06
INV_ROOT = 0.125
INV_ROOT_TWO_PI = 0.3989422804014327
F32, BF16 = jnp.float32, jnp.bfloat16
HALF = (3, 4, 4, 4, 16, 384)


def mm(a, b):
    return lax.dot_general(a, b, (((1,), (0,)), ((), ())), preferred_element_type=F32)


def mm_nt(a, b):
    return lax.dot_general(a, b, (((1,), (1,)), ((), ())), preferred_element_type=F32)


def mm_tn(a, b):
    return lax.dot_general(a, b, (((0,), (0,)), ((), ())), preferred_element_type=F32)


def lanes(start, size):
    return pl.ds(pl.multiple_of(start, 128), size)


def patch_offsets(token):
    patch = token - 1
    return patch + (SPAN - GRID) * ((patch * 4682) >> 16)


def ones(condition):
    return jnp.where(condition, 1.0, 0.0).astype(BF16)


def centre(h):
    average = jnp.mean(h, axis=-1, keepdims=True)
    centred = h - average
    inv_std = lax.rsqrt(jnp.mean(centred * centred, axis=-1, keepdims=True) + EPSILON)
    return centred * inv_std, inv_std


def gelu_pair(u):
    size = jnp.abs(u)
    t = 1.0 / (1.0 + 0.23164189 * size)
    bell = jnp.exp(-0.5 * u * u)
    poly = t * (
        0.127414796
        + t * (-0.142248368 + t * (0.7107068705 + t * (-0.7265760135 + t * 0.5307027145)))
    )
    tail = poly * bell
    phi = jnp.where(u >= 0.0, 1.0 - tail, tail)
    return u * phi, phi + u * bell * INV_ROOT_TWO_PI


def half_mask(rows, parity):
    lane = lax.broadcasted_iota(jnp.int32, (rows, 128), 1)
    return (lane < 64) if parity == 0 else (lane >= 64)


def keep_half(block, parity):
    return jnp.where(half_mask(block.shape[0], parity), block, jnp.zeros_like(block))


class Body:
    def __init__(self, **refs):
        self.__dict__.update(refs)

    def make_selectors(self):
        row = lax.broadcasted_iota(jnp.int32, (384, KEYS), 0)
        token = lax.broadcasted_iota(jnp.int32, (384, KEYS), 1)
        self.select_forward[...] = ones((row == patch_offsets(token)) & (token > 0) & (token < SEQ))
        row = lax.broadcasted_iota(jnp.int32, (16 * GRID, ROWS), 0)
        token = lax.broadcasted_iota(jnp.int32, (16 * GRID, ROWS), 1)
        patch = token - 1
        y = (patch * 4682) >> 16
        wanted = jnp.where(token == 0, GRID, (patch - GRID * y) * 16 + y)
        self.by_x[...] = ones((row == wanted) & (token < SEQ))

    def read_tables(self, tables):
        shape = (tables.shape[2], 896)
        entry = lax.broadcasted_iota(jnp.int32, shape, 0)
        lane = lax.broadcasted_iota(jnp.int32, shape, 1)
        source = jnp.where(lane < 768, SPAN * SPAN - 1 - lane, lane + (SPAN * SPAN - 768))
        select = ones(entry == source)
        for layer in range(2):
            self.table[layer * HEADS : (layer + 1) * HEADS, :] = mm(tables[:, layer, :].astype(BF16), select)

    def expand_bias(self, layer, lo, hi):
        def head(index, _):
            entries = self.table[pl.ds(layer * HEADS + index, 1), :]
            base = jnp.broadcast_to(entries[:, :768], (16, 768))
            base = pltpu.roll(base, 404, 1, stride=1, stride_axis=0)
            for yi in range(GRID):
                turned = pltpu.roll(base, SPAN * yi, 1) if yi else base
                for t in range(3):
                    self.sums[t, 1 + GRID * yi : 1 + GRID * (yi + 1), :] = turned[:GRID, 128 * t : 128 * t + 128]
            spread = jnp.concatenate([self.sums[0], self.sums[1], self.sums[2]], axis=1)
            grid = mm(spread.astype(BF16), self.select_forward[...])
            row = lax.broadcasted_iota(jnp.int32, (ROWS, KEYS), 0)
            column = lax.broadcasted_iota(jnp.int32, (ROWS, KEYS), 1)
            corner = entries[:, 768:]
            grid = jnp.where(row == 0, corner[:, 0:1], grid)
            grid = jnp.where(column == 0, corner[:, 1:2], grid)
            grid = jnp.where((row == 0) & (column == 0), corner[:, 2:3], grid)
            self.bias[layer, index] = jnp.where(column >= SEQ, -1e30, grid).astype(BF16)
            return 0

        lax.fori_loop(lo, hi, head, 0)

    def normed(self, s):
        scaled, _ = centre(self.h[s].astype(F32))
        gain = self.vecs[s, 0:1, :]
        shift = self.vecs[s, 1:2, :]
        self.n[0] = (scaled * gain + shift).astype(BF16)

    def finish(self, s, left, right):
        real = (lax.broadcasted_iota(jnp.int32, (ROWS, 1), 0) < SEQ).astype(F32) * self.valid

        projected = mm(left[...], right)
        branch = self.vecs[s, 2:3, :] * projected
        result = self.h[s].astype(F32) + branch
        self.p[s] = projected.astype(BF16)
        self.small[2 * s : 2 * s + 1, :] = jnp.sum(branch * branch * real, axis=0, keepdims=True)
        self.small[2 * s + 1 : 2 * s + 2, :] = jnp.sum(result * result * real, axis=0, keepdims=True)
        if s < 3:
            self.h[s + 1] = result.astype(BF16)
        else:
            self.block_out[0] = (result[:SEQ] * self.valid).astype(BF16)

    def attend_forward(self, s):
        layer = s // 2
        self.normed(s)

        def project(j, _):
            columns = lanes(j * 1152, 1152)
            weights = self.w[s, :, :, :, columns].reshape(D, 1152)
            self.qkv[layer, :ROWS, columns] = mm(self.n[0], weights).astype(BF16)
            return 0

        lax.fori_loop(0, 2, project, 0)
        self.qkv[layer, ROWS:, :] = jnp.zeros((KEYS - ROWS, 2304), BF16)

        def pair(j):
            q = self.qkv[layer, :ROWS, lanes(j * 128, 128)]
            k = self.qkv[layer, :, lanes(768 + j * 128, 128)]
            v = self.qkv[layer, :, lanes(1536 + j * 128, 128)]
            mixed = jnp.zeros((ROWS, 128), F32)
            for parity in range(2):
                scores = mm_nt(keep_half(q, parity), k) * INV_ROOT + self.bias[layer, 2 * j + parity].astype(F32)
                peak = jnp.max(scores, axis=-1, keepdims=True)
                exps = jnp.exp(scores - peak)
                total = jnp.sum(exps, axis=-1, keepdims=True)
                probs = (exps * (1.0 / total)).astype(BF16)
                self.probs[layer, 2 * j + parity, :ROWS] = probs
                mixed = mixed + mm(probs, keep_half(v, parity))
            self.o[layer, :, lanes(j * 128, 128)] = mixed.astype(BF16)

        def pairs(i, _):
            for j in range(3):
                pair(3 * i + j)
            return 0

        lax.fori_loop(0, 2, pairs, 0)
        self.finish(s, self.o.at[layer], self.w[s, :, :, :, 2304:].reshape(D, D))

    def dense_forward(self, s):
        layer = s // 2
        self.normed(s)

        def up(j, _):
            columns = lanes(j * 1024, 1024)
            u = mm(self.n[0], self.w[s, :, :, :, columns].reshape(D, 1024))
            act, slope = gelu_pair(u)
            self.a[layer, :, columns] = act.astype(BF16)
            self.slope[layer, :, columns] = slope.astype(BF16)
            return 0

        lax.fori_loop(0, 3, up, 0)
        self.finish(s, self.a.at[layer], self.w2[...])

    def enter(self, s):
        g = self.g[...].astype(F32)
        row = 8 + 3 * s
        self.small[row : row + 1, :] = jnp.sum(g * self.p[s].astype(F32), axis=0, keepdims=True)
        dp = (g * self.vecs[s, 2:3, :]).astype(BF16)
        self.dp[...] = dp
        self.normed(s)
        if s % 2 == 0:
            self.n[1] = self.o[s // 2]
            self.du[:, 2304:] = dp

    def leave(self, s):
        width = 2304 if s % 2 == 0 else FF
        dn = mm_nt(self.du[:, :width], self.w[s, :, :, :, :width].reshape(D, width))
        scaled, inv_std = centre(self.h[s].astype(F32))
        row = 8 + 3 * s
        self.small[row + 1 : row + 2, :] = jnp.sum(dn * scaled, axis=0, keepdims=True)
        self.small[row + 2 : row + 3, :] = jnp.sum(dn, axis=0, keepdims=True)
        e = dn * self.vecs[s, 0:1, :]
        mean_e = jnp.mean(e, axis=-1, keepdims=True)
        mean_ex = jnp.mean(e * scaled, axis=-1, keepdims=True)
        g = self.g[...].astype(F32) + inv_std * (e - mean_e - scaled * mean_ex)
        self.g[...] = g.astype(BF16)

    def put(self, k, mine, route, a1, a2, a3, piece):
        if mine:
            pair = self.pair.at[k % 2, route, a1, a2, a3]
            pair[...] = (piece + pair[...].astype(F32)).astype(BF16)
        else:
            self.stage[k % 2, route, a1, a2, a3] = piece.astype(BF16)

    def first_half(self, k, mine):
        half = self.core if mine else 1 - self.core

        def block(i, _):
            if mine:
                self.reduce.swapped(k, i)
            j = half * 2 + i
            left = jnp.where(j >= self.switch, 1, 0)
            grad = mm_tn(self.n[left], self.du[:, lanes(j * 768, 768)])
            for side in range(2):
                for rb in range(16):
                    for route in range(3):
                        top = rb * 48 + route * 16
                        self.put(
                            k, mine, route, rb // 4, rb % 4, 2 * i + side,
                            grad[top : top + 16, 384 * side : 384 * side + 384],
                        )
            if not mine:
                self.reduce.swap(k, i)
            return 0

        lax.fori_loop(0, 2, block, 0)

    def second_half(self, k, mine, layer):
        half = self.core if mine else 1 - self.core

        def block(i, _):
            if mine:
                self.reduce.swapped(k, i)
            grad = mm_tn(self.a[layer, :, lanes(i * 1536, 1536)], self.dp[:, lanes(half * 384, 384)])
            for z_low in range(2):
                z = 2 * i + z_low
                for x in range(4):
                    for y in range(4):
                        top = (z_low * 4 + x) * 192 + y * 24
                        part = jnp.concatenate([grad[top : top + 24], grad[top + 96 : top + 120]], axis=0)
                        self.put(k, mine, 0, x, y, z, part[0:16])
                        self.put(k, mine, 1, y, z, x, part[16:32])
                        self.put(k, mine, 2, z, x, y, part[32:48])
            if not mine:
                self.reduce.swap(k, i)
            return 0

        lax.fori_loop(0, 2, block, 0)

    def down(self, s):
        layer = s // 2

        def block(j, _):
            columns = lanes(j * 1536, 1536)
            rows = pl.ds(pl.multiple_of(j * 1536, 256), 1536)
            da = mm_nt(self.dp[...], self.w2[rows, :])
            self.du[:, columns] = (da * self.slope[layer, :, columns].astype(F32)).astype(BF16)
            return 0

        lax.fori_loop(0, 2, block, 0)

    def back_out(self, s):
        weights = self.w[s, :, :, :, 2304:].reshape(D, D)
        self.dp[...] = mm_nt(self.du[:, 2304:], weights).astype(BF16)

    def pairs(self, s, third):
        layer = s // 2

        def pair(j):
            q = self.qkv[layer, :ROWS, lanes(j * 128, 128)]
            k = self.qkv[layer, :, lanes(768 + j * 128, 128)]
            v = self.qkv[layer, :, lanes(1536 + j * 128, 128)]
            do = self.dp[:, lanes(j * 128, 128)]
            dq = jnp.zeros((ROWS, 128), F32)
            dk = jnp.zeros((KEYS, 128), F32)
            dv = jnp.zeros((KEYS, 128), F32)
            for parity in range(2):
                do_half = keep_half(do, parity)
                probs = self.probs[layer, 2 * j + parity, :ROWS]
                wide = probs.astype(F32)
                d_probs = mm_nt(do_half, v)
                inner = jnp.sum(d_probs * wide, axis=-1, keepdims=True)
                d_scores = (wide * (d_probs - inner)).astype(BF16)
                dv = dv + mm_tn(probs, do_half)
                dq = dq + mm(d_scores, keep_half(k, parity))
                dk = dk + mm_tn(d_scores, keep_half(q, parity))
                self.probs[layer, 2 * j + parity] = mm(self.by_x[...], d_scores).astype(BF16)
            self.du[:, lanes(j * 128, 128)] = (dq * INV_ROOT).astype(BF16)
            self.du[:, lanes(768 + j * 128, 128)] = (dk[:ROWS] * INV_ROOT).astype(BF16)
            self.du[:, lanes(1536 + j * 128, 128)] = dv[:ROWS].astype(BF16)

        def trio(i, _):
            for j in range(3):
                pair(3 * i + j)
            return 0

        lax.fori_loop(third, third + 1, trio, 0)

    def fold_bias(self, s):
        layer = s // 2
        shape = (KEYS, 384)
        token = lax.broadcasted_iota(jnp.int32, shape, 0)
        lane = lax.broadcasted_iota(jnp.int32, shape, 1)
        target = jnp.where(token >= SEQ, -1000, (SPAN + 1) * (GRID - 1) - patch_offsets(token))
        self.sums[...] = jnp.zeros((3, ROWS, 128), F32)

        def two(i, _):
            lefts, rights = [], []
            for odd in range(2):
                x = 2 * i + odd
                rows = pl.ds(pl.multiple_of(16 * x, 16), 16)
                lefts.append(self.probs[layer, :, rows, :].reshape(192, KEYS))
                here = jnp.where(token == 0, 383, target + x)
                rights.append(ones(lane == here))
            more = mm(jnp.concatenate(lefts, axis=1), jnp.concatenate(rights, axis=0))
            for t in range(3):
                self.sums[t, :192] += more[:, 128 * t : 128 * t + 128]
            return 0

        lax.fori_loop(0, GRID // 2, two, 0)
        last = lax.broadcasted_iota(jnp.int32, (HEADS, 384), 1) == 383
        total = jnp.zeros((HEADS, D), F32)
        side = jnp.zeros((HEADS, 1), F32)
        for y in range(GRID + 1):
            rows = jnp.concatenate([self.sums[t, pl.ds(y, HEADS, stride=16), :] for t in range(3)], axis=1)
            plain = jnp.where(last, 0.0, rows)
            if y < GRID:
                side = side + jnp.sum(rows - plain, axis=1, keepdims=True)
                wide = jnp.concatenate([plain, jnp.zeros((HEADS, 384), F32)], axis=1)
                total = total + (pltpu.roll(wide, SPAN * y, 1) if y else wide)
            else:
                top = jnp.sum(plain, axis=1, keepdims=True)
                corner = jnp.sum(rows - plain, axis=1, keepdims=True)
        entry = lax.broadcasted_iota(jnp.int32, (HEADS, D), 1)
        total = jnp.where(entry == 729, top, total)
        total = jnp.where(entry == 730, side, total)
        total = jnp.where(entry == 731, corner, total)
        self.small[24 + layer * HEADS : 24 + (layer + 1) * HEADS, :] = total


MESH = pl.DeviceIdType.MESH
AXES = ("x", "y", "z")
ROUTES = (("x", "y", "z"), ("y", "z", "x"), ("z", "x", "y"))
ORDER = (5, 3, 2, 4, 1, 0)


class Place:
    def __init__(self):
        dp = lax.axis_index("dp")
        self.at = {"z": dp // 8, "x": (dp // 2) % 4, "c": dp % 2, "y": lax.axis_index("section")}

    def go(self, axis, step):
        at = dict(self.at)
        at[axis] = (at[axis] + step) % (2 if axis == "c" else 4)
        return ((at["z"] * 4 + at["x"]) * 2 + at["c"], at["y"])

    def index(self, axis, step=0):
        return (self.at[axis] + step) % 4


def meet(place):
    barrier = pltpu.get_barrier_semaphore()
    count = 0
    for axis in AXES:
        for step in (1, 2, 3):
            pl.semaphore_signal(barrier, inc=1, device_id=place.go(axis, step), device_id_type=MESH)
            count += 1
    pl.semaphore_signal(barrier, inc=1, device_id=place.go("c", 1), device_id_type=MESH)
    pl.semaphore_wait(barrier, count + 1)


class Reduce:
    def __init__(self, place, **refs):
        self.place = place
        self.__dict__.update(refs)
        self.flying = {}

    def send(self, key, src, dst, number, device):
        k = key[1]
        copy = pltpu.make_async_remote_copy(
            src_ref=src, dst_ref=dst, send_sem=self.sems.at[0, k, number], recv_sem=self.sems.at[1, k, number],
            device_id=device, device_id_type=MESH,
        )
        copy.start()
        self.flying[key] = copy

    def sent(self, k, names):
        for name in names:
            for r in range(3):
                self.flying[(name, k, r)].wait_send()

    def part(self, buffer, k, i):
        pair = pl.ds(2 * i, 2)
        if ORDER[k] < 4:
            return [(3 * i, buffer.at[k % 2, :, :, :, pair])]
        return [
            (3 * i, buffer.at[k % 2, 0, :, :, pair]),
            (3 * i + 1, buffer.at[k % 2, 1, :, pair]),
            (3 * i + 2, buffer.at[k % 2, 2, pair]),
        ]

    def across(self, k, i):
        for (number, source), (_, target) in zip(self.part(self.stage, k, i), self.part(self.pair, k, i)):
            yield pltpu.make_async_remote_copy(
                src_ref=source, dst_ref=target, send_sem=self.sems.at[0, k, number],
                recv_sem=self.sems.at[1, k, number], device_id=self.place.go("c", 1), device_id_type=MESH,
            )

    def prepare(self, k):
        if k >= 2:
            self.swap_sent(k - 2)
            pl.semaphore_wait(self.pair_credit, 1)

    def swap(self, k, i):
        for copy in self.across(k, i):
            copy.start()

    def swapped(self, k, i):
        for copy in self.across(k, i):
            copy.wait_recv()

    def swap_sent(self, k):
        for i in range(2):
            for copy in self.across(k, i):
                copy.wait_send()

    def first(self, k):
        place = self.place
        for r, (axis, _, _) in enumerate(ROUTES):
            own, far = self.pair.at[k % 2, r], self.far.at[k % 2, r]
            across, ahead, behind = place.index(axis, 2), place.index(axis, 1), place.index(axis, 3)
            up, down = place.go(axis, 1), place.go(axis, 3)
            base = 6 + 6 * r
            if k >= 2:
                pl.semaphore_wait(self.far_credit.at[r, 0], 1)
                pl.semaphore_wait(self.far_credit.at[r, 1], 1)
            self.send(("fa", k, r), own.at[across, 0:2], far.at[0], base, up)
            self.send(("fb", k, r), own.at[across, 2:4], far.at[1], base + 1, down)
            self.send(("db", k, r), own.at[ahead, 2:4], far.at[2], base + 2, up)
            self.send(("da", k, r), own.at[behind, 0:2], far.at[3], base + 3, down)

    def merge(self, k):
        place = self.place
        for r, (axis, _, _) in enumerate(ROUTES):
            own, far = self.pair.at[k % 2, r], self.far.at[k % 2, r]
            ahead, behind = place.index(axis, 1), place.index(axis, 3)
            base = 6 + 6 * r
            self.flying[("fa", k, r)].wait_recv()
            far[0] = (far[0].astype(F32) + own[ahead, 0:2].astype(F32)).astype(BF16)
            self.send(("ma", k, r), far.at[0], far.at[4], base + 4, place.go(axis, 1))
            self.flying[("fb", k, r)].wait_recv()
            far[1] = (far[1].astype(F32) + own[behind, 2:4].astype(F32)).astype(BF16)
            self.send(("mb", k, r), far.at[1], far.at[5], base + 5, place.go(axis, 3))

    def second(self, k):
        place = self.place
        for r, (axis, nxt, _) in enumerate(ROUTES):
            for name in ("db", "da", "ma", "mb"):
                self.flying[(name, k, r)].wait_recv()
            own, far = self.pair.at[k % 2, r], self.far.at[k % 2, r]
            me = place.index(axis)
            low = own[me, 0:2].astype(F32) + far[4].astype(F32) + far[3].astype(F32)
            high = own[me, 2:4].astype(F32) + far[2].astype(F32) + far[5].astype(F32)
            line, line_in = self.line.at[k % 2, r], self.line_in.at[k, r]
            line[0:2] = low.astype(BF16)
            line[2:4] = high.astype(BF16)
            for step in (1, 2, 3):
                self.send(
                    (("s", step), k, r), line.at[place.index(nxt, step)], line_in.at[step - 1],
                    24 + 3 * r + step - 1, place.go(nxt, step),
                )
        self.sent(k, ("fa", "fb", "db", "da", "ma", "mb"))
        if k + 2 < 6:
            pl.semaphore_signal(self.pair_credit, inc=1, device_id=place.go("c", 1), device_id_type=MESH)
            for r, (axis, _, _) in enumerate(ROUTES):
                pl.semaphore_signal(self.far_credit.at[r, 0], inc=1, device_id=place.go(axis, 1), device_id_type=MESH)
                pl.semaphore_signal(self.far_credit.at[r, 1], inc=1, device_id=place.go(axis, 3), device_id_type=MESH)

    def third(self, k):
        place = self.place
        for r, (_, axis, nxt) in enumerate(ROUTES):
            line, line_in, spot, spot_in = self.line.at[k % 2, r], self.line_in.at[k, r], self.spot.at[k % 2, r], self.spot_in.at[k, r]
            total = line[place.index(axis)].astype(F32)
            for step in (1, 2, 3):
                self.flying[(("s", step), k, r)].wait_recv()
                total = total + line_in[step - 1].astype(F32)
            spot[...] = total.astype(BF16)
            for step in (1, 2, 3):
                self.send(
                    (("t", step), k, r), spot.at[place.index(nxt, step)], spot_in.at[step - 1],
                    33 + 3 * r + step - 1, place.go(nxt, step),
                )
        self.sent(k, (("s", 1), ("s", 2), ("s", 3)))

    def close(self, k):
        place, tensor = self.place, ORDER[k]
        for r, (_, _, axis) in enumerate(ROUTES):
            spot, spot_in = self.spot.at[k % 2, r], self.spot_in.at[k, r]
            total = spot[place.index(axis)].astype(F32)
            for step in (1, 2, 3):
                self.flying[(("t", step), k, r)].wait_recv()
                total = total + spot_in[step - 1].astype(F32)
            if tensor < 4:
                self.first_out[tensor, 0, 0, r] = total.astype(BF16)
            else:
                rows = self.rows.at[tensor - 4]
                if r == 0:
                    rows[0, 0:16] = total
                elif r == 1:
                    rows[0, 16:24] = total[0:8]
                    rows[1, 0:8] = total[8:16]
                else:
                    rows[1, 8:24] = total
        self.sent(k, (("t", 1), ("t", 2), ("t", 3)))
        if tensor >= 4:
            layer, me = tensor - 4, place.at["c"]
            self.send(("r", k, 0), self.rows.at[layer, 1 - me], self.rows_in.at[layer], 42, place.go("c", 1))

    def finish(self):
        me = self.place.at["c"]
        for k, tensor in enumerate(ORDER):
            if tensor >= 4:
                self.flying[("r", k, 0)].wait()
                layer = tensor - 4
                self.second_out[layer, :, lanes(me * 384, 384)] = self.rows[layer, me]
                self.second_out[layer, :, lanes((1 - me) * 384, 384)] = self.rows_in[layer]
        for k in (4, 5):
            self.swap_sent(k)


class Totals:
    def __init__(self, place, part, bufs, sems):
        self.place, self.part, self.bufs, self.sems = place, part, bufs, sems
        self.copies = []

    def send(self, src, dst, number, device):
        copy = pltpu.make_async_remote_copy(
            src_ref=src, dst_ref=dst, send_sem=self.sems.at[0, number], recv_sem=self.sems.at[1, number],
            device_id=device, device_id_type=MESH,
        )
        copy.start()
        self.copies.append(copy)
        return copy

    @staticmethod
    def half(core):
        return pl.ds(pl.multiple_of(core * 24, 8), 24)

    def start(self, small):
        me = self.place.at["c"]
        self.small = small
        self.now = [self.send(small.at[self.half(1 - me)], self.bufs.at[12], 0, self.place.go("c", 1))]

    def step(self, number):
        place, me = self.place, self.place.at["c"]
        for copy in self.now:
            copy.wait_recv()
        if number == 0:
            self.part[...] = self.small[self.half(me), :] + self.bufs[12]
        else:
            axis = AXES[number - 1]
            self.bufs[4 * number - 4 + place.at[axis]] = self.part[...]
            self.part[...] = (
                (self.bufs[4 * number - 4] + self.bufs[4 * number - 3])
                + (self.bufs[4 * number - 2] + self.bufs[4 * number - 1])
            )
        if number < 3:
            axis = AXES[number]
            self.now = [
                self.send(self.part, self.bufs.at[4 * number + place.at[axis]], 1 + 3 * number + step - 1, place.go(axis, step))
                for step in (1, 2, 3)
            ]
            for copy in self.now:
                copy.wait_send()
        else:
            self.now = [self.send(self.part, self.bufs.at[13], 10, place.go("c", 1))]

    def close(self, out):
        me = self.place.at["c"]
        for copy in self.now:
            copy.wait_recv()
        out[self.half(me), :] = self.part[...]
        out[self.half(1 - me), :] = self.bufs[13]
        self.copies[0].wait_send()
        self.copies[-1].wait_send()


class Spread:
    def __init__(self, place, sems):
        self.place, self.sems = place, sems
        self.sent = []

    def make(self, number, src, dst, device):
        return pltpu.make_async_remote_copy(
            src_ref=src, dst_ref=dst, send_sem=self.sems.at[0, number], recv_sem=self.sems.at[1, number],
            device_id=device, device_id_type=MESH,
        )

    def send(self, number, src, dst, device):
        copy = self.make(number, src, dst, device)
        copy.start()
        self.sent.append(copy)

    def wait(self, number, ref):
        pltpu.make_async_remote_copy(
            src_ref=ref, dst_ref=ref, send_sem=self.sems.at[0, number], recv_sem=self.sems.at[1, number],
            device_id=self.place.go("c", 1), device_id_type=MESH,
        ).wait_recv()

    def drain(self):
        for copy in self.sent:
            copy.wait_send()


GATHER_MESSAGES = 99


class Gather(Spread):
    def __init__(self, place, full, sems):
        super().__init__(place, sems)
        self.full = full
        y = place.at["y"]
        self.first = {"x": 3, "z": 1}
        self.second = {"x": jnp.where(y == 3, 1, 2), "z": jnp.where(y == 1, 3, 2)}
        self.third = {"x": jnp.where(y == 3, 2, 1), "z": jnp.where(y == 1, 2, 3)}

    def rows(self, route, step, sub=None, core=None):
        core = self.place.at["c"] if core is None else core
        block = (0 if route == "x" else 8) + self.place.index(route, step) * 2 + core
        return (block // 4, block % 4, slice(None) if sub is None else slice(16 * sub, 16 * sub + 16))

    def ref(self, rel, route, step, sub=None):
        return self.full.at[(self.place.index("y", rel),) + self.rows(route, step, sub)]

    @staticmethod
    def along_y(rel, route, sub):
        return 3 * (2 * (rel - 1) + (route == "z")) + sub

    @staticmethod
    def in_plane(rel, route, kind, sub):
        return 18 + 9 * (2 * (rel - 1) + (route == "z")) + 3 * kind + sub

    @staticmethod
    def across(rel, route, step):
        return 72 + 4 * (2 * (rel - 1) + (route == "z")) + step

    def load(self, source, sems):
        at = self.place.at
        mine, rest = [], []
        for half, route in enumerate(("x", "z")):
            for block in range(8):
                number = 8 * half + (at[route] * 2 + at["c"] + block) % 8
                rows = pl.ds(pl.multiple_of(number * 48, 16), 48)
                copy = pltpu.make_async_copy(
                    source.at[rows], self.full.at[at["y"], number // 4, number % 4], sems.at[half, block]
                )
                (rest if block else mine).append(copy)
        for copy in mine + rest:
            copy.start()
        for copy in mine:
            copy.wait()
        return rest

    def own(self, up, down):
        copies = []
        for sub in range(3):
            for route, step in ((up, 1), (down, 3)):
                mine = self.ref(0, route, 0, sub)
                copies.append(self.make(self.along_y(4 - step, route, sub), mine, mine, self.place.go("y", step)))
        self.sent += copies
        return copies

    def arrive(self, rels):
        for sub in range(3):
            for route, rel in rels.items():
                piece = self.ref(rel, route, 0, sub)
                self.wait(self.along_y(rel, route, sub), piece)
                if rels is self.first:
                    self.send(self.along_y(2, route, sub), piece, piece, self.place.go("y", 4 - rel))
                for kind, step in ((0, 1), (1, 3)):
                    self.send(self.in_plane(rel, route, kind, sub), piece, piece, self.place.go(route, step))
        for route, rel in rels.items():
            piece = self.ref(rel, route, 0)
            self.send(self.across(rel, route, 0), piece, piece, self.place.go("c", 1))

    def turn(self, rels):
        place = self.place
        clockwise = 1 - 2 * place.at["c"]
        for sub, way in ((0, 1), (1, clockwise), (2, -1)):
            for route, rel in rels.items():
                for kind, step in ((0, 3), (1, 1)):
                    self.wait(self.in_plane(rel, route, kind, sub), self.ref(rel, route, step, sub))
                piece = self.ref(rel, route, 4 - way, sub)
                self.send(self.in_plane(rel, route, 2, sub), piece, piece, place.go(route, 4 + way))
        for route, rel in rels.items():
            for step in (3, 1):
                piece = self.ref(rel, route, step)
                self.send(self.across(rel, route, step), piece, piece, place.go("c", 1))

    def end(self, rels):
        for route, rel in rels.items():
            for sub in range(3):
                self.wait(self.in_plane(rel, route, 2, sub), self.ref(rel, route, 2, sub))
            piece = self.ref(rel, route, 2)
            self.send(self.across(rel, route, 2), piece, piece, self.place.go("c", 1))

    def settle(self, section):
        rel = (section - self.place.at["y"] + 4) % 4
        other = 1 - self.place.at["c"]

        def run():
            for route in ("x", "z"):
                for step in range(4):
                    self.wait(self.across(rel, route, step), self.full.at[(section,) + self.rows(route, step, core=other)])

        pl.when(rel > 0)(run)


def layers_kernel(
    tokens, masked, cotangent, live, mask_token, norm_gain, norm_shift, layer_scale, w_own, w2_hbm,
    tables,
    block_out, tokens_grad, first_grad, second_out, totals,
    w, w2, h, qkv, probs, o, a, slope, p, n, bias, table, select_f, by_x, fold_sums, du, dp, g, vec, vecs, small,
    stage, pair, far, line, line_in, spot, spot_in, rows, rows_in, part, bufs, first_out,
    load_sems, w2_sems, gather_sems, sems, small_sems, share_sems, share_out_sems, pair_credit, far_credit,
):
    place = Place()
    vec[0:1] = norm_gain[...]
    vec[1:2] = norm_shift[...]
    vec[2:3] = layer_scale[...]
    vec[3:8] = jnp.zeros((5, D), F32)
    meet(place)
    y = place.at["y"]
    gather = Gather(place, w, gather_sems)
    own_rest = gather.load(w_own.at[0], load_sems)
    for copy in gather.own("x", "z"):
        copy.start()
    own_later = gather.own("z", "x")

    @pl.when(y == 0)
    def _():
        for copy in own_later:
            copy.start()

    def load_second(layer):
        copies = []
        for block in range(8):
            rows = pl.ds(block * 384, 384)
            copies.append(pltpu.make_async_copy(w2_hbm.at[layer, rows], w2.at[rows], w2_sems.at[block]))
            copies[-1].start()
        return copies

    def loaded(copies):
        for copy in copies:
            copy.wait()

    w2_load = load_second(0)
    vecs[y] = vec[...]
    for step in (1, 2, 3):
        gather.send(95 + step, vec, vecs.at[y], place.go("y", step))
    valid = jnp.where(y < live[lax.axis_index("dp")], 1.0, 0.0)
    body = Body(
        valid=valid, core=place.at["c"], vecs=vecs, table=table,
        select_forward=select_f, by_x=by_x, block_out=block_out, small=small,
        w=w, w2=w2, h=h, qkv=qkv, probs=probs, o=o, a=a, slope=slope, p=p, n=n, bias=bias,
        sums=fold_sums, du=du, dp=dp, g=g, stage=stage, pair=pair,
    )
    reduce = Reduce(
        place, stage=stage, pair=pair, far=far, line=line, line_in=line_in, spot=spot, spot_in=spot_in,
        rows=rows, rows_in=rows_in, first_out=first_out, second_out=second_out, sems=sems,
        pair_credit=pair_credit, far_credit=far_credit,
    )
    body.reduce = reduce
    sums = Totals(place, part, bufs, small_sems)

    gather.arrive(gather.first)

    @pl.when(y != 0)
    def _():
        for copy in own_later:
            copy.start()

    fold_sums[...] = jnp.zeros_like(fold_sums)
    square = (ROWS, KEYS)
    diagonal = lax.broadcasted_iota(jnp.int32, square, 0) == lax.broadcasted_iota(jnp.int32, square, 1)
    flags = jnp.concatenate([masked[...].astype(F32), jnp.zeros((1, KEYS - SEQ), F32)], axis=1)
    here = jnp.sum(jnp.where(diagonal, flags, 0.0), axis=1, keepdims=True)
    h[0, 192:] = jnp.zeros((16, D), BF16)
    start = tokens[0].astype(F32)
    h[0, :SEQ] = (start + here[:SEQ] * (mask_token[...].astype(F32).reshape(1, D) - start)).astype(BF16)
    g[192:] = jnp.zeros((16, D), BF16)
    g[:SEQ] = (cotangent[0].astype(F32) * valid).astype(BF16)
    body.make_selectors()
    body.read_tables(tables)
    body.expand_bias(0, 0, 6)
    gather.arrive(gather.second)
    body.expand_bias(0, 6, 12)
    gather.turn(gather.first)
    body.expand_bias(1, 0, 6)
    gather.arrive(gather.third)
    gather.turn(gather.second)
    body.expand_bias(1, 6, 12)
    gather.end(gather.first)
    gather.end(gather.second)
    for step in (1, 2, 3):
        gather.wait(95 + step, vecs.at[place.index("y", 4 - step)])
    loaded(own_rest)
    gather.turn(gather.third)
    gather.settle(0)
    body.attend_forward(0)
    gather.end(gather.third)
    gather.settle(1)
    loaded(w2_load)
    body.dense_forward(1)
    w2_load = load_second(1)
    gather.settle(2)
    body.attend_forward(2)
    gather.settle(3)
    loaded(w2_load)
    body.dense_forward(3)
    gather.drain()

    body.switch = 4
    body.enter(3)
    body.second_half(0, False, 1)
    body.down(3)
    w2_load = load_second(0)
    body.second_half(0, True, 1)
    reduce.first(0)
    body.first_half(1, False)
    body.leave(3)
    reduce.merge(0)
    body.first_half(1, True)
    reduce.first(1)
    body.switch = 3
    body.enter(2)
    body.back_out(2)
    body.pairs(2, 0)
    reduce.second(0)
    body.pairs(2, 1)
    reduce.merge(1)
    body.fold_bias(2)
    reduce.third(0)
    reduce.prepare(2)
    body.first_half(2, False)
    body.leave(2)
    reduce.second(1)
    body.first_half(2, True)
    reduce.first(2)
    reduce.close(0)
    body.switch = 4
    body.enter(1)
    reduce.prepare(3)
    body.second_half(3, False, 0)
    reduce.third(1)
    loaded(w2_load)
    body.down(1)
    reduce.merge(2)
    body.second_half(3, True, 0)
    reduce.first(3)
    reduce.second(2)
    reduce.prepare(4)
    body.first_half(4, False)
    reduce.close(1)
    body.leave(1)
    reduce.merge(3)
    body.first_half(4, True)
    reduce.first(4)
    body.switch = 3
    body.enter(0)
    body.back_out(0)
    reduce.third(2)
    body.pairs(0, 0)
    reduce.second(3)
    reduce.merge(4)
    body.pairs(0, 1)
    reduce.close(2)
    reduce.prepare(5)
    body.first_half(5, False)
    reduce.third(3)
    body.fold_bias(0)
    body.leave(0)
    grad = g[...].astype(F32)
    tokens_grad[0] = (grad * (1.0 - here)).astype(BF16)[:SEQ]
    small[20:21, :] = jnp.sum(grad * here, axis=0, keepdims=True)
    small[21:24, :] = jnp.zeros((3, D), F32)
    sums.start(small)
    reduce.second(4)
    body.first_half(5, True)
    reduce.first(5)
    reduce.close(3)
    sums.step(0)
    reduce.third(4)
    reduce.merge(5)
    sums.step(1)
    reduce.close(4)
    reduce.second(5)
    sums.step(2)
    reduce.third(5)
    sums.step(3)
    reduce.close(5)
    sums.close(totals)
    Share(place, first_out, w.at[3], share_sems).run(first_grad, share_out_sems)
    reduce.finish()


def layers(tokens, masked, cotangent, live, mask_token, norm_gain, norm_shift, layer_scale, w_own, w2, tables):
    vm = pl.BlockSpec(memory_space=pltpu.VMEM)
    hbm = pl.BlockSpec(memory_space=pl.ANY)
    sm = pl.BlockSpec(memory_space=pltpu.SMEM)
    V, DMA, REGULAR = pltpu.VMEM, pltpu.SemaphoreType.DMA, pltpu.SemaphoreType.REGULAR
    return pl.pallas_call(
        layers_kernel,
        out_shape=(
            jax.ShapeDtypeStruct((1, SEQ, D), BF16),
            jax.ShapeDtypeStruct((1, SEQ, D), BF16),
            jax.ShapeDtypeStruct((4, 4, 48, FF), BF16),
            jax.ShapeDtypeStruct((2, 24, D), F32),
            jax.ShapeDtypeStruct((48, D), F32),
        ),
        in_specs=[vm, vm, vm, sm, vm, vm, vm, vm, hbm, hbm, vm],
        out_specs=(vm, vm, hbm, vm, vm),
        scratch_shapes=[
            V((4, 4, 4, 48, FF), BF16), V((FF, D), BF16), V((4, ROWS, D), BF16), V((2, KEYS, 2304), BF16),
            V((2, HEADS, 16 * GRID, KEYS), BF16), V((2, ROWS, D), BF16), V((2, ROWS, FF), BF16), V((2, ROWS, FF), BF16),
            V((4, ROWS, D), BF16), V((2, ROWS, D), BF16), V((2, HEADS, ROWS, KEYS), BF16), V((2 * HEADS, 896), F32), V((384, KEYS), BF16),
            V((16 * GRID, ROWS), BF16),
            V((3, ROWS, 128), F32), V((ROWS, FF), BF16), V((ROWS, D), BF16), V((ROWS, D), BF16),
            V((8, D), F32), V((4, 8, D), F32), V((48, D), F32),
            V((2,) + HALF, BF16), V((2,) + HALF, BF16), V((2, 3, 6, 2, 4, 16, 384), BF16),
            V((2, 3, 4, 4, 16, 384), BF16), V((6, 3, 3, 4, 16, 384), BF16),
            V((2, 3, 4, 16, 384), BF16), V((6, 3, 3, 16, 384), BF16),
            V((2, 2, 24, 384), F32), V((2, 24, 384), F32), V((24, D), F32), V((14, 24, D), F32),
            V((4, 1, 1, 3, 16, 384), BF16),
            DMA((2, 8)), DMA((8,)), DMA((2, GATHER_MESSAGES)), DMA((2, 6, 43)), DMA((2, 11)), DMA((2, 75)), DMA((48,)), REGULAR, REGULAR((3, 2)),
        ],
        compiler_params=pltpu.CompilerParams(
            collective_id=1, has_side_effects=True, vmem_limit_bytes=64 * 2**20
        ),
    )(tokens, masked, cotangent, live, mask_token, norm_gain, norm_shift, layer_scale, w_own, w2, tables)


class Share(Spread):
    def __init__(self, place, blocks, full, sems):
        super().__init__(place, sems)
        self.blocks, self.full = blocks, full

    def regions(self, c, x, y, z):
        def columns(third):
            return pl.ds(pl.multiple_of((c * 4 + third[0]) * 384, 128), third[1] * 384)

        for route, (a1, a2, a3) in enumerate(((x, y, z), (y, z, x), (z, x, y))):
            yield route, self.full.at[
                pl.ds(*a1), pl.ds(*a2), slice(16 * route, 16 * route + 16), columns(a3)
            ]

    def pass_on(self, base, regions, device):
        for route, region in regions:
            self.send(base + route, region, region, device)

    def await_all(self, base, regions):
        for route, region in regions:
            self.wait(base + route, region)

    def keep(self, out, c, x, y, z):
        for (route, region), (_, target) in zip(self.regions(c, x, y, z), Share(self.place, None, out, None).regions(c, x, y, z)):
            copy = pltpu.make_async_copy(region, target, self.out_sems.at[len(self.kept)])
            copy.start()
            self.kept.append(copy)

    def run(self, out, out_sems):
        place = self.place
        at = place.at
        self.out_sems, self.kept = out_sems, []
        c, x, y, z = at["c"], (at["x"], 1), (at["y"], 1), (at["z"], 1)
        other = 1 - c
        every = (0, 4)
        halves = ((0, 2), (2, 2))

        def near(axis, step):
            return (place.index(axis, step), 1)

        for route, region in self.regions(c, x, y, z):
            for step in (1, 2, 3):
                source = self.blocks.at[place.index("y", step), :, :, route]
                self.send(3 * (step - 1) + route, source, region, place.go("y", step))
            region[...] = self.blocks[at["y"], :, :, route]
        for step in (1, 2, 3):
            self.await_all(3 * (step - 1), self.regions(c, x, near("y", 4 - step), z))
        for step in (1, 3, 2):
            self.pass_on(9 + 3 * (step - 1), self.regions(c, x, halves[0], z), place.go("x", step))
            self.pass_on(18 + 3 * (step - 1), self.regions(c, x, halves[1], z), place.go("z", step))
        for step in (1, 3, 2):
            self.await_all(9 + 3 * (step - 1), self.regions(c, near("x", 4 - step), halves[0], z))
            self.await_all(18 + 3 * (step - 1), self.regions(c, x, halves[1], near("z", 4 - step)))
        for step in (1, 3):
            self.pass_on(27 + 3 * (step - 1), self.regions(c, every, halves[0], z), place.go("z", step))
            self.pass_on(36 + 3 * (step - 1), self.regions(c, x, halves[1], every), place.go("x", step))
        self.pass_on(45, self.regions(c, every, halves[0], z), place.go("c", 1))
        self.pass_on(48, self.regions(c, x, halves[1], every), place.go("c", 1))
        self.keep(out, c, every, halves[0], z)
        self.keep(out, c, x, halves[1], every)
        for step, part, base in ((1, (0, 1), 30), (3, (1, 1), 69)):
            self.await_all(27 + 3 * (step - 1), self.regions(c, every, halves[0], near("z", 4 - step)))
            self.pass_on(base, self.regions(c, every, part, near("z", 4 - step)), place.go("z", step))
            part = (part[0] + 2, 1)
            self.await_all(36 + 3 * (step - 1), self.regions(c, near("x", 4 - step), halves[1], every))
            self.pass_on(base + (9 if base == 30 else 3), self.regions(c, near("x", 4 - step), part, every), place.go("x", step))
        for step in (1, 3):
            self.pass_on(51 + 3 * (step - 1), self.regions(c, every, halves[0], near("z", 4 - step)), place.go("c", 1))
            self.pass_on(60 + 3 * (step - 1), self.regions(c, near("x", 4 - step), halves[1], every), place.go("c", 1))
            self.keep(out, c, every, halves[0], near("z", 4 - step))
            self.keep(out, c, near("x", 4 - step), halves[1], every)
        self.await_all(45, self.regions(other, every, halves[0], z))
        self.keep(out, other, every, halves[0], z)
        self.await_all(48, self.regions(other, x, halves[1], every))
        self.keep(out, other, x, halves[1], every)
        for step in (1, 3):
            self.await_all(51 + 3 * (step - 1), self.regions(other, every, halves[0], near("z", 4 - step)))
            self.keep(out, other, every, halves[0], near("z", 4 - step))
            self.await_all(60 + 3 * (step - 1), self.regions(other, near("x", 4 - step), halves[1], every))
            self.keep(out, other, near("x", 4 - step), halves[1], every)
        for part, base in ((0, 30), (1, 69)):
            self.await_all(base, self.regions(c, every, (part, 1), near("z", 2)))
            self.await_all(base + (9 if base == 30 else 3), self.regions(c, near("x", 2), (part + 2, 1), every))
        self.pass_on(54, self.regions(c, every, halves[0], near("z", 2)), place.go("c", 1))
        self.pass_on(63, self.regions(c, near("x", 2), halves[1], every), place.go("c", 1))
        self.keep(out, c, every, halves[0], near("z", 2))
        self.keep(out, c, near("x", 2), halves[1], every)
        self.await_all(54, self.regions(other, every, halves[0], near("z", 2)))
        self.keep(out, other, every, halves[0], near("z", 2))
        self.await_all(63, self.regions(other, near("x", 2), halves[1], every))
        self.keep(out, other, near("x", 2), halves[1], every)
        for copy in self.kept:
            copy.wait()
        self.drain()


def finish_kernel(
    first, block_in, tokens_in, second_in, totals, live,
    block_out, tokens_grad, first_grad, second_grad, gain_grad, shift_grad, scale_grad, table_grad, mask_grad, rms_out,
    narrow, wide, load_sems, store_sems,
):
    loads, stores = [], []
    for block in range(16):
        a1, a2 = block // 4, block % 4
        rows = pl.ds(block * 48, 48)
        loads.append(pltpu.make_async_copy(first.at[a1, a2], narrow.at[a1, a2], load_sems.at[block]))
        stores.append(pltpu.make_async_copy(wide.at[rows], first_grad.at[0, rows], store_sems.at[block]))
    for load in loads:
        load.start()
    for block in range(16):
        loads[block].wait()
        wide[block * 48 : block * 48 + 48, :] = narrow[block // 4, block % 4].astype(F32)
        stores[block].start()
    block_out[...] = block_in[...]
    tokens_grad[...] = tokens_in[...]
    second_grad[...] = second_in[...]
    own = 8 + 3 * lax.axis_index("section")
    scale_grad[...] = totals[pl.ds(own, 1), :]
    gain_grad[...] = totals[pl.ds(own + 1, 1), :]
    shift_grad[...] = totals[pl.ds(own + 2, 1), :]
    mask_grad[...] = totals[20, :]
    count = lax.fori_loop(0, live.shape[0], lambda i, total: total + live[i], 0)
    tokens = count.astype(F32) * (SEQ * D)
    rms = jnp.sqrt(jnp.sum(totals[0:8, :], axis=1, keepdims=True) / tokens)
    rms_out[...] = jnp.concatenate(
        [jnp.concatenate([rms[2 * s + k : 2 * s + k + 1] for s in range(4)], axis=1) for k in range(2)], axis=0
    )
    for layer in range(2):
        table_grad[:, layer, :] = totals[24 + layer * HEADS : 24 + (layer + 1) * HEADS, : table_grad.shape[2]]
    for store in stores:
        store.wait()


def finish_all(first, block_out, tokens_grad, second, totals, live, entries):
    vm = pl.BlockSpec(memory_space=pltpu.VMEM)
    hbm = pl.BlockSpec(memory_space=pl.ANY)
    image, pair, vector = (1, SEQ, D), (2, 24, D), (1, D)
    return pl.pallas_call(
        finish_kernel,
        out_shape=(
            jax.ShapeDtypeStruct(image, BF16), jax.ShapeDtypeStruct(image, BF16), jax.ShapeDtypeStruct((1, D, FF), F32),
            jax.ShapeDtypeStruct(pair, F32), jax.ShapeDtypeStruct(vector, F32), jax.ShapeDtypeStruct(vector, F32),
            jax.ShapeDtypeStruct(vector, F32), jax.ShapeDtypeStruct((HEADS, 2, entries), F32),
            jax.ShapeDtypeStruct((D,), F32), jax.ShapeDtypeStruct((2, 4), F32),
        ),
        in_specs=[hbm, vm, vm, vm, vm, pl.BlockSpec(memory_space=pltpu.SMEM)],
        out_specs=(vm, vm, hbm) + (vm,) * 7,
        scratch_shapes=[
            pltpu.VMEM((4, 4, 48, FF), BF16), pltpu.VMEM((D, FF), F32),
            pltpu.SemaphoreType.DMA((16,)), pltpu.SemaphoreType.DMA((16,)),
        ],
        compiler_params=pltpu.CompilerParams(vmem_limit_bytes=62 * 2**20),
    )(first, block_out, tokens_grad, second, totals, live)


def on_device(
    tokens, masked, live_images, mask_token, norm_gain, norm_shift, w_first, w_second, layer_scale, rel_table, cotangent
):
    block_out, tokens_grad, first, second, totals = layers(
        tokens, masked, cotangent, live_images, mask_token, norm_gain, norm_shift, layer_scale, w_first, w_second,
        jnp.transpose(rel_table, (2, 0, 1)),
    )
    *outs, table_grad, mask_grad, rms = finish_all(
        first, block_out, tokens_grad, second, totals, live_images, rel_table.shape[1]
    )
    return (*outs, jnp.transpose(table_grad, (1, 2, 0)), mask_grad, rms.T)


def solution(mesh):
    both = P(("dp", "section"), None, None)
    part = P("section", None)
    return jax.shard_map(
        on_device,
        mesh=mesh,
        in_specs=(both, P(("dp", "section"), None), P(), P(), part, part, P("section", None, None), P(), part, P(), both),
        out_specs=(
            both, both, P("section", None, None), P(None, ("dp", "section"), None), part, part, part, P(), P(), P(),
        ),
        check_vma=False,
    )
```

```python
import functools
import math

import jax
import jax.numpy as jnp
from jax import lax
from jax.experimental import pallas as pl
from jax.experimental.pallas import tpu as pltpu
from jax.sharding import PartitionSpec as P

SEQ, ROWS, KEYS = 197, 208, 256
D, FF, HEADS, GRID = 768, 3072, 12, 14
SPAN = 2 * GRID - 1
EPSILON = 1e-06
INV_ROOT = 0.125
INV_ROOT_TWO_PI = 0.3989422804014327
F32, BF16 = jnp.float32, jnp.bfloat16
HALF = (3, 4, 4, 4, 16, 384)


def mm(a, b):
    return lax.dot_general(a, b, (((1,), (0,)), ((), ())), preferred_element_type=F32)


def mm_nt(a, b):
    return lax.dot_general(a, b, (((1,), (1,)), ((), ())), preferred_element_type=F32)


def mm_tn(a, b):
    return lax.dot_general(a, b, (((0,), (0,)), ((), ())), preferred_element_type=F32)


def lanes(start, size):
    return pl.ds(pl.multiple_of(start, 128), size)


def patch_offsets(token):
    patch = token - 1
    return patch + (SPAN - GRID) * ((patch * 4682) >> 16)


def ones(condition):
    return jnp.where(condition, 1.0, 0.0).astype(BF16)


def centre(h):
    average = jnp.mean(h, axis=-1, keepdims=True)
    centred = h - average
    inv_std = lax.rsqrt(jnp.mean(centred * centred, axis=-1, keepdims=True) + EPSILON)
    return centred * inv_std, inv_std


def gelu_pair(u):
    size = jnp.abs(u)
    t = 1.0 / (1.0 + 0.23164189 * size)
    bell = jnp.exp(-0.5 * u * u)
    poly = t * (
        0.127414796
        + t * (-0.142248368 + t * (0.7107068705 + t * (-0.7265760135 + t * 0.5307027145)))
    )
    tail = poly * bell
    phi = jnp.where(u >= 0.0, 1.0 - tail, tail)
    return u * phi, phi + u * bell * INV_ROOT_TWO_PI


def half_mask(rows, parity):
    lane = lax.broadcasted_iota(jnp.int32, (rows, 128), 1)
    return (lane < 64) if parity == 0 else (lane >= 64)


def keep_half(block, parity):
    return jnp.where(half_mask(block.shape[0], parity), block, jnp.zeros_like(block))


class Body:
    def __init__(self, **refs):
        self.__dict__.update(refs)

    def make_selectors(self):
        row = lax.broadcasted_iota(jnp.int32, (384, KEYS), 0)
        token = lax.broadcasted_iota(jnp.int32, (384, KEYS), 1)
        self.select_forward[...] = ones((row == patch_offsets(token)) & (token > 0) & (token < SEQ))
        row = lax.broadcasted_iota(jnp.int32, (16 * GRID, ROWS), 0)
        token = lax.broadcasted_iota(jnp.int32, (16 * GRID, ROWS), 1)
        patch = token - 1
        y = (patch * 4682) >> 16
        wanted = jnp.where(token == 0, GRID, (patch - GRID * y) * 16 + y)
        self.by_x[...] = ones((row == wanted) & (token < SEQ))

    def read_tables(self, tables):
        shape = (tables.shape[2], 896)
        entry = lax.broadcasted_iota(jnp.int32, shape, 0)
        lane = lax.broadcasted_iota(jnp.int32, shape, 1)
        source = jnp.where(lane < 768, SPAN * SPAN - 1 - lane, lane + (SPAN * SPAN - 768))
        select = ones(entry == source)
        for layer in range(2):
            self.table[layer * HEADS : (layer + 1) * HEADS, :] = mm(tables[:, layer, :].astype(BF16), select)

    def expand_bias(self, layer, lo, hi):
        def head(index, _):
            entries = self.table[pl.ds(layer * HEADS + index, 1), :]
            base = jnp.broadcast_to(entries[:, :768], (16, 768))
            base = pltpu.roll(base, 404, 1, stride=1, stride_axis=0)
            for yi in range(GRID):
                turned = pltpu.roll(base, SPAN * yi, 1) if yi else base
                for t in range(3):
                    self.sums[t, 1 + GRID * yi : 1 + GRID * (yi + 1), :] = turned[:GRID, 128 * t : 128 * t + 128]
            spread = jnp.concatenate([self.sums[0], self.sums[1], self.sums[2]], axis=1)
            grid = mm(spread.astype(BF16), self.select_forward[...])
            row = lax.broadcasted_iota(jnp.int32, (ROWS, KEYS), 0)
            column = lax.broadcasted_iota(jnp.int32, (ROWS, KEYS), 1)
            corner = entries[:, 768:]
            grid = jnp.where(row == 0, corner[:, 0:1], grid)
            grid = jnp.where(column == 0, corner[:, 1:2], grid)
            grid = jnp.where((row == 0) & (column == 0), corner[:, 2:3], grid)
            self.bias[layer, index] = jnp.where(column >= SEQ, -1e30, grid).astype(BF16)
            return 0

        lax.fori_loop(lo, hi, head, 0)

    def normed(self, s):
        scaled, _ = centre(self.h[s].astype(F32))
        gain = self.vecs[s, 0:1, :]
        shift = self.vecs[s, 1:2, :]
        self.n[0] = (scaled * gain + shift).astype(BF16)

    def note(self, row, value):
        self.small[pl.ds(row, 1), :] = value

    def finish(self, s, left, right):
        real = (lax.broadcasted_iota(jnp.int32, (ROWS, 1), 0) < SEQ).astype(F32) * self.valid

        projected = mm(left[...], right)
        branch = self.vecs[s, 2:3, :] * projected
        result = self.h[s].astype(F32) + branch
        self.p[s] = projected.astype(BF16)
        self.note(2 * s, jnp.sum(branch * branch * real, axis=0, keepdims=True))
        self.note(2 * s + 1, jnp.sum(result * result * real, axis=0, keepdims=True))

        @pl.when(s < 3)
        def _():
            self.h[s + 1] = result.astype(BF16)

        @pl.when(s == 3)
        def _():
            self.block_out[0] = (result[:SEQ] * self.valid).astype(BF16)

    def attend_forward(self, layer):
        s = 2 * layer
        self.normed(s)

        def project(j, _):
            columns = lanes(j * 1152, 1152)
            weights = self.w[s, :, :, :, columns].reshape(D, 1152)
            self.qkv[layer, :ROWS, columns] = mm(self.n[0], weights).astype(BF16)
            return 0

        lax.fori_loop(0, 2, project, 0)
        self.qkv[layer, ROWS:, :] = jnp.zeros((KEYS - ROWS, 2304), BF16)

        def pair(j):
            q = self.qkv[layer, :ROWS, lanes(j * 128, 128)]
            k = self.qkv[layer, :, lanes(768 + j * 128, 128)]
            v = self.qkv[layer, :, lanes(1536 + j * 128, 128)]
            mixed = jnp.zeros((ROWS, 128), F32)
            for parity in range(2):
                scores = mm_nt(keep_half(q, parity), k) * INV_ROOT + self.bias[layer, 2 * j + parity].astype(F32)
                peak = jnp.max(scores, axis=-1, keepdims=True)
                exps = jnp.exp(scores - peak)
                total = jnp.sum(exps, axis=-1, keepdims=True)
                probs = (exps * (1.0 / total)).astype(BF16)
                self.probs[layer, 2 * j + parity, :ROWS] = probs
                mixed = mixed + mm(probs, keep_half(v, parity))
            self.o[layer, :, lanes(j * 128, 128)] = mixed.astype(BF16)

        def pairs(i, _):
            for j in range(3):
                pair(3 * i + j)
            return 0

        lax.fori_loop(0, 2, pairs, 0)
        self.finish(s, self.o.at[layer], self.w[s, :, :, :, 2304:].reshape(D, D))

    def dense_forward(self, layer):
        s = 2 * layer + 1
        self.normed(s)

        def up(j, _):
            columns = lanes(j * 1024, 1024)
            u = mm(self.n[0], self.w[s, :, :, :, columns].reshape(D, 1024))
            act, slope = gelu_pair(u)
            self.a[layer, :, columns] = act.astype(BF16)
            self.slope[layer, :, columns] = slope.astype(BF16)
            return 0

        lax.fori_loop(0, 3, up, 0)
        self.finish(s, self.a.at[layer], self.w2[...])

    def enter(self, layer, dense):
        s = 2 * layer + dense
        g = self.g[...].astype(F32)
        row = 8 + 3 * s
        self.note(row, jnp.sum(g * self.p[s].astype(F32), axis=0, keepdims=True))
        dp = (g * self.vecs[s, 2:3, :]).astype(BF16)
        self.dp[...] = dp
        self.normed(s)
        if not dense:
            self.n[1] = self.o[layer]
            self.du[:, 2304:] = dp

    def leave(self, layer, dense):
        s = 2 * layer + dense
        width = FF if dense else 2304
        dn = mm_nt(self.du[:, :width], self.w[s, :, :, :, :width].reshape(D, width))
        scaled, inv_std = centre(self.h[s].astype(F32))
        row = 8 + 3 * s
        self.note(row + 1, jnp.sum(dn * scaled, axis=0, keepdims=True))
        self.note(row + 2, jnp.sum(dn, axis=0, keepdims=True))
        e = dn * self.vecs[s, 0:1, :]
        mean_e = jnp.mean(e, axis=-1, keepdims=True)
        mean_ex = jnp.mean(e * scaled, axis=-1, keepdims=True)
        g = self.g[...].astype(F32) + inv_std * (e - mean_e - scaled * mean_ex)
        self.g[...] = g.astype(BF16)

    def put(self, t, mine, route, a1, a2, a3, piece):
        if mine:
            pair = self.pair.at[t.slot, route, a1, a2, a3]
            pair[...] = (piece + pair[...].astype(F32)).astype(BF16)
        else:
            self.stage[t.slot, route, a1, a2, a3] = piece.astype(BF16)

    def first_half(self, t, mine):
        half = self.core if mine else 1 - self.core

        def block(i, _):
            if mine:
                self.reduce.swapped(t, i)
            j = half * 2 + i
            left = jnp.where(j == 3, 1, 0) if t.which == 2 else 0
            grad = mm_tn(self.n[left], self.du[:, lanes(j * 768, 768)])
            for side in range(2):
                for rb in range(16):
                    for route in range(3):
                        top = rb * 48 + route * 16
                        self.put(
                            t, mine, route, rb // 4, rb % 4, 2 * i + side,
                            grad[top : top + 16, 384 * side : 384 * side + 384],
                        )
            if not mine:
                self.reduce.swap(t, i)
            return 0

        lax.fori_loop(0, 2, block, 0)

    def second_half(self, t, mine):
        half = self.core if mine else 1 - self.core

        def block(i, _):
            if mine:
                self.reduce.swapped(t, i)
            grad = mm_tn(self.a[t.layer, :, lanes(i * 1536, 1536)], self.dp[:, lanes(half * 384, 384)])
            for z_low in range(2):
                z = 2 * i + z_low
                for x in range(4):
                    for y in range(4):
                        top = (z_low * 4 + x) * 192 + y * 24
                        part = jnp.concatenate([grad[top : top + 24], grad[top + 96 : top + 120]], axis=0)
                        self.put(t, mine, 0, x, y, z, part[0:16])
                        self.put(t, mine, 1, y, z, x, part[16:32])
                        self.put(t, mine, 2, z, x, y, part[32:48])
            if not mine:
                self.reduce.swap(t, i)
            return 0

        lax.fori_loop(0, 2, block, 0)

    def down(self, layer):
        def block(j, _):
            columns = lanes(j * 1536, 1536)
            rows = pl.ds(pl.multiple_of(j * 1536, 256), 1536)
            da = mm_nt(self.dp[...], self.w2[rows, :])
            self.du[:, columns] = (da * self.slope[layer, :, columns].astype(F32)).astype(BF16)
            return 0

        lax.fori_loop(0, 2, block, 0)

    def back_out(self, layer):
        weights = self.w[2 * layer, :, :, :, 2304:].reshape(D, D)
        self.dp[...] = mm_nt(self.du[:, 2304:], weights).astype(BF16)

    def pairs(self, layer, third):
        def pair(j):
            q = self.qkv[layer, :ROWS, lanes(j * 128, 128)]
            k = self.qkv[layer, :, lanes(768 + j * 128, 128)]
            v = self.qkv[layer, :, lanes(1536 + j * 128, 128)]
            do = self.dp[:, lanes(j * 128, 128)]
            dq = jnp.zeros((ROWS, 128), F32)
            dk = jnp.zeros((KEYS, 128), F32)
            dv = jnp.zeros((KEYS, 128), F32)
            for parity in range(2):
                do_half = keep_half(do, parity)
                probs = self.probs[layer, 2 * j + parity, :ROWS]
                wide = probs.astype(F32)
                d_probs = mm_nt(do_half, v)
                inner = jnp.sum(d_probs * wide, axis=-1, keepdims=True)
                d_scores = (wide * (d_probs - inner)).astype(BF16)
                dv = dv + mm_tn(probs, do_half)
                dq = dq + mm(d_scores, keep_half(k, parity))
                dk = dk + mm_tn(d_scores, keep_half(q, parity))
                self.probs[layer, 2 * j + parity] = mm(self.by_x[...], d_scores).astype(BF16)
            self.du[:, lanes(j * 128, 128)] = (dq * INV_ROOT).astype(BF16)
            self.du[:, lanes(768 + j * 128, 128)] = (dk[:ROWS] * INV_ROOT).astype(BF16)
            self.du[:, lanes(1536 + j * 128, 128)] = dv[:ROWS].astype(BF16)

        def trio(i, _):
            for j in range(3):
                pair(3 * i + j)
            return 0

        lax.fori_loop(third, third + 1, trio, 0)

    def fold_bias(self, layer):
        shape = (KEYS, 384)
        token = lax.broadcasted_iota(jnp.int32, shape, 0)
        lane = lax.broadcasted_iota(jnp.int32, shape, 1)
        target = jnp.where(token >= SEQ, -1000, (SPAN + 1) * (GRID - 1) - patch_offsets(token))
        self.sums[...] = jnp.zeros((3, ROWS, 128), F32)

        def two(i, _):
            lefts, rights = [], []
            for odd in range(2):
                x = 2 * i + odd
                rows = pl.ds(pl.multiple_of(16 * x, 16), 16)
                lefts.append(self.probs[layer, :, rows, :].reshape(192, KEYS))
                here = jnp.where(token == 0, 383, target + x)
                rights.append(ones(lane == here))
            more = mm(jnp.concatenate(lefts, axis=1), jnp.concatenate(rights, axis=0))
            for t in range(3):
                self.sums[t, :192] += more[:, 128 * t : 128 * t + 128]
            return 0

        lax.fori_loop(0, GRID // 2, two, 0)
        last = lax.broadcasted_iota(jnp.int32, (HEADS, 384), 1) == 383
        total = jnp.zeros((HEADS, D), F32)
        side = jnp.zeros((HEADS, 1), F32)
        for y in range(GRID + 1):
            rows = jnp.concatenate([self.sums[t, pl.ds(y, HEADS, stride=16), :] for t in range(3)], axis=1)
            plain = jnp.where(last, 0.0, rows)
            if y < GRID:
                side = side + jnp.sum(rows - plain, axis=1, keepdims=True)
                wide = jnp.concatenate([plain, jnp.zeros((HEADS, 384), F32)], axis=1)
                total = total + (pltpu.roll(wide, SPAN * y, 1) if y else wide)
            else:
                top = jnp.sum(plain, axis=1, keepdims=True)
                corner = jnp.sum(rows - plain, axis=1, keepdims=True)
        entry = lax.broadcasted_iota(jnp.int32, (HEADS, D), 1)
        total = jnp.where(entry == 729, top, total)
        total = jnp.where(entry == 730, side, total)
        total = jnp.where(entry == 731, corner, total)
        for head in range(HEADS):
            self.note(24 + layer * HEADS + head, total[head : head + 1])


MESH = pl.DeviceIdType.MESH
AXES = ("x", "y", "z")
ROUTES = (("x", "y", "z"), ("y", "z", "x"), ("z", "x", "y"))


class Place:
    def __init__(self):
        dp = lax.axis_index("dp")
        self.at = {"z": dp // 8, "x": (dp // 2) % 4, "c": dp % 2, "y": lax.axis_index("section")}

    def go(self, axis, step):
        at = dict(self.at)
        at[axis] = (at[axis] + step) % (2 if axis == "c" else 4)
        return ((at["z"] * 4 + at["x"]) * 2 + at["c"], at["y"])

    def index(self, axis, step=0):
        return (self.at[axis] + step) % 4


def meet(place):
    barrier = pltpu.get_barrier_semaphore()
    count = 0
    for axis in AXES:
        for step in (1, 2, 3):
            pl.semaphore_signal(barrier, inc=1, device_id=place.go(axis, step), device_id_type=MESH)
            count += 1
    pl.semaphore_signal(barrier, inc=1, device_id=place.go("c", 1), device_id_type=MESH)
    pl.semaphore_wait(barrier, count + 1)


class Tensor:
    def __init__(self, turn, which):
        self.number, self.slot = 3 * turn + which, (turn + which) % 2
        self.layer, self.which = 1 - turn, which
        self.second = which == 0
        self.section = 2 * self.layer + (which == 1)


class Reduce:
    def __init__(self, place, **refs):
        self.place = place
        self.__dict__.update(refs)

    def link(self, t, number, src, dst, device):
        return pltpu.make_async_remote_copy(
            src_ref=src, dst_ref=dst, send_sem=self.sems.at[0, t.number, number],
            recv_sem=self.sems.at[1, t.number, number], device_id=device, device_id_type=MESH,
        )

    def ring(self, name, t, r):
        place, axis = self.place, ROUTES[r][0]
        own, far = self.pair.at[t.slot, r], self.far.at[t.slot, r]
        across, ahead, behind = place.index(axis, 2), place.index(axis, 1), place.index(axis, 3)
        source, number, step = {
            "fa": lambda: (own.at[across, 0:2], 0, 1),
            "fb": lambda: (own.at[across, 2:4], 1, 3),
            "db": lambda: (own.at[ahead, 2:4], 2, 1),
            "da": lambda: (own.at[behind, 0:2], 3, 3),
            "ma": lambda: (far.at[0], 4, 1),
            "mb": lambda: (far.at[1], 5, 3),
        }[name]()
        return self.link(t, 6 + 6 * r + number, source, far.at[number], place.go(axis, step))

    def line_copy(self, t, r, step):
        axis = ROUTES[r][1]
        source = self.line.at[t.slot, r, self.place.index(axis, step)]
        return self.link(t, 23 + 3 * r + step, source, self.line_in.at[t.slot, r, step - 1], self.place.go(axis, step))

    def spot_copy(self, t, r, step):
        axis = ROUTES[r][2]
        source = self.spot.at[t.slot, r, self.place.index(axis, step)]
        return self.link(t, 32 + 3 * r + step, source, self.spot_in.at[t.number, r, step - 1], self.place.go(axis, step))

    def rows_copy(self, t):
        source = self.rows.at[t.layer, 1 - self.place.at["c"]]
        return self.link(t, 42, source, self.rows_in.at[t.layer], self.place.go("c", 1))

    def part(self, buffer, t, i):
        pair = pl.ds(2 * i, 2)
        if not t.second:
            return [(3 * i, buffer.at[t.slot, :, :, :, pair])]
        return [
            (3 * i, buffer.at[t.slot, 0, :, :, pair]),
            (3 * i + 1, buffer.at[t.slot, 1, :, pair]),
            (3 * i + 2, buffer.at[t.slot, 2, pair]),
        ]

    def across(self, t, i):
        for (number, source), (_, target) in zip(self.part(self.stage, t, i), self.part(self.pair, t, i)):
            yield self.link(t, number, source, target, self.place.go("c", 1))

    def prepare(self, t, before):
        for i in range(2):
            for copy in self.across(before, i):
                copy.wait_send()
        pl.semaphore_wait(self.pair_credit, 1)

    def swap(self, t, i):
        for copy in self.across(t, i):
            copy.start()

    def swapped(self, t, i):
        for copy in self.across(t, i):
            copy.wait_recv()

    def first(self, t):
        for r in range(3):
            @pl.when(t.number >= 2)
            def _():
                pl.semaphore_wait(self.far_credit.at[r, 0], 1)
                pl.semaphore_wait(self.far_credit.at[r, 1], 1)

            for name in ("fa", "fb", "db", "da"):
                self.ring(name, t, r).start()

    def merge(self, t):
        place = self.place
        for r, (axis, _, _) in enumerate(ROUTES):
            own, far = self.pair.at[t.slot, r], self.far.at[t.slot, r]
            ahead, behind = place.index(axis, 1), place.index(axis, 3)
            self.ring("fa", t, r).wait_recv()
            far[0] = (far[0].astype(F32) + own[ahead, 0:2].astype(F32)).astype(BF16)
            self.ring("ma", t, r).start()
            self.ring("fb", t, r).wait_recv()
            far[1] = (far[1].astype(F32) + own[behind, 2:4].astype(F32)).astype(BF16)
            self.ring("mb", t, r).start()

    def second(self, t):
        place = self.place
        for r in range(3):
            for name in ("db", "da", "ma", "mb"):
                self.ring(name, t, r).wait_recv()
        for r, (axis, nxt, _) in enumerate(ROUTES):
            own, far = self.pair.at[t.slot, r], self.far.at[t.slot, r]
            me = place.index(axis)
            low = own[me, 0:2].astype(F32) + far[4].astype(F32) + far[3].astype(F32)
            high = own[me, 2:4].astype(F32) + far[2].astype(F32) + far[5].astype(F32)
            line = self.line.at[t.slot, r]
            line[0:2] = low.astype(BF16)
            line[2:4] = high.astype(BF16)
            for step in (1, 2, 3):
                self.line_copy(t, r, step).start()
        for r in range(3):
            for name in ("fa", "fb", "db", "da", "ma", "mb"):
                self.ring(name, t, r).wait_send()

        @pl.when(t.number + 2 < 6)
        def _():
            pl.semaphore_signal(self.pair_credit, inc=1, device_id=place.go("c", 1), device_id_type=MESH)
            for r, (axis, _, _) in enumerate(ROUTES):
                pl.semaphore_signal(self.far_credit.at[r, 0], inc=1, device_id=place.go(axis, 1), device_id_type=MESH)
                pl.semaphore_signal(self.far_credit.at[r, 1], inc=1, device_id=place.go(axis, 3), device_id_type=MESH)

    def third(self, t):
        for r, (_, axis, _) in enumerate(ROUTES):
            total = self.line[t.slot, r, self.place.index(axis)].astype(F32)
            for step in (1, 2, 3):
                self.line_copy(t, r, step).wait_recv()
                total = total + self.line_in[t.slot, r, step - 1].astype(F32)
            self.spot[t.slot, r] = total.astype(BF16)
            for step in (1, 2, 3):
                self.spot_copy(t, r, step).start()
        for r in range(3):
            for step in (1, 2, 3):
                self.line_copy(t, r, step).wait_send()

    def close(self, t):
        for r, (_, _, axis) in enumerate(ROUTES):
            total = self.spot[t.slot, r, self.place.index(axis)].astype(F32)
            for step in (1, 2, 3):
                self.spot_copy(t, r, step).wait_recv()
                total = total + self.spot_in[t.number, r, step - 1].astype(F32)
            if not t.second:
                self.first_out[t.section, 0, 0, r] = total.astype(BF16)
            elif r == 0:
                self.rows[t.layer, 0, 0:16] = total
            elif r == 1:
                self.rows[t.layer, 0, 16:24] = total[0:8]
                self.rows[t.layer, 1, 0:8] = total[8:16]
            else:
                self.rows[t.layer, 1, 8:24] = total
        for r in range(3):
            for step in (1, 2, 3):
                self.spot_copy(t, r, step).wait_send()
        if t.second:
            self.rows_copy(t).start()

    def finish(self):
        me = self.place.at["c"]
        for turn in range(2):
            t = Tensor(turn, 0)
            self.rows_copy(t).wait()
            self.second_out[t.layer, :, lanes(me * 384, 384)] = self.rows[t.layer, me]
            self.second_out[t.layer, :, lanes((1 - me) * 384, 384)] = self.rows_in[t.layer]
        for which in (1, 2):
            for i in range(2):
                for copy in self.across(Tensor(1, which), i):
                    copy.wait_send()


class Totals:
    def __init__(self, place, part, bufs, sems):
        self.place, self.part, self.bufs, self.sems = place, part, bufs, sems
        self.copies = []

    def send(self, src, dst, number, device):
        copy = pltpu.make_async_remote_copy(
            src_ref=src, dst_ref=dst, send_sem=self.sems.at[0, number], recv_sem=self.sems.at[1, number],
            device_id=device, device_id_type=MESH,
        )
        copy.start()
        self.copies.append(copy)
        return copy

    @staticmethod
    def half(core):
        return pl.ds(pl.multiple_of(core * 24, 8), 24)

    def start(self, small):
        me = self.place.at["c"]
        self.small = small
        self.now = [self.send(small.at[self.half(1 - me)], self.bufs.at[12], 0, self.place.go("c", 1))]

    def step(self, number):
        place, me = self.place, self.place.at["c"]
        for copy in self.now:
            copy.wait_recv()
        if number == 0:
            self.part[...] = self.small[self.half(me), :] + self.bufs[12]
        else:
            axis = AXES[number - 1]
            self.bufs[4 * number - 4 + place.at[axis]] = self.part[...]
            self.part[...] = (
                (self.bufs[4 * number - 4] + self.bufs[4 * number - 3])
                + (self.bufs[4 * number - 2] + self.bufs[4 * number - 1])
            )
        if number < 3:
            axis = AXES[number]
            self.now = [
                self.send(self.part, self.bufs.at[4 * number + place.at[axis]], 1 + 3 * number + step - 1, place.go(axis, step))
                for step in (1, 2, 3)
            ]
            for copy in self.now:
                copy.wait_send()
        else:
            self.now = [self.send(self.part, self.bufs.at[13], 10, place.go("c", 1))]

    def close(self, out):
        me = self.place.at["c"]
        for copy in self.now:
            copy.wait_recv()
        out[self.half(me), :] = self.part[...]
        out[self.half(1 - me), :] = self.bufs[13]
        self.copies[0].wait_send()
        self.copies[-1].wait_send()


class Spread:
    def __init__(self, place, sems):
        self.place, self.sems = place, sems
        self.sent = []

    def make(self, number, src, dst, device):
        return pltpu.make_async_remote_copy(
            src_ref=src, dst_ref=dst, send_sem=self.sems.at[0, number], recv_sem=self.sems.at[1, number],
            device_id=device, device_id_type=MESH,
        )

    def send(self, number, src, dst, device):
        copy = self.make(number, src, dst, device)
        copy.start()
        self.sent.append(copy)

    def wait(self, number, ref):
        pltpu.make_async_remote_copy(
            src_ref=ref, dst_ref=ref, send_sem=self.sems.at[0, number], recv_sem=self.sems.at[1, number],
            device_id=self.place.go("c", 1), device_id_type=MESH,
        ).wait_recv()

    def drain(self):
        for copy in self.sent:
            copy.wait_send()


GATHER_MESSAGES = 99


class Gather(Spread):
    def __init__(self, place, full, sems):
        super().__init__(place, sems)
        self.full = full
        y = place.at["y"]
        self.first = {"x": 3, "z": 1}
        self.second = {"x": jnp.where(y == 3, 1, 2), "z": jnp.where(y == 1, 3, 2)}
        self.third = {"x": jnp.where(y == 3, 2, 1), "z": jnp.where(y == 1, 2, 3)}

    def rows(self, route, step, sub=None, core=None):
        core = self.place.at["c"] if core is None else core
        block = (0 if route == "x" else 8) + self.place.index(route, step) * 2 + core
        return (block // 4, block % 4, slice(None) if sub is None else slice(16 * sub, 16 * sub + 16))

    def ref(self, rel, route, step, sub=None):
        return self.full.at[(self.place.index("y", rel),) + self.rows(route, step, sub)]

    @staticmethod
    def along_y(rel, route, sub):
        return 3 * (2 * (rel - 1) + (route == "z")) + sub

    @staticmethod
    def in_plane(rel, route, kind, sub):
        return 18 + 9 * (2 * (rel - 1) + (route == "z")) + 3 * kind + sub

    @staticmethod
    def across(rel, route, step):
        return 72 + 4 * (2 * (rel - 1) + (route == "z")) + step

    def load(self, source, sems):
        at = self.place.at
        mine, rest = [], []
        for half, route in enumerate(("x", "z")):
            for block in range(8):
                number = 8 * half + (at[route] * 2 + at["c"] + block) % 8
                rows = pl.ds(pl.multiple_of(number * 48, 16), 48)
                copy = pltpu.make_async_copy(
                    source.at[rows], self.full.at[at["y"], number // 4, number % 4], sems.at[half, block]
                )
                (rest if block else mine).append(copy)
        for copy in mine + rest:
            copy.start()
        for copy in mine:
            copy.wait()
        return rest

    def own(self, up, down):
        copies = []
        for sub in range(3):
            for route, step in ((up, 1), (down, 3)):
                mine = self.ref(0, route, 0, sub)
                copies.append(self.make(self.along_y(4 - step, route, sub), mine, mine, self.place.go("y", step)))
        self.sent += copies
        return copies

    def arrive(self, rels):
        for sub in range(3):
            for route, rel in rels.items():
                piece = self.ref(rel, route, 0, sub)
                self.wait(self.along_y(rel, route, sub), piece)
                if rels is self.first:
                    self.send(self.along_y(2, route, sub), piece, piece, self.place.go("y", 4 - rel))
                for kind, step in ((0, 1), (1, 3)):
                    self.send(self.in_plane(rel, route, kind, sub), piece, piece, self.place.go(route, step))
        for route, rel in rels.items():
            piece = self.ref(rel, route, 0)
            self.send(self.across(rel, route, 0), piece, piece, self.place.go("c", 1))

    def turn(self, rels):
        place = self.place
        clockwise = 1 - 2 * place.at["c"]
        for sub, way in ((0, 1), (1, clockwise), (2, -1)):
            for route, rel in rels.items():
                for kind, step in ((0, 3), (1, 1)):
                    self.wait(self.in_plane(rel, route, kind, sub), self.ref(rel, route, step, sub))
                piece = self.ref(rel, route, 4 - way, sub)
                self.send(self.in_plane(rel, route, 2, sub), piece, piece, place.go(route, 4 + way))
        for route, rel in rels.items():
            for step in (3, 1):
                piece = self.ref(rel, route, step)
                self.send(self.across(rel, route, step), piece, piece, place.go("c", 1))

    def end(self, rels):
        for route, rel in rels.items():
            for sub in range(3):
                self.wait(self.in_plane(rel, route, 2, sub), self.ref(rel, route, 2, sub))
            piece = self.ref(rel, route, 2)
            self.send(self.across(rel, route, 2), piece, piece, self.place.go("c", 1))

    def ending(self, rels):
        waits, copies = [], []
        for route, rel in rels.items():
            for sub in range(3):
                ref = self.ref(rel, route, 2, sub)
                waits.append(self.make(self.in_plane(rel, route, 2, sub), ref, ref, self.place.go("c", 1)))
            piece = self.ref(rel, route, 2)
            copies.append(self.make(self.across(rel, route, 2), piece, piece, self.place.go("c", 1)))
        self.sent += copies
        return waits, copies

    def settle(self, section):
        rel = (section - self.place.at["y"] + 4) % 4
        other = 1 - self.place.at["c"]

        def run():
            for route in ("x", "z"):
                for step in range(4):
                    self.wait(self.across(rel, route, step), self.full.at[(section,) + self.rows(route, step, core=other)])

        pl.when(rel > 0)(run)


def layers_kernel(
    tokens, masked, cotangent, live, mask_token, norm_gain, norm_shift, layer_scale, w_own, w2_hbm,
    tables,
    block_out, tokens_grad, first_grad, second_out, totals,
    w, w2, h, qkv, probs, o, a, slope, p, n, bias, table, select_f, by_x, fold_sums, du, dp, g, vec, vecs, small,
    stage, pair, far, line, line_in, spot, spot_in, rows, rows_in, part, bufs, first_out,
    load_sems, w2_sems, gather_sems, sems, small_sems, share_sems, share_out_sems, pair_credit, far_credit,
):
    place = Place()
    vec[0:1] = norm_gain[...]
    vec[1:2] = norm_shift[...]
    vec[2:3] = layer_scale[...]
    vec[3:8] = jnp.zeros((5, D), F32)
    meet(place)
    y = place.at["y"]
    gather = Gather(place, w, gather_sems)
    own_rest = gather.load(w_own.at[0], load_sems)
    for copy in gather.own("x", "z"):
        copy.start()
    own_later = gather.own("z", "x")

    @pl.when(y == 0)
    def _():
        for copy in own_later:
            copy.start()

    def second_weights(layer):
        copies = []
        for block in range(8):
            rows = pl.ds(block * 384, 384)
            copies.append(pltpu.make_async_copy(w2_hbm.at[layer, rows], w2.at[rows], w2_sems.at[block]))
        return copies

    def load_second(layer):
        for copy in second_weights(layer):
            copy.start()

    def loaded_second(layer):
        for copy in second_weights(layer):
            copy.wait()

    def loaded(copies):
        for copy in copies:
            copy.wait()

    load_second(0)
    vecs[y] = vec[...]
    for step in (1, 2, 3):
        gather.send(95 + step, vec, vecs.at[y], place.go("y", step))
    valid = jnp.where(y < live[lax.axis_index("dp")], 1.0, 0.0)
    body = Body(
        valid=valid, core=place.at["c"], vecs=vecs, table=table,
        select_forward=select_f, by_x=by_x, block_out=block_out, small=small,
        w=w, w2=w2, h=h, qkv=qkv, probs=probs, o=o, a=a, slope=slope, p=p, n=n, bias=bias,
        sums=fold_sums, du=du, dp=dp, g=g, stage=stage, pair=pair,
    )
    reduce = Reduce(
        place, stage=stage, pair=pair, far=far, line=line, line_in=line_in, spot=spot, spot_in=spot_in,
        rows=rows, rows_in=rows_in, first_out=first_out, second_out=second_out, sems=sems,
        pair_credit=pair_credit, far_credit=far_credit,
    )
    body.reduce = reduce
    sums = Totals(place, part, bufs, small_sems)

    gather.arrive(gather.first)

    @pl.when(y != 0)
    def _():
        for copy in own_later:
            copy.start()

    fold_sums[...] = jnp.zeros_like(fold_sums)
    square = (ROWS, KEYS)
    diagonal = lax.broadcasted_iota(jnp.int32, square, 0) == lax.broadcasted_iota(jnp.int32, square, 1)
    flags = jnp.concatenate([masked[...].astype(F32), jnp.zeros((1, KEYS - SEQ), F32)], axis=1)
    here = jnp.sum(jnp.where(diagonal, flags, 0.0), axis=1, keepdims=True)
    h[0, 192:] = jnp.zeros((16, D), BF16)
    start = tokens[0].astype(F32)
    h[0, :SEQ] = (start + here[:SEQ] * (mask_token[...].astype(F32).reshape(1, D) - start)).astype(BF16)
    g[192:] = jnp.zeros((16, D), BF16)
    g[:SEQ] = (cotangent[0].astype(F32) * valid).astype(BF16)
    body.make_selectors()
    body.read_tables(tables)
    body.expand_bias(0, 0, 6)
    gather.arrive(gather.second)
    body.expand_bias(0, 6, 12)
    gather.turn(gather.first)
    body.expand_bias(1, 0, 6)
    gather.arrive(gather.third)
    gather.turn(gather.second)
    body.expand_bias(1, 6, 12)
    gather.end(gather.first)
    gather.end(gather.second)
    for step in (1, 2, 3):
        gather.wait(95 + step, vecs.at[place.index("y", 4 - step)])
    loaded(own_rest)
    gather.turn(gather.third)
    last_waits, last_copies = gather.ending(gather.third)

    def forward_layer(layer, _):
        gather.settle(2 * layer)
        body.attend_forward(layer)

        @pl.when(layer == 0)
        def _():
            for copy in last_waits:
                copy.wait_recv()
            for copy in last_copies:
                copy.start()

        gather.settle(2 * layer + 1)
        loaded_second(layer)
        body.dense_forward(layer)

        @pl.when(layer == 0)
        def _():
            load_second(1)

        return 0

    lax.fori_loop(0, 2, forward_layer, 0)
    gather.drain()

    def backward_layer(turn, _):
        layer = 1 - turn
        again = turn > 0
        second, dense, attention = (Tensor(turn, which) for which in range(3))
        _, dense_before, attention_before = (Tensor(turn - 1, which) for which in range(3))
        body.enter(layer, 1)

        @pl.when(again)
        def _():
            reduce.prepare(second, dense_before)

        body.second_half(second, False)

        @pl.when(again)
        def _():
            reduce.third(dense_before)
            loaded_second(0)

        body.down(layer)

        @pl.when(turn == 0)
        def _():
            load_second(0)

        @pl.when(again)
        def _():
            reduce.merge(attention_before)

        body.second_half(second, True)
        reduce.first(second)

        @pl.when(again)
        def _():
            reduce.second(attention_before)
            reduce.prepare(dense, attention_before)

        body.first_half(dense, False)

        @pl.when(again)
        def _():
            reduce.close(dense_before)

        body.leave(layer, 1)
        reduce.merge(second)
        body.first_half(dense, True)
        reduce.first(dense)
        body.enter(layer, 0)
        body.back_out(layer)

        @pl.when(again)
        def _():
            reduce.third(attention_before)

        body.pairs(layer, 0)
        reduce.second(second)
        reduce.merge(dense)
        body.pairs(layer, 1)

        @pl.when(again)
        def _():
            reduce.close(attention_before)

        reduce.prepare(attention, second)
        body.first_half(attention, False)
        reduce.third(second)
        body.fold_bias(layer)
        body.leave(layer, 0)
        reduce.second(dense)
        body.first_half(attention, True)
        reduce.first(attention)
        reduce.close(second)
        return 0

    lax.fori_loop(0, 2, backward_layer, 0)
    dense, attention = Tensor(1, 1), Tensor(1, 2)
    grad = g[...].astype(F32)
    tokens_grad[0] = (grad * (1.0 - here)).astype(BF16)[:SEQ]
    small[20:21, :] = jnp.sum(grad * here, axis=0, keepdims=True)
    small[21:24, :] = jnp.zeros((3, D), F32)
    sums.start(small)
    reduce.third(dense)
    sums.step(0)
    reduce.merge(attention)
    sums.step(1)
    reduce.close(dense)
    reduce.second(attention)
    sums.step(2)
    reduce.third(attention)
    sums.step(3)
    reduce.close(attention)
    sums.close(totals)
    Share(place, first_out, w.at[3], share_sems).run(first_grad, share_out_sems)
    reduce.finish()


def layers(tokens, masked, cotangent, live, mask_token, norm_gain, norm_shift, layer_scale, w_own, w2, tables):
    vm = pl.BlockSpec(memory_space=pltpu.VMEM)
    hbm = pl.BlockSpec(memory_space=pl.ANY)
    sm = pl.BlockSpec(memory_space=pltpu.SMEM)
    V, DMA, REGULAR = pltpu.VMEM, pltpu.SemaphoreType.DMA, pltpu.SemaphoreType.REGULAR
    return pl.pallas_call(
        layers_kernel,
        out_shape=(
            jax.ShapeDtypeStruct((1, SEQ, D), BF16),
            jax.ShapeDtypeStruct((1, SEQ, D), BF16),
            jax.ShapeDtypeStruct((4, 4, 48, FF), BF16),
            jax.ShapeDtypeStruct((2, 24, D), F32),
            jax.ShapeDtypeStruct((48, D), F32),
        ),
        in_specs=[vm, vm, vm, sm, vm, vm, vm, vm, hbm, hbm, vm],
        out_specs=(vm, vm, hbm, vm, vm),
        scratch_shapes=[
            V((4, 4, 4, 48, FF), BF16), V((FF, D), BF16), V((4, ROWS, D), BF16), V((2, KEYS, 2304), BF16),
            V((2, HEADS, 16 * GRID, KEYS), BF16), V((2, ROWS, D), BF16), V((2, ROWS, FF), BF16), V((2, ROWS, FF), BF16),
            V((4, ROWS, D), BF16), V((2, ROWS, D), BF16), V((2, HEADS, ROWS, KEYS), BF16), V((2 * HEADS, 896), F32), V((384, KEYS), BF16),
            V((16 * GRID, ROWS), BF16),
            V((3, ROWS, 128), F32), V((ROWS, FF), BF16), V((ROWS, D), BF16), V((ROWS, D), BF16),
            V((8, D), F32), V((4, 8, D), F32), V((48, D), F32),
            V((2,) + HALF, BF16), V((2,) + HALF, BF16), V((2, 3, 6, 2, 4, 16, 384), BF16),
            V((2, 3, 4, 4, 16, 384), BF16), V((2, 3, 3, 4, 16, 384), BF16),
            V((2, 3, 4, 16, 384), BF16), V((6, 3, 3, 16, 384), BF16),
            V((2, 2, 24, 384), F32), V((2, 24, 384), F32), V((24, D), F32), V((14, 24, D), F32),
            V((4, 1, 1, 3, 16, 384), BF16),
            DMA((2, 8)), DMA((8,)), DMA((2, GATHER_MESSAGES)), DMA((2, 6, 43)), DMA((2, 11)), DMA((2, 75)), DMA((48,)), REGULAR, REGULAR((3, 2)),
        ],
        compiler_params=pltpu.CompilerParams(
            collective_id=1, has_side_effects=True, vmem_limit_bytes=64 * 2**20
        ),
    )(tokens, masked, cotangent, live, mask_token, norm_gain, norm_shift, layer_scale, w_own, w2, tables)


class Share(Spread):
    def __init__(self, place, blocks, full, sems):
        super().__init__(place, sems)
        self.blocks, self.full = blocks, full

    def regions(self, c, x, y, z):
        def columns(third):
            return pl.ds(pl.multiple_of((c * 4 + third[0]) * 384, 128), third[1] * 384)

        for route, (a1, a2, a3) in enumerate(((x, y, z), (y, z, x), (z, x, y))):
            yield route, self.full.at[
                pl.ds(*a1), pl.ds(*a2), slice(16 * route, 16 * route + 16), columns(a3)
            ]

    def pass_on(self, base, regions, device):
        for route, region in regions:
            self.send(base + route, region, region, device)

    def await_all(self, base, regions):
        for route, region in regions:
            self.wait(base + route, region)

    def keep(self, out, c, x, y, z):
        for (route, region), (_, target) in zip(self.regions(c, x, y, z), Share(self.place, None, out, None).regions(c, x, y, z)):
            copy = pltpu.make_async_copy(region, target, self.out_sems.at[len(self.kept)])
            copy.start()
            self.kept.append(copy)

    def run(self, out, out_sems):
        place = self.place
        at = place.at
        self.out_sems, self.kept = out_sems, []
        c, x, y, z = at["c"], (at["x"], 1), (at["y"], 1), (at["z"], 1)
        other = 1 - c
        every = (0, 4)
        halves = ((0, 2), (2, 2))

        def near(axis, step):
            return (place.index(axis, step), 1)

        for route, region in self.regions(c, x, y, z):
            for step in (1, 2, 3):
                source = self.blocks.at[place.index("y", step), :, :, route]
                self.send(3 * (step - 1) + route, source, region, place.go("y", step))
            region[...] = self.blocks[at["y"], :, :, route]
        for step in (1, 2, 3):
            self.await_all(3 * (step - 1), self.regions(c, x, near("y", 4 - step), z))
        for step in (1, 3, 2):
            self.pass_on(9 + 3 * (step - 1), self.regions(c, x, halves[0], z), place.go("x", step))
            self.pass_on(18 + 3 * (step - 1), self.regions(c, x, halves[1], z), place.go("z", step))
        for step in (1, 3, 2):
            self.await_all(9 + 3 * (step - 1), self.regions(c, near("x", 4 - step), halves[0], z))
            self.await_all(18 + 3 * (step - 1), self.regions(c, x, halves[1], near("z", 4 - step)))
        for step in (1, 3):
            self.pass_on(27 + 3 * (step - 1), self.regions(c, every, halves[0], z), place.go("z", step))
            self.pass_on(36 + 3 * (step - 1), self.regions(c, x, halves[1], every), place.go("x", step))
        self.pass_on(45, self.regions(c, every, halves[0], z), place.go("c", 1))
        self.pass_on(48, self.regions(c, x, halves[1], every), place.go("c", 1))
        self.keep(out, c, every, halves[0], z)
        self.keep(out, c, x, halves[1], every)
        for step, part, base in ((1, (0, 1), 30), (3, (1, 1), 69)):
            self.await_all(27 + 3 * (step - 1), self.regions(c, every, halves[0], near("z", 4 - step)))
            self.pass_on(base, self.regions(c, every, part, near("z", 4 - step)), place.go("z", step))
            part = (part[0] + 2, 1)
            self.await_all(36 + 3 * (step - 1), self.regions(c, near("x", 4 - step), halves[1], every))
            self.pass_on(base + (9 if base == 30 else 3), self.regions(c, near("x", 4 - step), part, every), place.go("x", step))
        for step in (1, 3):
            self.pass_on(51 + 3 * (step - 1), self.regions(c, every, halves[0], near("z", 4 - step)), place.go("c", 1))
            self.pass_on(60 + 3 * (step - 1), self.regions(c, near("x", 4 - step), halves[1], every), place.go("c", 1))
            self.keep(out, c, every, halves[0], near("z", 4 - step))
            self.keep(out, c, near("x", 4 - step), halves[1], every)
        self.await_all(45, self.regions(other, every, halves[0], z))
        self.keep(out, other, every, halves[0], z)
        self.await_all(48, self.regions(other, x, halves[1], every))
        self.keep(out, other, x, halves[1], every)
        for step in (1, 3):
            self.await_all(51 + 3 * (step - 1), self.regions(other, every, halves[0], near("z", 4 - step)))
            self.keep(out, other, every, halves[0], near("z", 4 - step))
            self.await_all(60 + 3 * (step - 1), self.regions(other, near("x", 4 - step), halves[1], every))
            self.keep(out, other, near("x", 4 - step), halves[1], every)
        for part, base in ((0, 30), (1, 69)):
            self.await_all(base, self.regions(c, every, (part, 1), near("z", 2)))
            self.await_all(base + (9 if base == 30 else 3), self.regions(c, near("x", 2), (part + 2, 1), every))
        self.pass_on(54, self.regions(c, every, halves[0], near("z", 2)), place.go("c", 1))
        self.pass_on(63, self.regions(c, near("x", 2), halves[1], every), place.go("c", 1))
        self.keep(out, c, every, halves[0], near("z", 2))
        self.keep(out, c, near("x", 2), halves[1], every)
        self.await_all(54, self.regions(other, every, halves[0], near("z", 2)))
        self.keep(out, other, every, halves[0], near("z", 2))
        self.await_all(63, self.regions(other, near("x", 2), halves[1], every))
        self.keep(out, other, near("x", 2), halves[1], every)
        for copy in self.kept:
            copy.wait()
        self.drain()


def finish_kernel(
    first, block_in, tokens_in, second_in, totals, live,
    block_out, tokens_grad, first_grad, second_grad, gain_grad, shift_grad, scale_grad, table_grad, mask_grad, rms_out,
    narrow, wide, load_sems, store_sems,
):
    loads, stores = [], []
    for block in range(16):
        a1, a2 = block // 4, block % 4
        rows = pl.ds(block * 48, 48)
        loads.append(pltpu.make_async_copy(first.at[a1, a2], narrow.at[a1, a2], load_sems.at[block]))
        stores.append(pltpu.make_async_copy(wide.at[rows], first_grad.at[0, rows], store_sems.at[block]))
    for load in loads:
        load.start()
    for block in range(16):
        loads[block].wait()
        wide[block * 48 : block * 48 + 48, :] = narrow[block // 4, block % 4].astype(F32)
        stores[block].start()
    block_out[...] = block_in[...]
    tokens_grad[...] = tokens_in[...]
    second_grad[...] = second_in[...]
    own = 8 + 3 * lax.axis_index("section")
    scale_grad[...] = totals[pl.ds(own, 1), :]
    gain_grad[...] = totals[pl.ds(own + 1, 1), :]
    shift_grad[...] = totals[pl.ds(own + 2, 1), :]
    mask_grad[...] = totals[20, :]
    count = lax.fori_loop(0, live.shape[0], lambda i, total: total + live[i], 0)
    tokens = count.astype(F32) * (SEQ * D)
    rms = jnp.sqrt(jnp.sum(totals[0:8, :], axis=1, keepdims=True) / tokens)
    rms_out[...] = jnp.concatenate(
        [jnp.concatenate([rms[2 * s + k : 2 * s + k + 1] for s in range(4)], axis=1) for k in range(2)], axis=0
    )
    for layer in range(2):
        table_grad[:, layer, :] = totals[24 + layer * HEADS : 24 + (layer + 1) * HEADS, : table_grad.shape[2]]
    for store in stores:
        store.wait()


def finish_all(first, block_out, tokens_grad, second, totals, live, entries):
    vm = pl.BlockSpec(memory_space=pltpu.VMEM)
    hbm = pl.BlockSpec(memory_space=pl.ANY)
    image, pair, vector = (1, SEQ, D), (2, 24, D), (1, D)
    return pl.pallas_call(
        finish_kernel,
        out_shape=(
            jax.ShapeDtypeStruct(image, BF16), jax.ShapeDtypeStruct(image, BF16), jax.ShapeDtypeStruct((1, D, FF), F32),
            jax.ShapeDtypeStruct(pair, F32), jax.ShapeDtypeStruct(vector, F32), jax.ShapeDtypeStruct(vector, F32),
            jax.ShapeDtypeStruct(vector, F32), jax.ShapeDtypeStruct((HEADS, 2, entries), F32),
            jax.ShapeDtypeStruct((D,), F32), jax.ShapeDtypeStruct((2, 4), F32),
        ),
        in_specs=[hbm, vm, vm, vm, vm, pl.BlockSpec(memory_space=pltpu.SMEM)],
        out_specs=(vm, vm, hbm) + (vm,) * 7,
        scratch_shapes=[
            pltpu.VMEM((4, 4, 48, FF), BF16), pltpu.VMEM((D, FF), F32),
            pltpu.SemaphoreType.DMA((16,)), pltpu.SemaphoreType.DMA((16,)),
        ],
        compiler_params=pltpu.CompilerParams(vmem_limit_bytes=62 * 2**20),
    )(first, block_out, tokens_grad, second, totals, live)


def on_device(
    tokens, masked, live_images, mask_token, norm_gain, norm_shift, w_first, w_second, layer_scale, rel_table, cotangent
):
    block_out, tokens_grad, first, second, totals = layers(
        tokens, masked, cotangent, live_images, mask_token, norm_gain, norm_shift, layer_scale, w_first, w_second,
        jnp.transpose(rel_table, (2, 0, 1)),
    )
    *outs, table_grad, mask_grad, rms = finish_all(
        first, block_out, tokens_grad, second, totals, live_images, rel_table.shape[1]
    )
    return (*outs, jnp.transpose(table_grad, (1, 2, 0)), mask_grad, rms.T)


def solution(mesh):
    both = P(("dp", "section"), None, None)
    part = P("section", None)
    return jax.shard_map(
        on_device,
        mesh=mesh,
        in_specs=(both, P(("dp", "section"), None), P(), P(), part, part, P("section", None, None), P(), part, P(), both),
        out_specs=(
            both, both, P("section", None, None), P(None, ("dp", "section"), None), part, part, part, P(), P(), P(),
        ),
        check_vma=False,
    )
```

```python
import functools
import math

import jax
import jax.numpy as jnp
from jax import lax
from jax.experimental import pallas as pl
from jax.experimental.pallas import tpu as pltpu
from jax.sharding import PartitionSpec as P

SEQ, ROWS, KEYS = 197, 208, 256
D, FF, HEADS, GRID = 768, 3072, 12, 14
SPAN = 2 * GRID - 1
EPSILON = 1e-06
INV_ROOT = 0.125
INV_ROOT_TWO_PI = 0.3989422804014327
F32, BF16 = jnp.float32, jnp.bfloat16
HALF = (3, 4, 4, 4, 16, 384)


def mm(a, b):
    return lax.dot_general(a, b, (((1,), (0,)), ((), ())), preferred_element_type=F32)


def mm_nt(a, b):
    return lax.dot_general(a, b, (((1,), (1,)), ((), ())), preferred_element_type=F32)


def mm_tn(a, b):
    return lax.dot_general(a, b, (((0,), (0,)), ((), ())), preferred_element_type=F32)


def lanes(start, size):
    return pl.ds(pl.multiple_of(start, 128), size)


def patch_offsets(token):
    patch = token - 1
    return patch + (SPAN - GRID) * ((patch * 4682) >> 16)


def ones(condition):
    return jnp.where(condition, 1.0, 0.0).astype(BF16)


def centre(h):
    average = jnp.mean(h, axis=-1, keepdims=True)
    centred = h - average
    inv_std = lax.rsqrt(jnp.mean(centred * centred, axis=-1, keepdims=True) + EPSILON)
    return centred * inv_std, inv_std


def gelu_pair(u):
    size = jnp.abs(u)
    t = 1.0 / (1.0 + 0.23164189 * size)
    bell = jnp.exp(-0.5 * u * u)
    poly = t * (
        0.127414796
        + t * (-0.142248368 + t * (0.7107068705 + t * (-0.7265760135 + t * 0.5307027145)))
    )
    tail = poly * bell
    phi = jnp.where(u >= 0.0, 1.0 - tail, tail)
    return u * phi, phi + u * bell * INV_ROOT_TWO_PI


def half_mask(rows, parity):
    lane = lax.broadcasted_iota(jnp.int32, (rows, 128), 1)
    return (lane < 64) if parity == 0 else (lane >= 64)


def keep_half(block, parity):
    return jnp.where(half_mask(block.shape[0], parity), block, jnp.zeros_like(block))


class Body:
    def __init__(self, **refs):
        self.__dict__.update(refs)

    def make_selectors(self):
        row = lax.broadcasted_iota(jnp.int32, (384, KEYS), 0)
        token = lax.broadcasted_iota(jnp.int32, (384, KEYS), 1)
        self.select_forward[...] = ones((row == patch_offsets(token)) & (token > 0) & (token < SEQ))
        row = lax.broadcasted_iota(jnp.int32, (16 * GRID, ROWS), 0)
        token = lax.broadcasted_iota(jnp.int32, (16 * GRID, ROWS), 1)
        patch = token - 1
        y = (patch * 4682) >> 16
        wanted = jnp.where(token == 0, GRID, (patch - GRID * y) * 16 + y)
        self.by_x[...] = ones((row == wanted) & (token < SEQ))

    def read_tables(self, tables):
        shape = (tables.shape[2], 896)
        entry = lax.broadcasted_iota(jnp.int32, shape, 0)
        lane = lax.broadcasted_iota(jnp.int32, shape, 1)
        source = jnp.where(lane < 768, SPAN * SPAN - 1 - lane, lane + (SPAN * SPAN - 768))
        select = ones(entry == source)
        for layer in range(2):
            self.table[layer * HEADS : (layer + 1) * HEADS, :] = mm(tables[:, layer, :].astype(BF16), select)

    def expand_bias(self, layer, lo, hi):
        def head(index, _):
            entries = self.table[pl.ds(layer * HEADS + index, 1), :]
            base = jnp.broadcast_to(entries[:, :768], (16, 768))
            base = pltpu.roll(base, 404, 1, stride=1, stride_axis=0)
            for yi in range(GRID):
                turned = pltpu.roll(base, SPAN * yi, 1) if yi else base
                for t in range(3):
                    self.sums[t, 1 + GRID * yi : 1 + GRID * (yi + 1), :] = turned[:GRID, 128 * t : 128 * t + 128]
            spread = jnp.concatenate([self.sums[0], self.sums[1], self.sums[2]], axis=1)
            grid = mm(spread.astype(BF16), self.select_forward[...])
            row = lax.broadcasted_iota(jnp.int32, (ROWS, KEYS), 0)
            column = lax.broadcasted_iota(jnp.int32, (ROWS, KEYS), 1)
            corner = entries[:, 768:]
            grid = jnp.where(row == 0, corner[:, 0:1], grid)
            grid = jnp.where(column == 0, corner[:, 1:2], grid)
            grid = jnp.where((row == 0) & (column == 0), corner[:, 2:3], grid)
            self.bias[layer, index] = jnp.where(column >= SEQ, -1e30, grid).astype(BF16)
            return 0

        lax.fori_loop(lo, hi, head, 0)

    def normed(self, s):
        scaled, _ = centre(self.h[s].astype(F32))
        gain = self.vecs[s, 0:1, :]
        shift = self.vecs[s, 1:2, :]
        self.n[0] = (scaled * gain + shift).astype(BF16)

    def note(self, row, value):
        self.small[pl.ds(row, 1), :] = value

    def finish(self, s, left, right):
        real = (lax.broadcasted_iota(jnp.int32, (ROWS, 1), 0) < SEQ).astype(F32) * self.valid

        projected = mm(left[...], right)
        branch = self.vecs[s, 2:3, :] * projected
        result = self.h[s].astype(F32) + branch
        self.p[s] = projected.astype(BF16)
        self.note(2 * s, jnp.sum(branch * branch * real, axis=0, keepdims=True))
        self.note(2 * s + 1, jnp.sum(result * result * real, axis=0, keepdims=True))

        @pl.when(s < 3)
        def _():
            self.h[s + 1] = result.astype(BF16)

        @pl.when(s == 3)
        def _():
            self.block_out[0] = (result[:SEQ] * self.valid).astype(BF16)

    def attend_forward(self, layer):
        s = 2 * layer
        self.normed(s)

        def project(j, _):
            columns = lanes(j * 1152, 1152)
            weights = self.w[s, :, :, :, columns].reshape(D, 1152)
            self.qkv[layer, :ROWS, columns] = mm(self.n[0], weights).astype(BF16)
            return 0

        lax.fori_loop(0, 2, project, 0)
        self.qkv[layer, ROWS:, :] = jnp.zeros((KEYS - ROWS, 2304), BF16)

        def pair(j):
            q = self.qkv[layer, :ROWS, lanes(j * 128, 128)]
            k = self.qkv[layer, :, lanes(768 + j * 128, 128)]
            v = self.qkv[layer, :, lanes(1536 + j * 128, 128)]
            mixed = jnp.zeros((ROWS, 128), F32)
            for parity in range(2):
                scores = mm_nt(keep_half(q, parity), k) * INV_ROOT + self.bias[layer, 2 * j + parity].astype(F32)
                peak = jnp.max(scores, axis=-1, keepdims=True)
                exps = jnp.exp(scores - peak)
                total = jnp.sum(exps, axis=-1, keepdims=True)
                probs = (exps * (1.0 / total)).astype(BF16)
                self.probs[layer, 2 * j + parity, :ROWS] = probs
                mixed = mixed + mm(probs, keep_half(v, parity))
            self.o[layer, :, lanes(j * 128, 128)] = mixed.astype(BF16)

        def pairs(i, _):
            for j in range(3):
                pair(3 * i + j)
            return 0

        lax.fori_loop(0, 2, pairs, 0)
        self.finish(s, self.o.at[layer], self.w[s, :, :, :, 2304:].reshape(D, D))

    def dense_forward(self, layer):
        s = 2 * layer + 1
        self.normed(s)

        def up(j, _):
            columns = lanes(j * 1024, 1024)
            u = mm(self.n[0], self.w[s, :, :, :, columns].reshape(D, 1024))
            act, slope = gelu_pair(u)
            self.a[layer, :, columns] = act.astype(BF16)
            self.slope[layer, :, columns] = slope.astype(BF16)
            return 0

        lax.fori_loop(0, 3, up, 0)
        self.finish(s, self.a.at[layer], self.w2[...])

    def enter(self, layer, dense):
        s = 2 * layer + dense
        g = self.g[...].astype(F32)
        row = 8 + 3 * s
        self.note(row, jnp.sum(g * self.p[s].astype(F32), axis=0, keepdims=True))
        dp = (g * self.vecs[s, 2:3, :]).astype(BF16)
        self.dp[...] = dp
        self.normed(s)
        if not dense:
            self.n[1] = self.o[layer]
            self.du[:, 2304:] = dp

    def leave(self, layer, dense):
        s = 2 * layer + dense
        width = FF if dense else 2304
        dn = mm_nt(self.du[:, :width], self.w[s, :, :, :, :width].reshape(D, width))
        scaled, inv_std = centre(self.h[s].astype(F32))
        row = 8 + 3 * s
        self.note(row + 1, jnp.sum(dn * scaled, axis=0, keepdims=True))
        self.note(row + 2, jnp.sum(dn, axis=0, keepdims=True))
        e = dn * self.vecs[s, 0:1, :]
        mean_e = jnp.mean(e, axis=-1, keepdims=True)
        mean_ex = jnp.mean(e * scaled, axis=-1, keepdims=True)
        g = self.g[...].astype(F32) + inv_std * (e - mean_e - scaled * mean_ex)
        self.g[...] = g.astype(BF16)

    def put(self, t, mine, route, a1, a2, a3, piece):
        if mine:
            pair = self.pair.at[t.slot, route, a1, a2, a3]
            pair[...] = (piece + pair[...].astype(F32)).astype(BF16)
        else:
            self.stage[t.slot, route, a1, a2, a3] = piece.astype(BF16)

    def first_half(self, t, mine):
        half = self.core if mine else 1 - self.core

        def block(i, _):
            if mine:
                self.reduce.swapped(t, i)
            j = half * 2 + i
            left = jnp.where(j == 3, 1, 0) if t.which == 2 else 0
            grad = mm_tn(self.n[left], self.du[:, lanes(j * 768, 768)])
            for side in range(2):
                for rb in range(16):
                    for route in range(3):
                        top = rb * 48 + route * 16
                        self.put(
                            t, mine, route, rb // 4, rb % 4, 2 * i + side,
                            grad[top : top + 16, 384 * side : 384 * side + 384],
                        )
            if not mine:
                self.reduce.swap(t, i)
            return 0

        lax.fori_loop(0, 2, block, 0)

    def second_half(self, t, mine):
        half = self.core if mine else 1 - self.core

        def block(i, _):
            if mine:
                self.reduce.swapped(t, i)
            grad = mm_tn(self.a[t.layer, :, lanes(i * 1536, 1536)], self.dp[:, lanes(half * 384, 384)])
            for z_low in range(2):
                z = 2 * i + z_low
                for x in range(4):
                    for y in range(4):
                        top = (z_low * 4 + x) * 192 + y * 24
                        part = jnp.concatenate([grad[top : top + 24], grad[top + 96 : top + 120]], axis=0)
                        self.put(t, mine, 0, x, y, z, part[0:16])
                        self.put(t, mine, 1, y, z, x, part[16:32])
                        self.put(t, mine, 2, z, x, y, part[32:48])
            if not mine:
                self.reduce.swap(t, i)
            return 0

        lax.fori_loop(0, 2, block, 0)

    def down(self, layer):
        def block(j, _):
            columns = lanes(j * 1536, 1536)
            rows = pl.ds(pl.multiple_of(j * 1536, 256), 1536)
            da = mm_nt(self.dp[...], self.w2[rows, :])
            self.du[:, columns] = (da * self.slope[layer, :, columns].astype(F32)).astype(BF16)
            return 0

        lax.fori_loop(0, 2, block, 0)

    def back_out(self, layer):
        weights = self.w[2 * layer, :, :, :, 2304:].reshape(D, D)
        self.dp[...] = mm_nt(self.du[:, 2304:], weights).astype(BF16)

    def pairs(self, layer, third):
        def pair(j):
            q = self.qkv[layer, :ROWS, lanes(j * 128, 128)]
            k = self.qkv[layer, :, lanes(768 + j * 128, 128)]
            v = self.qkv[layer, :, lanes(1536 + j * 128, 128)]
            do = self.dp[:, lanes(j * 128, 128)]
            dq = jnp.zeros((ROWS, 128), F32)
            dk = jnp.zeros((KEYS, 128), F32)
            dv = jnp.zeros((KEYS, 128), F32)
            for parity in range(2):
                do_half = keep_half(do, parity)
                probs = self.probs[layer, 2 * j + parity, :ROWS]
                wide = probs.astype(F32)
                d_probs = mm_nt(do_half, v)
                inner = jnp.sum(d_probs * wide, axis=-1, keepdims=True)
                d_scores = (wide * (d_probs - inner)).astype(BF16)
                dv = dv + mm_tn(probs, do_half)
                dq = dq + mm(d_scores, keep_half(k, parity))
                dk = dk + mm_tn(d_scores, keep_half(q, parity))
                self.probs[layer, 2 * j + parity] = mm(self.by_x[...], d_scores).astype(BF16)
            self.du[:, lanes(j * 128, 128)] = (dq * INV_ROOT).astype(BF16)
            self.du[:, lanes(768 + j * 128, 128)] = (dk[:ROWS] * INV_ROOT).astype(BF16)
            self.du[:, lanes(1536 + j * 128, 128)] = dv[:ROWS].astype(BF16)

        def trio(i, _):
            for j in range(3):
                pair(3 * i + j)
            return 0

        lax.fori_loop(third, third + 1, trio, 0)

    def fold_bias(self, layer):
        shape = (KEYS, 384)
        token = lax.broadcasted_iota(jnp.int32, shape, 0)
        lane = lax.broadcasted_iota(jnp.int32, shape, 1)
        target = jnp.where(token >= SEQ, -1000, (SPAN + 1) * (GRID - 1) - patch_offsets(token))
        self.sums[...] = jnp.zeros((3, ROWS, 128), F32)

        def two(i, _):
            lefts, rights = [], []
            for odd in range(2):
                x = 2 * i + odd
                rows = pl.ds(pl.multiple_of(16 * x, 16), 16)
                lefts.append(self.probs[layer, :, rows, :].reshape(192, KEYS))
                here = jnp.where(token == 0, 383, target + x)
                rights.append(ones(lane == here))
            more = mm(jnp.concatenate(lefts, axis=1), jnp.concatenate(rights, axis=0))
            for t in range(3):
                self.sums[t, :192] += more[:, 128 * t : 128 * t + 128]
            return 0

        lax.fori_loop(0, GRID // 2, two, 0)
        last = lax.broadcasted_iota(jnp.int32, (HEADS, 384), 1) == 383
        total = jnp.zeros((HEADS, D), F32)
        side = jnp.zeros((HEADS, 1), F32)
        for y in range(GRID + 1):
            rows = jnp.concatenate([self.sums[t, pl.ds(y, HEADS, stride=16), :] for t in range(3)], axis=1)
            plain = jnp.where(last, 0.0, rows)
            if y < GRID:
                side = side + jnp.sum(rows - plain, axis=1, keepdims=True)
                wide = jnp.concatenate([plain, jnp.zeros((HEADS, 384), F32)], axis=1)
                total = total + (pltpu.roll(wide, SPAN * y, 1) if y else wide)
            else:
                top = jnp.sum(plain, axis=1, keepdims=True)
                corner = jnp.sum(rows - plain, axis=1, keepdims=True)
        entry = lax.broadcasted_iota(jnp.int32, (HEADS, D), 1)
        total = jnp.where(entry == 729, top, total)
        total = jnp.where(entry == 730, side, total)
        total = jnp.where(entry == 731, corner, total)
        for head in range(HEADS):
            self.note(24 + layer * HEADS + head, total[head : head + 1])


MESH = pl.DeviceIdType.MESH
AXES = ("x", "y", "z")
ROUTES = (("x", "y", "z"), ("y", "z", "x"), ("z", "x", "y"))


class Place:
    def __init__(self):
        dp = lax.axis_index("dp")
        self.at = {"z": dp // 8, "x": (dp // 2) % 4, "c": dp % 2, "y": lax.axis_index("section")}

    def go(self, axis, step):
        at = dict(self.at)
        at[axis] = (at[axis] + step) % (2 if axis == "c" else 4)
        return ((at["z"] * 4 + at["x"]) * 2 + at["c"], at["y"])

    def index(self, axis, step=0):
        return (self.at[axis] + step) % 4


def meet(place):
    barrier = pltpu.get_barrier_semaphore()
    count = 0
    for axis in AXES:
        for step in (1, 2, 3):
            pl.semaphore_signal(barrier, inc=1, device_id=place.go(axis, step), device_id_type=MESH)
            count += 1
    pl.semaphore_signal(barrier, inc=1, device_id=place.go("c", 1), device_id_type=MESH)
    pl.semaphore_wait(barrier, count + 1)


class Tensor:
    def __init__(self, turn, which):
        self.number, self.slot = 3 * turn + which, (turn + which) % 2
        self.layer, self.which = 1 - turn, which
        self.second = which == 0
        self.section = 2 * self.layer + (which == 1)


class Reduce:
    def __init__(self, place, **refs):
        self.place = place
        self.__dict__.update(refs)

    def link(self, t, number, src, dst, device):
        return pltpu.make_async_remote_copy(
            src_ref=src, dst_ref=dst, send_sem=self.sems.at[0, t.number, number],
            recv_sem=self.sems.at[1, t.number, number], device_id=device, device_id_type=MESH,
        )

    def ring(self, name, t, r):
        place, axis = self.place, ROUTES[r][0]
        own, far = self.pair.at[t.slot, r], self.far.at[t.slot, r]
        across, ahead, behind = place.index(axis, 2), place.index(axis, 1), place.index(axis, 3)
        source, number, step = {
            "fa": lambda: (own.at[across, 0:2], 0, 1),
            "fb": lambda: (own.at[across, 2:4], 1, 3),
            "db": lambda: (own.at[ahead, 2:4], 2, 1),
            "da": lambda: (own.at[behind, 0:2], 3, 3),
            "ma": lambda: (far.at[0], 4, 1),
            "mb": lambda: (far.at[1], 5, 3),
        }[name]()
        return self.link(t, 6 + 6 * r + number, source, far.at[number], place.go(axis, step))

    def line_copy(self, t, r, step):
        axis = ROUTES[r][1]
        source = self.line.at[t.slot, r, self.place.index(axis, step)]
        return self.link(t, 23 + 3 * r + step, source, self.line_in.at[t.slot, r, step - 1], self.place.go(axis, step))

    def spot_copy(self, t, r, step):
        axis = ROUTES[r][2]
        source = self.spot.at[t.slot, r, self.place.index(axis, step)]
        return self.link(t, 32 + 3 * r + step, source, self.spot_in.at[t.number, r, step - 1], self.place.go(axis, step))

    def rows_copy(self, t):
        source = self.rows.at[t.layer, 1 - self.place.at["c"]]
        return self.link(t, 42, source, self.rows_in.at[t.layer], self.place.go("c", 1))

    def part(self, buffer, t, i):
        pair = pl.ds(2 * i, 2)
        if not t.second:
            return [(3 * i, buffer.at[t.slot, :, :, :, pair])]
        return [
            (3 * i, buffer.at[t.slot, 0, :, :, pair]),
            (3 * i + 1, buffer.at[t.slot, 1, :, pair]),
            (3 * i + 2, buffer.at[t.slot, 2, pair]),
        ]

    def across(self, t, i):
        for (number, source), (_, target) in zip(self.part(self.stage, t, i), self.part(self.pair, t, i)):
            yield self.link(t, number, source, target, self.place.go("c", 1))

    def prepare(self, t, before):
        for i in range(2):
            for copy in self.across(before, i):
                copy.wait_send()
        pl.semaphore_wait(self.pair_credit, 1)

    def swap(self, t, i):
        for copy in self.across(t, i):
            copy.start()

    def swapped(self, t, i):
        for copy in self.across(t, i):
            copy.wait_recv()

    def first(self, t):
        for r in range(3):
            @pl.when(t.number >= 2)
            def _():
                pl.semaphore_wait(self.far_credit.at[r, 0], 1)
                pl.semaphore_wait(self.far_credit.at[r, 1], 1)

            for name in ("fa", "fb", "db", "da"):
                self.ring(name, t, r).start()

    def merge(self, t):
        place = self.place
        for r, (axis, _, _) in enumerate(ROUTES):
            own, far = self.pair.at[t.slot, r], self.far.at[t.slot, r]
            ahead, behind = place.index(axis, 1), place.index(axis, 3)
            self.ring("fa", t, r).wait_recv()
            far[0] = (far[0].astype(F32) + own[ahead, 0:2].astype(F32)).astype(BF16)
            self.ring("ma", t, r).start()
            self.ring("fb", t, r).wait_recv()
            far[1] = (far[1].astype(F32) + own[behind, 2:4].astype(F32)).astype(BF16)
            self.ring("mb", t, r).start()

    def second(self, t):
        place = self.place
        for r in range(3):
            for name in ("db", "da", "ma", "mb"):
                self.ring(name, t, r).wait_recv()
        for r, (axis, nxt, _) in enumerate(ROUTES):
            own, far = self.pair.at[t.slot, r], self.far.at[t.slot, r]
            me = place.index(axis)
            low = own[me, 0:2].astype(F32) + far[4].astype(F32) + far[3].astype(F32)
            high = own[me, 2:4].astype(F32) + far[2].astype(F32) + far[5].astype(F32)
            line = self.line.at[t.slot, r]
            line[0:2] = low.astype(BF16)
            line[2:4] = high.astype(BF16)
            for step in (1, 2, 3):
                self.line_copy(t, r, step).start()
        for r in range(3):
            for name in ("fa", "fb", "db", "da", "ma", "mb"):
                self.ring(name, t, r).wait_send()

        @pl.when(t.number + 2 < 6)
        def _():
            pl.semaphore_signal(self.pair_credit, inc=1, device_id=place.go("c", 1), device_id_type=MESH)
            for r, (axis, _, _) in enumerate(ROUTES):
                pl.semaphore_signal(self.far_credit.at[r, 0], inc=1, device_id=place.go(axis, 1), device_id_type=MESH)
                pl.semaphore_signal(self.far_credit.at[r, 1], inc=1, device_id=place.go(axis, 3), device_id_type=MESH)

    def third(self, t):
        for r, (_, axis, _) in enumerate(ROUTES):
            total = self.line[t.slot, r, self.place.index(axis)].astype(F32)
            for step in (1, 2, 3):
                self.line_copy(t, r, step).wait_recv()
                total = total + self.line_in[t.slot, r, step - 1].astype(F32)
            self.spot[t.slot, r] = total.astype(BF16)
            for step in (1, 2, 3):
                self.spot_copy(t, r, step).start()
        for r in range(3):
            for step in (1, 2, 3):
                self.line_copy(t, r, step).wait_send()

    def close(self, t):
        for r, (_, _, axis) in enumerate(ROUTES):
            total = self.spot[t.slot, r, self.place.index(axis)].astype(F32)
            for step in (1, 2, 3):
                self.spot_copy(t, r, step).wait_recv()
                total = total + self.spot_in[t.number, r, step - 1].astype(F32)
            if not t.second:
                self.first_out[t.section, 0, 0, r] = total.astype(BF16)
            elif r == 0:
                self.rows[t.layer, 0, 0:16] = total
            elif r == 1:
                self.rows[t.layer, 0, 16:24] = total[0:8]
                self.rows[t.layer, 1, 0:8] = total[8:16]
            else:
                self.rows[t.layer, 1, 8:24] = total
        for r in range(3):
            for step in (1, 2, 3):
                self.spot_copy(t, r, step).wait_send()
        if t.second:
            self.rows_copy(t).start()

    def finish(self):
        me = self.place.at["c"]
        for turn in range(2):
            t = Tensor(turn, 0)
            self.rows_copy(t).wait()
            self.second_out[t.layer, :, lanes(me * 384, 384)] = self.rows[t.layer, me]
            self.second_out[t.layer, :, lanes((1 - me) * 384, 384)] = self.rows_in[t.layer]
        for which in (1, 2):
            for i in range(2):
                for copy in self.across(Tensor(1, which), i):
                    copy.wait_send()


class Totals:
    def __init__(self, place, part, bufs, sems):
        self.place, self.part, self.bufs, self.sems = place, part, bufs, sems
        self.copies = []

    def send(self, src, dst, number, device):
        copy = pltpu.make_async_remote_copy(
            src_ref=src, dst_ref=dst, send_sem=self.sems.at[0, number], recv_sem=self.sems.at[1, number],
            device_id=device, device_id_type=MESH,
        )
        copy.start()
        self.copies.append(copy)
        return copy

    @staticmethod
    def half(core):
        return pl.ds(pl.multiple_of(core * 24, 8), 24)

    def start(self, small):
        me = self.place.at["c"]
        self.small = small
        self.now = [self.send(small.at[self.half(1 - me)], self.bufs.at[12], 0, self.place.go("c", 1))]

    def step(self, number):
        place, me = self.place, self.place.at["c"]
        for copy in self.now:
            copy.wait_recv()
        if number == 0:
            self.part[0] = self.small[self.half(me), :] + self.bufs[12]
        else:
            axis = AXES[number - 1]
            self.bufs[4 * number - 4 + place.at[axis]] = self.part[number - 1]
            self.part[number] = (
                (self.bufs[4 * number - 4] + self.bufs[4 * number - 3])
                + (self.bufs[4 * number - 2] + self.bufs[4 * number - 1])
            )
        if number < 3:
            axis = AXES[number]
            self.now = [
                self.send(self.part.at[number], self.bufs.at[4 * number + place.at[axis]], 1 + 3 * number + step - 1, place.go(axis, step))
                for step in (1, 2, 3)
            ]
        else:
            self.now = [self.send(self.part.at[3], self.bufs.at[13], 10, place.go("c", 1))]

    def close(self, out):
        me = self.place.at["c"]
        for copy in self.now:
            copy.wait_recv()
        out[self.half(me), :] = self.part[3]
        out[self.half(1 - me), :] = self.bufs[13]
        for copy in self.copies:
            copy.wait_send()


class Spread:
    def __init__(self, place, sems):
        self.place, self.sems = place, sems
        self.sent = []

    def make(self, number, src, dst, device):
        return pltpu.make_async_remote_copy(
            src_ref=src, dst_ref=dst, send_sem=self.sems.at[0, number], recv_sem=self.sems.at[1, number],
            device_id=device, device_id_type=MESH,
        )

    def send(self, number, src, dst, device):
        copy = self.make(number, src, dst, device)
        copy.start()
        self.sent.append(copy)

    def wait(self, number, ref):
        pltpu.make_async_remote_copy(
            src_ref=ref, dst_ref=ref, send_sem=self.sems.at[0, number], recv_sem=self.sems.at[1, number],
            device_id=self.place.go("c", 1), device_id_type=MESH,
        ).wait_recv()

    def drain(self):
        for copy in self.sent:
            copy.wait_send()


GATHER_MESSAGES = 99


class Gather(Spread):
    def __init__(self, place, full, sems):
        super().__init__(place, sems)
        self.full = full
        y = place.at["y"]
        self.first = {"x": 3, "z": 1}
        self.second = {"x": jnp.where(y == 3, 1, 2), "z": jnp.where(y == 1, 3, 2)}
        self.third = {"x": jnp.where(y == 3, 2, 1), "z": jnp.where(y == 1, 2, 3)}

    def rows(self, route, step, sub=None, core=None):
        core = self.place.at["c"] if core is None else core
        block = (0 if route == "x" else 8) + self.place.index(route, step) * 2 + core
        return (block // 4, block % 4, slice(None) if sub is None else slice(16 * sub, 16 * sub + 16))

    def ref(self, rel, route, step, sub=None):
        return self.full.at[(self.place.index("y", rel),) + self.rows(route, step, sub)]

    @staticmethod
    def along_y(rel, route, sub):
        return 3 * (2 * (rel - 1) + (route == "z")) + sub

    @staticmethod
    def in_plane(rel, route, kind, sub):
        return 18 + 9 * (2 * (rel - 1) + (route == "z")) + 3 * kind + sub

    @staticmethod
    def across(rel, route, step):
        return 72 + 4 * (2 * (rel - 1) + (route == "z")) + step

    def load(self, source, sems):
        at = self.place.at
        mine, rest = [], []
        for half, route in enumerate(("x", "z")):
            for block in range(8):
                number = 8 * half + (at[route] * 2 + at["c"] + block) % 8
                rows = pl.ds(pl.multiple_of(number * 48, 16), 48)
                copy = pltpu.make_async_copy(
                    source.at[rows], self.full.at[at["y"], number // 4, number % 4], sems.at[half, block]
                )
                (rest if block else mine).append(copy)
        for copy in mine + rest:
            copy.start()
        return mine, rest

    def own(self, up, down):
        copies = []
        for sub in range(3):
            for route, step in ((up, 1), (down, 3)):
                mine = self.ref(0, route, 0, sub)
                copies.append(self.make(self.along_y(4 - step, route, sub), mine, mine, self.place.go("y", step)))
        self.sent += copies
        return copies

    def arrive(self, rels):
        for sub in range(3):
            for route, rel in rels.items():
                piece = self.ref(rel, route, 0, sub)
                self.wait(self.along_y(rel, route, sub), piece)
                if rels is self.first:
                    self.send(self.along_y(2, route, sub), piece, piece, self.place.go("y", 4 - rel))
                for kind, step in ((0, 1), (1, 3)):
                    self.send(self.in_plane(rel, route, kind, sub), piece, piece, self.place.go(route, step))
        for route, rel in rels.items():
            piece = self.ref(rel, route, 0)
            self.send(self.across(rel, route, 0), piece, piece, self.place.go("c", 1))

    def turn(self, rels):
        place = self.place
        clockwise = 1 - 2 * place.at["c"]
        for sub, way in ((0, 1), (1, clockwise), (2, -1)):
            for route, rel in rels.items():
                for kind, step in ((0, 3), (1, 1)):
                    self.wait(self.in_plane(rel, route, kind, sub), self.ref(rel, route, step, sub))
                piece = self.ref(rel, route, 4 - way, sub)
                self.send(self.in_plane(rel, route, 2, sub), piece, piece, place.go(route, 4 + way))
        for route, rel in rels.items():
            for step in (3, 1):
                piece = self.ref(rel, route, step)
                self.send(self.across(rel, route, step), piece, piece, place.go("c", 1))

    def end(self, rels):
        for route, rel in rels.items():
            for sub in range(3):
                self.wait(self.in_plane(rel, route, 2, sub), self.ref(rel, route, 2, sub))
            piece = self.ref(rel, route, 2)
            self.send(self.across(rel, route, 2), piece, piece, self.place.go("c", 1))

    def ending(self, rels):
        waits, copies = [], []
        for route, rel in rels.items():
            for sub in range(3):
                ref = self.ref(rel, route, 2, sub)
                waits.append(self.make(self.in_plane(rel, route, 2, sub), ref, ref, self.place.go("c", 1)))
            piece = self.ref(rel, route, 2)
            copies.append(self.make(self.across(rel, route, 2), piece, piece, self.place.go("c", 1)))
        self.sent += copies
        return waits, copies

    def settle(self, section):
        rel = (section - self.place.at["y"] + 4) % 4
        other = 1 - self.place.at["c"]

        def run():
            for route in ("x", "z"):
                for step in range(4):
                    self.wait(self.across(rel, route, step), self.full.at[(section,) + self.rows(route, step, core=other)])

        pl.when(rel > 0)(run)


def layers_kernel(
    tokens, masked, cotangent, live, mask_token, norm_gain, norm_shift, layer_scale, w_own, w2_hbm,
    tables,
    block_out, tokens_grad, first_grad, second_out, totals,
    w, w2, h, qkv, probs, o, a, slope, p, n, bias, table, select_f, by_x, fold_sums, du, dp, g, vec, vecs, small,
    stage, pair, far, line, line_in, spot, spot_in, rows, rows_in, part, bufs, first_out,
    tokens_in, cotangent_in, load_sems, w2_sems, image_sems, gather_sems, sems, small_sems, share_sems, share_out_sems, pair_credit, far_credit,
):
    place = Place()
    vec[0:1] = norm_gain[...]
    vec[1:2] = norm_shift[...]
    vec[2:3] = layer_scale[...]
    vec[3:8] = jnp.zeros((5, D), F32)
    y = place.at["y"]
    gather = Gather(place, w, gather_sems)
    own_first, own_rest = gather.load(w_own.at[0], load_sems)
    images = [
        pltpu.make_async_copy(source, target, image_sems.at[i])
        for i, (source, target) in enumerate(((tokens, tokens_in), (cotangent, cotangent_in)))
    ]
    for copy in images:
        copy.start()
    meet(place)
    for copy in own_first:
        copy.wait()
    for copy in gather.own("x", "z"):
        copy.start()
    own_later = gather.own("z", "x")

    @pl.when(y == 0)
    def _():
        for copy in own_later:
            copy.start()

    def second_weights(layer):
        copies = []
        for block in range(8):
            rows = pl.ds(block * 384, 384)
            copies.append(pltpu.make_async_copy(w2_hbm.at[layer, rows], w2.at[rows], w2_sems.at[block]))
        return copies

    def load_second(layer):
        for copy in second_weights(layer):
            copy.start()

    def loaded_second(layer):
        for copy in second_weights(layer):
            copy.wait()

    def loaded(copies):
        for copy in copies:
            copy.wait()

    load_second(0)
    vecs[y] = vec[...]
    for step in (1, 2, 3):
        gather.send(95 + step, vec, vecs.at[y], place.go("y", step))
    valid = jnp.where(y < live[lax.axis_index("dp")], 1.0, 0.0)
    body = Body(
        valid=valid, core=place.at["c"], vecs=vecs, table=table,
        select_forward=select_f, by_x=by_x, block_out=tokens_in, small=small,
        w=w, w2=w2, h=h, qkv=qkv, probs=probs, o=o, a=a, slope=slope, p=p, n=n, bias=bias,
        sums=fold_sums, du=du, dp=dp, g=g, stage=stage, pair=pair,
    )
    reduce = Reduce(
        place, stage=stage, pair=pair, far=far, line=line, line_in=line_in, spot=spot, spot_in=spot_in,
        rows=rows, rows_in=rows_in, first_out=first_out, second_out=second_out, sems=sems,
        pair_credit=pair_credit, far_credit=far_credit,
    )
    body.reduce = reduce
    sums = Totals(place, part, bufs, small_sems)

    gather.arrive(gather.first)

    @pl.when(y != 0)
    def _():
        for copy in own_later:
            copy.start()

    fold_sums[...] = jnp.zeros_like(fold_sums)
    square = (ROWS, KEYS)
    diagonal = lax.broadcasted_iota(jnp.int32, square, 0) == lax.broadcasted_iota(jnp.int32, square, 1)
    flags = jnp.concatenate([masked[...].astype(F32), jnp.zeros((1, KEYS - SEQ), F32)], axis=1)
    here = jnp.sum(jnp.where(diagonal, flags, 0.0), axis=1, keepdims=True)
    h[0, 192:] = jnp.zeros((16, D), BF16)
    for copy in images:
        copy.wait()
    start = tokens_in[0].astype(F32)
    h[0, :SEQ] = (start + here[:SEQ] * (mask_token[...].astype(F32).reshape(1, D) - start)).astype(BF16)
    g[192:] = jnp.zeros((16, D), BF16)
    g[:SEQ] = (cotangent_in[0].astype(F32) * valid).astype(BF16)
    body.make_selectors()
    body.read_tables(tables)
    body.expand_bias(0, 0, 6)
    gather.arrive(gather.second)
    body.expand_bias(0, 6, 12)
    gather.turn(gather.first)
    body.expand_bias(1, 0, 6)
    gather.arrive(gather.third)
    gather.turn(gather.second)
    body.expand_bias(1, 6, 12)
    gather.end(gather.first)
    gather.end(gather.second)
    for step in (1, 2, 3):
        gather.wait(95 + step, vecs.at[place.index("y", 4 - step)])
    loaded(own_rest)
    gather.turn(gather.third)
    last_waits, last_copies = gather.ending(gather.third)

    def forward_layer(layer, _):
        gather.settle(2 * layer)
        body.attend_forward(layer)

        @pl.when(layer == 0)
        def _():
            for copy in last_waits:
                copy.wait_recv()
            for copy in last_copies:
                copy.start()

        gather.settle(2 * layer + 1)
        loaded_second(layer)
        body.dense_forward(layer)

        @pl.when(layer == 0)
        def _():
            load_second(1)

        return 0

    lax.fori_loop(0, 2, forward_layer, 0)
    block_copy = pltpu.make_async_copy(tokens_in, block_out, image_sems.at[0])
    block_copy.start()
    gather.drain()

    def backward_layer(turn, _):
        layer = 1 - turn
        again = turn > 0
        second, dense, attention = (Tensor(turn, which) for which in range(3))
        _, dense_before, attention_before = (Tensor(turn - 1, which) for which in range(3))
        body.enter(layer, 1)

        @pl.when(again)
        def _():
            reduce.prepare(second, dense_before)

        body.second_half(second, False)

        @pl.when(again)
        def _():
            reduce.third(dense_before)
            loaded_second(0)

        body.down(layer)

        @pl.when(turn == 0)
        def _():
            load_second(0)

        @pl.when(again)
        def _():
            reduce.merge(attention_before)

        body.second_half(second, True)
        reduce.first(second)

        @pl.when(again)
        def _():
            reduce.second(attention_before)
            reduce.prepare(dense, attention_before)

        body.first_half(dense, False)

        @pl.when(again)
        def _():
            reduce.close(dense_before)

        body.leave(layer, 1)
        reduce.merge(second)
        body.first_half(dense, True)
        reduce.first(dense)
        body.enter(layer, 0)
        body.back_out(layer)

        @pl.when(again)
        def _():
            reduce.third(attention_before)

        body.pairs(layer, 0)
        reduce.second(second)
        body.pairs(layer, 1)
        reduce.merge(dense)

        @pl.when(again)
        def _():
            reduce.close(attention_before)

        reduce.prepare(attention, second)
        body.first_half(attention, False)
        body.fold_bias(layer)
        reduce.third(second)
        body.leave(layer, 0)
        reduce.second(dense)
        body.first_half(attention, True)
        reduce.first(attention)
        reduce.close(second)
        return 0

    lax.fori_loop(0, 2, backward_layer, 0)
    dense, attention = Tensor(1, 1), Tensor(1, 2)
    grad = g[...].astype(F32)
    cotangent_in[0] = (grad * (1.0 - here)).astype(BF16)[:SEQ]
    tokens_copy = pltpu.make_async_copy(cotangent_in, tokens_grad, image_sems.at[1])
    tokens_copy.start()
    small[20:21, :] = jnp.sum(grad * here, axis=0, keepdims=True)
    small[21:24, :] = jnp.zeros((3, D), F32)
    sums.start(small)
    reduce.third(dense)
    reduce.merge(attention)
    reduce.close(dense)
    reduce.second(attention)
    sums.step(0)
    reduce.third(attention)
    sums.step(1)
    reduce.close(attention)
    beside = [lambda: sums.step(2), lambda: sums.step(3), lambda: sums.close(totals)]
    Share(place, first_out, w.at[3], share_sems).run(first_grad, share_out_sems, beside)
    reduce.finish()
    block_copy.wait()
    tokens_copy.wait()


def layers(tokens, masked, cotangent, live, mask_token, norm_gain, norm_shift, layer_scale, w_own, w2, tables):
    vm = pl.BlockSpec(memory_space=pltpu.VMEM)
    hbm = pl.BlockSpec(memory_space=pl.ANY)
    sm = pl.BlockSpec(memory_space=pltpu.SMEM)
    V, DMA, REGULAR = pltpu.VMEM, pltpu.SemaphoreType.DMA, pltpu.SemaphoreType.REGULAR
    return pl.pallas_call(
        layers_kernel,
        out_shape=(
            jax.ShapeDtypeStruct((1, SEQ, D), BF16),
            jax.ShapeDtypeStruct((1, SEQ, D), BF16),
            jax.ShapeDtypeStruct((4, 4, 48, FF), BF16),
            jax.ShapeDtypeStruct((2, 24, D), F32),
            jax.ShapeDtypeStruct((48, D), F32),
        ),
        in_specs=[hbm, vm, hbm, sm, vm, vm, vm, vm, hbm, hbm, vm],
        out_specs=(hbm, hbm, hbm, vm, vm),
        scratch_shapes=[
            V((4, 4, 4, 48, FF), BF16), V((FF, D), BF16), V((4, ROWS, D), BF16), V((2, KEYS, 2304), BF16),
            V((2, HEADS, 16 * GRID, KEYS), BF16), V((2, ROWS, D), BF16), V((2, ROWS, FF), BF16), V((2, ROWS, FF), BF16),
            V((4, ROWS, D), BF16), V((2, ROWS, D), BF16), V((2, HEADS, ROWS, KEYS), BF16), V((2 * HEADS, 896), F32), V((384, KEYS), BF16),
            V((16 * GRID, ROWS), BF16),
            V((3, ROWS, 128), F32), V((ROWS, FF), BF16), V((ROWS, D), BF16), V((ROWS, D), BF16),
            V((8, D), F32), V((4, 8, D), F32), V((48, D), F32),
            V((2,) + HALF, BF16), V((2,) + HALF, BF16), V((2, 3, 6, 2, 4, 16, 384), BF16),
            V((2, 3, 4, 4, 16, 384), BF16), V((2, 3, 3, 4, 16, 384), BF16),
            V((2, 3, 4, 16, 384), BF16), V((6, 3, 3, 16, 384), BF16),
            V((2, 2, 24, 384), F32), V((2, 24, 384), F32), V((4, 24, D), F32), V((14, 24, D), F32),
            V((4, 1, 1, 3, 16, 384), BF16), V((1, SEQ, D), BF16), V((1, SEQ, D), BF16),
            DMA((2, 8)), DMA((8,)), DMA((2,)), DMA((2, GATHER_MESSAGES)), DMA((2, 6, 43)), DMA((2, 11)), DMA((2, 75)), DMA((48,)), REGULAR, REGULAR((3, 2)),
        ],
        compiler_params=pltpu.CompilerParams(
            collective_id=1, has_side_effects=True, vmem_limit_bytes=64 * 2**20
        ),
    )(tokens, masked, cotangent, live, mask_token, norm_gain, norm_shift, layer_scale, w_own, w2, tables)


class Share(Spread):
    def __init__(self, place, blocks, full, sems):
        super().__init__(place, sems)
        self.blocks, self.full = blocks, full

    def regions(self, c, x, y, z):
        def columns(third):
            return pl.ds(pl.multiple_of((c * 4 + third[0]) * 384, 128), third[1] * 384)

        for route, (a1, a2, a3) in enumerate(((x, y, z), (y, z, x), (z, x, y))):
            yield route, self.full.at[
                pl.ds(*a1), pl.ds(*a2), slice(16 * route, 16 * route + 16), columns(a3)
            ]

    def pass_on(self, base, regions, device):
        for route, region in regions:
            self.send(base + route, region, region, device)

    def await_all(self, base, regions):
        for route, region in regions:
            self.wait(base + route, region)

    def keep(self, out, c, x, y, z):
        for (route, region), (_, target) in zip(self.regions(c, x, y, z), Share(self.place, None, out, None).regions(c, x, y, z)):
            copy = pltpu.make_async_copy(region, target, self.out_sems.at[len(self.kept)])
            copy.start()
            self.kept.append(copy)

    def run(self, out, out_sems, beside):
        place = self.place
        at = place.at
        self.out_sems, self.kept = out_sems, []
        c, x, y, z = at["c"], (at["x"], 1), (at["y"], 1), (at["z"], 1)
        other = 1 - c
        every = (0, 4)
        halves = ((0, 2), (2, 2))

        def near(axis, step):
            return (place.index(axis, step), 1)

        for route, region in self.regions(c, x, y, z):
            for step in (1, 2, 3):
                source = self.blocks.at[place.index("y", step), :, :, route]
                self.send(3 * (step - 1) + route, source, region, place.go("y", step))
            region[...] = self.blocks[at["y"], :, :, route]
        beside[0]()
        for step in (1, 2, 3):
            self.await_all(3 * (step - 1), self.regions(c, x, near("y", 4 - step), z))
        for step in (1, 3, 2):
            self.pass_on(9 + 3 * (step - 1), self.regions(c, x, halves[0], z), place.go("x", step))
            self.pass_on(18 + 3 * (step - 1), self.regions(c, x, halves[1], z), place.go("z", step))
        beside[1]()
        for step in (1, 3, 2):
            self.await_all(9 + 3 * (step - 1), self.regions(c, near("x", 4 - step), halves[0], z))
            self.await_all(18 + 3 * (step - 1), self.regions(c, x, halves[1], near("z", 4 - step)))
        for step in (1, 3):
            self.pass_on(27 + 3 * (step - 1), self.regions(c, every, halves[0], z), place.go("z", step))
            self.pass_on(36 + 3 * (step - 1), self.regions(c, x, halves[1], every), place.go("x", step))
        self.pass_on(45, self.regions(c, every, halves[0], z), place.go("c", 1))
        self.pass_on(48, self.regions(c, x, halves[1], every), place.go("c", 1))
        self.keep(out, c, every, halves[0], z)
        self.keep(out, c, x, halves[1], every)
        beside[2]()
        for step, part, base in ((1, (0, 1), 30), (3, (1, 1), 69)):
            self.await_all(27 + 3 * (step - 1), self.regions(c, every, halves[0], near("z", 4 - step)))
            self.pass_on(base, self.regions(c, every, part, near("z", 4 - step)), place.go("z", step))
            part = (part[0] + 2, 1)
            self.await_all(36 + 3 * (step - 1), self.regions(c, near("x", 4 - step), halves[1], every))
            self.pass_on(base + (9 if base == 30 else 3), self.regions(c, near("x", 4 - step), part, every), place.go("x", step))
        for step in (1, 3):
            self.pass_on(51 + 3 * (step - 1), self.regions(c, every, halves[0], near("z", 4 - step)), place.go("c", 1))
            self.pass_on(60 + 3 * (step - 1), self.regions(c, near("x", 4 - step), halves[1], every), place.go("c", 1))
            self.keep(out, c, every, halves[0], near("z", 4 - step))
            self.keep(out, c, near("x", 4 - step), halves[1], every)
        self.await_all(45, self.regions(other, every, halves[0], z))
        self.keep(out, other, every, halves[0], z)
        self.await_all(48, self.regions(other, x, halves[1], every))
        self.keep(out, other, x, halves[1], every)
        for step in (1, 3):
            self.await_all(51 + 3 * (step - 1), self.regions(other, every, halves[0], near("z", 4 - step)))
            self.keep(out, other, every, halves[0], near("z", 4 - step))
            self.await_all(60 + 3 * (step - 1), self.regions(other, near("x", 4 - step), halves[1], every))
            self.keep(out, other, near("x", 4 - step), halves[1], every)
        for part, base in ((0, 30), (1, 69)):
            self.await_all(base, self.regions(c, every, (part, 1), near("z", 2)))
            self.await_all(base + (9 if base == 30 else 3), self.regions(c, near("x", 2), (part + 2, 1), every))
        self.pass_on(54, self.regions(c, every, halves[0], near("z", 2)), place.go("c", 1))
        self.pass_on(63, self.regions(c, near("x", 2), halves[1], every), place.go("c", 1))
        self.keep(out, c, every, halves[0], near("z", 2))
        self.keep(out, c, near("x", 2), halves[1], every)
        self.await_all(54, self.regions(other, every, halves[0], near("z", 2)))
        self.keep(out, other, every, halves[0], near("z", 2))
        self.await_all(63, self.regions(other, near("x", 2), halves[1], every))
        self.keep(out, other, near("x", 2), halves[1], every)
        for copy in self.kept:
            copy.wait()
        self.drain()


def finish_kernel(
    first, block_in, tokens_in, second_in, totals, live,
    block_out, tokens_grad, first_grad, second_grad, gain_grad, shift_grad, scale_grad, table_grad, mask_grad, rms_out,
    narrow, wide, images, load_sems, store_sems, image_sems,
):
    loads, stores = [], []
    through = []
    for i, (source, target) in enumerate(((block_in, block_out), (tokens_in, tokens_grad))):
        through.append((
            pltpu.make_async_copy(source, images.at[i], image_sems.at[i]),
            pltpu.make_async_copy(images.at[i], target, image_sems.at[2 + i]),
        ))
    for block in range(16):
        a1, a2 = block // 4, block % 4
        rows = pl.ds(block * 48, 48)
        loads.append(pltpu.make_async_copy(first.at[a1, a2], narrow.at[a1, a2], load_sems.at[block]))
        stores.append(pltpu.make_async_copy(wide.at[rows], first_grad.at[0, rows], store_sems.at[block]))
    for load in loads:
        load.start()
    for load, _ in through:
        load.start()
    for block in range(16):
        loads[block].wait()
        wide[block * 48 : block * 48 + 48, :] = narrow[block // 4, block % 4].astype(F32)
        stores[block].start()
    for load, store in through:
        load.wait()
        store.start()
    second_grad[...] = second_in[...]
    own = 8 + 3 * lax.axis_index("section")
    scale_grad[...] = totals[pl.ds(own, 1), :]
    gain_grad[...] = totals[pl.ds(own + 1, 1), :]
    shift_grad[...] = totals[pl.ds(own + 2, 1), :]
    mask_grad[...] = totals[20, :]
    count = lax.fori_loop(0, live.shape[0], lambda i, total: total + live[i], 0)
    tokens = count.astype(F32) * (SEQ * D)
    rms = jnp.sqrt(jnp.sum(totals[0:8, :], axis=1, keepdims=True) / tokens)
    rms_out[...] = jnp.concatenate(
        [jnp.concatenate([rms[2 * s + k : 2 * s + k + 1] for s in range(4)], axis=1) for k in range(2)], axis=0
    )
    for layer in range(2):
        table_grad[:, layer, :] = totals[24 + layer * HEADS : 24 + (layer + 1) * HEADS, : table_grad.shape[2]]
    for store in stores:
        store.wait()
    for _, store in through:
        store.wait()


def finish_all(first, block_out, tokens_grad, second, totals, live, entries):
    vm = pl.BlockSpec(memory_space=pltpu.VMEM)
    hbm = pl.BlockSpec(memory_space=pl.ANY)
    image, pair, vector = (1, SEQ, D), (2, 24, D), (1, D)
    return pl.pallas_call(
        finish_kernel,
        out_shape=(
            jax.ShapeDtypeStruct(image, BF16), jax.ShapeDtypeStruct(image, BF16), jax.ShapeDtypeStruct((1, D, FF), F32),
            jax.ShapeDtypeStruct(pair, F32), jax.ShapeDtypeStruct(vector, F32), jax.ShapeDtypeStruct(vector, F32),
            jax.ShapeDtypeStruct(vector, F32), jax.ShapeDtypeStruct((HEADS, 2, entries), F32),
            jax.ShapeDtypeStruct((D,), F32), jax.ShapeDtypeStruct((2, 4), F32),
        ),
        in_specs=[hbm, hbm, hbm, vm, vm, pl.BlockSpec(memory_space=pltpu.SMEM)],
        out_specs=(hbm, hbm, hbm) + (vm,) * 7,
        scratch_shapes=[
            pltpu.VMEM((4, 4, 48, FF), BF16), pltpu.VMEM((D, FF), F32), pltpu.VMEM((2, 1, SEQ, D), BF16),
            pltpu.SemaphoreType.DMA((16,)), pltpu.SemaphoreType.DMA((16,)), pltpu.SemaphoreType.DMA((4,)),
        ],
        compiler_params=pltpu.CompilerParams(vmem_limit_bytes=62 * 2**20),
    )(first, block_out, tokens_grad, second, totals, live)


def on_device(
    tokens, masked, live_images, mask_token, norm_gain, norm_shift, w_first, w_second, layer_scale, rel_table, cotangent
):
    block_out, tokens_grad, first, second, totals = layers(
        tokens, masked, cotangent, live_images, mask_token, norm_gain, norm_shift, layer_scale, w_first, w_second,
        jnp.transpose(rel_table, (2, 0, 1)),
    )
    *outs, table_grad, mask_grad, rms = finish_all(
        first, block_out, tokens_grad, second, totals, live_images, rel_table.shape[1]
    )
    return (*outs, jnp.transpose(table_grad, (1, 2, 0)), mask_grad, rms.T)


def solution(mesh):
    both = P(("dp", "section"), None, None)
    part = P("section", None)
    return jax.shard_map(
        on_device,
        mesh=mesh,
        in_specs=(both, P(("dp", "section"), None), P(), P(), part, part, P("section", None, None), P(), part, P(), both),
        out_specs=(
            both, both, P("section", None, None), P(None, ("dp", "section"), None), part, part, part, P(), P(), P(),
        ),
        check_vma=False,
    )
```

```python
import functools
import math

import jax
import jax.numpy as jnp
from jax import lax
from jax.experimental import pallas as pl
from jax.experimental.pallas import tpu as pltpu
from jax.sharding import PartitionSpec as P

SEQ, ROWS, KEYS = 197, 208, 256
D, FF, HEADS, GRID = 768, 3072, 12, 14
SPAN = 2 * GRID - 1
EPSILON = 1e-06
INV_ROOT = 0.125
INV_ROOT_TWO_PI = 0.3989422804014327
F32, BF16 = jnp.float32, jnp.bfloat16
HALF = (3, 4, 4, 4, 16, 384)


def mm(a, b):
    return lax.dot_general(a, b, (((1,), (0,)), ((), ())), preferred_element_type=F32)


def mm_nt(a, b):
    return lax.dot_general(a, b, (((1,), (1,)), ((), ())), preferred_element_type=F32)


def mm_tn(a, b):
    return lax.dot_general(a, b, (((0,), (0,)), ((), ())), preferred_element_type=F32)


def lanes(start, size):
    return pl.ds(pl.multiple_of(start, 128), size)


def patch_offsets(token):
    patch = token - 1
    return patch + (SPAN - GRID) * ((patch * 4682) >> 16)


def ones(condition):
    return jnp.where(condition, 1.0, 0.0).astype(BF16)


def centre(h):
    average = jnp.mean(h, axis=-1, keepdims=True)
    centred = h - average
    inv_std = lax.rsqrt(jnp.mean(centred * centred, axis=-1, keepdims=True) + EPSILON)
    return centred * inv_std, inv_std


def gelu_pair(u):
    size = jnp.abs(u)
    t = 1.0 / (1.0 + 0.23164189 * size)
    bell = jnp.exp(-0.5 * u * u)
    poly = t * (
        0.127414796
        + t * (-0.142248368 + t * (0.7107068705 + t * (-0.7265760135 + t * 0.5307027145)))
    )
    tail = poly * bell
    phi = jnp.where(u >= 0.0, 1.0 - tail, tail)
    return u * phi, phi + u * bell * INV_ROOT_TWO_PI


def half_mask(rows, parity):
    lane = lax.broadcasted_iota(jnp.int32, (rows, 128), 1)
    return (lane < 64) if parity == 0 else (lane >= 64)


def keep_half(block, parity):
    return jnp.where(half_mask(block.shape[0], parity), block, jnp.zeros_like(block))


class Body:
    def __init__(self, **refs):
        self.__dict__.update(refs)

    def make_selectors(self):
        row = lax.broadcasted_iota(jnp.int32, (384, KEYS), 0)
        token = lax.broadcasted_iota(jnp.int32, (384, KEYS), 1)
        self.select_forward[...] = ones((row == patch_offsets(token)) & (token > 0) & (token < SEQ))
        row = lax.broadcasted_iota(jnp.int32, (16 * GRID, ROWS), 0)
        token = lax.broadcasted_iota(jnp.int32, (16 * GRID, ROWS), 1)
        patch = token - 1
        y = (patch * 4682) >> 16
        wanted = jnp.where(token == 0, GRID, (patch - GRID * y) * 16 + y)
        self.by_x[...] = ones((row == wanted) & (token < SEQ))

    def read_tables(self, tables):
        shape = (tables.shape[2], 896)
        entry = lax.broadcasted_iota(jnp.int32, shape, 0)
        lane = lax.broadcasted_iota(jnp.int32, shape, 1)
        source = jnp.where(lane < 768, SPAN * SPAN - 1 - lane, lane + (SPAN * SPAN - 768))
        select = ones(entry == source)
        for layer in range(2):
            self.table[layer * HEADS : (layer + 1) * HEADS, :] = mm(tables[:, layer, :].astype(BF16), select)

    def expand_bias(self, layer, lo, hi):
        def head(index, _):
            entries = self.table[pl.ds(layer * HEADS + index, 1), :]
            base = jnp.broadcast_to(entries[:, :768], (16, 768))
            base = pltpu.roll(base, 404, 1, stride=1, stride_axis=0)
            for yi in range(GRID):
                turned = pltpu.roll(base, SPAN * yi, 1) if yi else base
                for t in range(3):
                    self.sums[t, 1 + GRID * yi : 1 + GRID * (yi + 1), :] = turned[:GRID, 128 * t : 128 * t + 128]
            spread = jnp.concatenate([self.sums[0], self.sums[1], self.sums[2]], axis=1)
            grid = mm(spread.astype(BF16), self.select_forward[...])
            row = lax.broadcasted_iota(jnp.int32, (ROWS, KEYS), 0)
            column = lax.broadcasted_iota(jnp.int32, (ROWS, KEYS), 1)
            corner = entries[:, 768:]
            grid = jnp.where(row == 0, corner[:, 0:1], grid)
            grid = jnp.where(column == 0, corner[:, 1:2], grid)
            grid = jnp.where((row == 0) & (column == 0), corner[:, 2:3], grid)
            self.bias[layer, index] = jnp.where(column >= SEQ, -1e30, grid).astype(BF16)
            return 0

        lax.fori_loop(lo, hi, head, 0)

    def normed(self, s):
        scaled, _ = centre(self.h[s].astype(F32))
        gain = self.vecs[s, 0:1, :]
        shift = self.vecs[s, 1:2, :]
        self.n[0] = (scaled * gain + shift).astype(BF16)

    def note(self, row, value):
        self.small[pl.ds(row, 1), :] = value

    def finish(self, s, left, right):
        real = (lax.broadcasted_iota(jnp.int32, (ROWS, 1), 0) < SEQ).astype(F32) * self.valid

        projected = mm(left[...], right)
        branch = self.vecs[s, 2:3, :] * projected
        result = self.h[s].astype(F32) + branch
        self.p[s] = projected.astype(BF16)
        self.note(2 * s, jnp.sum(branch * branch * real, axis=0, keepdims=True))
        self.note(2 * s + 1, jnp.sum(result * result * real, axis=0, keepdims=True))
        self.h[s + 1] = result.astype(BF16)

    def attend_forward(self, layer):
        s = 2 * layer
        self.normed(s)

        def project(j, _):
            columns = lanes(j * 1152, 1152)
            weights = self.w[s, :, :, :, columns].reshape(D, 1152)
            self.qkv[layer, :ROWS, columns] = mm(self.n[0], weights).astype(BF16)
            return 0

        lax.fori_loop(0, 2, project, 0)
        self.qkv[layer, ROWS:, :] = jnp.zeros((KEYS - ROWS, 2304), BF16)

        def pair(j):
            q = self.qkv[layer, :ROWS, lanes(j * 128, 128)]
            k = self.qkv[layer, :, lanes(768 + j * 128, 128)]
            v = self.qkv[layer, :, lanes(1536 + j * 128, 128)]
            mixed = jnp.zeros((ROWS, 128), F32)
            for parity in range(2):
                scores = mm_nt(keep_half(q, parity), k) * INV_ROOT + self.bias[layer, 2 * j + parity].astype(F32)
                peak = jnp.max(scores, axis=-1, keepdims=True)
                exps = jnp.exp(scores - peak)
                total = jnp.sum(exps, axis=-1, keepdims=True)
                probs = (exps * (1.0 / total)).astype(BF16)
                self.probs[layer, 2 * j + parity, :ROWS] = probs
                mixed = mixed + mm(probs, keep_half(v, parity))
            self.n[1 + layer, :, lanes(j * 128, 128)] = mixed.astype(BF16)

        def pairs(i, _):
            for j in range(3):
                pair(3 * i + j)
            return 0

        lax.fori_loop(0, 2, pairs, 0)
        self.finish(s, self.n.at[1 + layer], self.w[s, :, :, :, 2304:].reshape(D, D))

    def dense_forward(self, layer):
        s = 2 * layer + 1
        self.normed(s)

        def up(j, _):
            columns = lanes(j * 1024, 1024)
            u = mm(self.n[0], self.w[s, :, :, :, columns].reshape(D, 1024))
            act, slope = gelu_pair(u)
            self.a[layer, :, columns] = act.astype(BF16)
            self.slope[layer, :, columns] = slope.astype(BF16)
            return 0

        lax.fori_loop(0, 3, up, 0)

    def last_finish(self):
        real = (lax.broadcasted_iota(jnp.int32, (ROWS, 1), 0) < SEQ).astype(F32) * self.valid

        def block(j, _):
            columns = lanes(j * 384, 384)
            projected = mm(self.a[1], self.w2[:, columns])
            branch = self.vecs[3, 2:3, columns] * projected
            result = self.h[3, :, columns].astype(F32) + branch
            self.p[3, :, columns] = projected.astype(BF16)
            self.small[6:7, columns] = jnp.sum(branch * branch * real, axis=0, keepdims=True)
            self.small[7:8, columns] = jnp.sum(result * result * real, axis=0, keepdims=True)
            self.block_out[0, :, columns] = (result[:SEQ] * self.valid).astype(BF16)
            return 0

        lax.fori_loop(0, 2, block, 0)

    def enter(self, layer, dense):
        s = 2 * layer + dense
        g = self.g[...].astype(F32)
        dp = (g * self.vecs[s, 2:3, :]).astype(BF16)
        self.dp[...] = dp
        self.normed(s)
        if not dense:
            self.du[:, 2304:] = dp

    def leave(self, layer, dense):
        s = 2 * layer + dense
        width = FF if dense else 2304
        dn = mm_nt(self.du[:, :width], self.w[s, :, :, :, :width].reshape(D, width))
        scaled, inv_std = centre(self.h[s].astype(F32))
        row = 8 + 3 * s
        g = self.g[...].astype(F32)
        self.note(row, jnp.sum(g * self.p[s].astype(F32), axis=0, keepdims=True))
        self.note(row + 1, jnp.sum(dn * scaled, axis=0, keepdims=True))
        self.note(row + 2, jnp.sum(dn, axis=0, keepdims=True))
        e = dn * self.vecs[s, 0:1, :]
        mean_e = jnp.mean(e, axis=-1, keepdims=True)
        mean_ex = jnp.mean(e * scaled, axis=-1, keepdims=True)
        g = g + inv_std * (e - mean_e - scaled * mean_ex)
        self.g[...] = g.astype(BF16)

    def put(self, t, mine, route, a1, a2, a3, piece):
        if mine:
            pair = self.pair.at[t.slot, route, a1, a2, a3]
            pair[...] = (piece + pair[...].astype(F32)).astype(BF16)
        else:
            self.stage[t.slot, route, a1, a2, a3] = piece.astype(BF16)

    def first_half(self, t, mine):
        half = self.core if mine else 1 - self.core

        def block(i, _):
            if mine:
                self.reduce.swapped(t, i)
            j = half * 2 + i
            left = jnp.where(j == 3, 1 + t.layer, 0) if t.which == 2 else 0
            grad = mm_tn(self.n[left], self.du[:, lanes(j * 768, 768)])
            for side in range(2):
                for rb in range(16):
                    for route in range(3):
                        top = rb * 48 + route * 16
                        self.put(
                            t, mine, route, rb // 4, rb % 4, 2 * i + side,
                            grad[top : top + 16, 384 * side : 384 * side + 384],
                        )
            if not mine:
                self.reduce.swap(t, i)
            return 0

        lax.fori_loop(0, 2, block, 0)

    def second_half(self, t, mine):
        half = self.core if mine else 1 - self.core

        def block(i, _):
            if mine:
                self.reduce.swapped(t, i)
            grad = mm_tn(self.a[t.layer, :, lanes(i * 1536, 1536)], self.dp[:, lanes(half * 384, 384)])
            for z_low in range(2):
                z = 2 * i + z_low
                for x in range(4):
                    for y in range(4):
                        top = (z_low * 4 + x) * 192 + y * 24
                        part = jnp.concatenate([grad[top : top + 24], grad[top + 96 : top + 120]], axis=0)
                        self.put(t, mine, 0, x, y, z, part[0:16])
                        self.put(t, mine, 1, y, z, x, part[16:32])
                        self.put(t, mine, 2, z, x, y, part[32:48])
            if not mine:
                self.reduce.swap(t, i)
            return 0

        lax.fori_loop(0, 2, block, 0)

    def down(self, layer):
        def block(j, _):
            columns = lanes(j * 1536, 1536)
            rows = pl.ds(pl.multiple_of(j * 1536, 256), 1536)
            da = mm_nt(self.dp[...], self.w2[rows, :])
            self.du[:, columns] = (da * self.slope[layer, :, columns].astype(F32)).astype(BF16)
            return 0

        lax.fori_loop(0, 2, block, 0)

    def back_out(self, layer):
        weights = self.w[2 * layer, :, :, :, 2304:].reshape(D, D)
        self.dp[...] = mm_nt(self.du[:, 2304:], weights).astype(BF16)

    def pairs(self, layer, third):
        def pair(j):
            q = self.qkv[layer, :ROWS, lanes(j * 128, 128)]
            k = self.qkv[layer, :, lanes(768 + j * 128, 128)]
            v = self.qkv[layer, :, lanes(1536 + j * 128, 128)]
            do = self.dp[:, lanes(j * 128, 128)]
            dq = jnp.zeros((ROWS, 128), F32)
            dk = jnp.zeros((KEYS, 128), F32)
            dv = jnp.zeros((KEYS, 128), F32)
            for parity in range(2):
                do_half = keep_half(do, parity)
                probs = self.probs[layer, 2 * j + parity, :ROWS]
                wide = probs.astype(F32)
                d_probs = mm_nt(do_half, v)
                inner = jnp.sum(d_probs * wide, axis=-1, keepdims=True)
                d_scores = (wide * (d_probs - inner)).astype(BF16)
                dv = dv + mm_tn(probs, do_half)
                dq = dq + mm(d_scores, keep_half(k, parity))
                dk = dk + mm_tn(d_scores, keep_half(q, parity))
                self.probs[layer, 2 * j + parity] = mm(self.by_x[...], d_scores).astype(BF16)
            self.du[:, lanes(j * 128, 128)] = (dq * INV_ROOT).astype(BF16)
            self.du[:, lanes(768 + j * 128, 128)] = (dk[:ROWS] * INV_ROOT).astype(BF16)
            self.du[:, lanes(1536 + j * 128, 128)] = dv[:ROWS].astype(BF16)

        def trio(i, _):
            for j in range(3):
                pair(3 * i + j)
            return 0

        lax.fori_loop(third, third + 1, trio, 0)

    def fold_bias(self, layer):
        shape = (KEYS, 384)
        token = lax.broadcasted_iota(jnp.int32, shape, 0)
        lane = lax.broadcasted_iota(jnp.int32, shape, 1)
        target = jnp.where(token >= SEQ, -1000, (SPAN + 1) * (GRID - 1) - patch_offsets(token))
        self.sums[...] = jnp.zeros((3, ROWS, 128), F32)

        def two(i, _):
            lefts, rights = [], []
            for odd in range(2):
                x = 2 * i + odd
                rows = pl.ds(pl.multiple_of(16 * x, 16), 16)
                lefts.append(self.probs[layer, :, rows, :].reshape(192, KEYS))
                here = jnp.where(token == 0, 383, target + x)
                rights.append(ones(lane == here))
            more = mm(jnp.concatenate(lefts, axis=1), jnp.concatenate(rights, axis=0))
            for t in range(3):
                self.sums[t, :192] += more[:, 128 * t : 128 * t + 128]
            return 0

        lax.fori_loop(0, GRID // 2, two, 0)
        last = lax.broadcasted_iota(jnp.int32, (HEADS, 384), 1) == 383
        total = jnp.zeros((HEADS, D), F32)
        side = jnp.zeros((HEADS, 1), F32)
        for y in range(GRID + 1):
            rows = jnp.concatenate([self.sums[t, pl.ds(y, HEADS, stride=16), :] for t in range(3)], axis=1)
            plain = jnp.where(last, 0.0, rows)
            if y < GRID:
                side = side + jnp.sum(rows - plain, axis=1, keepdims=True)
                wide = jnp.concatenate([plain, jnp.zeros((HEADS, 384), F32)], axis=1)
                total = total + (pltpu.roll(wide, SPAN * y, 1) if y else wide)
            else:
                top = jnp.sum(plain, axis=1, keepdims=True)
                corner = jnp.sum(rows - plain, axis=1, keepdims=True)
        entry = lax.broadcasted_iota(jnp.int32, (HEADS, D), 1)
        total = jnp.where(entry == 729, top, total)
        total = jnp.where(entry == 730, side, total)
        total = jnp.where(entry == 731, corner, total)
        for head in range(HEADS):
            self.note(24 + layer * HEADS + head, total[head : head + 1])


MESH = pl.DeviceIdType.MESH
AXES = ("x", "y", "z")
ROUTES = (("x", "y", "z"), ("y", "z", "x"), ("z", "x", "y"))


class Place:
    def __init__(self):
        dp = lax.axis_index("dp")
        self.at = {"z": dp // 8, "x": (dp // 2) % 4, "c": dp % 2, "y": lax.axis_index("section")}

    def go(self, axis, step):
        at = dict(self.at)
        at[axis] = (at[axis] + step) % (2 if axis == "c" else 4)
        return ((at["z"] * 4 + at["x"]) * 2 + at["c"], at["y"])

    def index(self, axis, step=0):
        return (self.at[axis] + step) % 4


def meet(place):
    barrier = pltpu.get_barrier_semaphore()
    count = 0
    for axis in AXES:
        for step in (1, 2, 3):
            pl.semaphore_signal(barrier, inc=1, device_id=place.go(axis, step), device_id_type=MESH)
            count += 1
    pl.semaphore_signal(barrier, inc=1, device_id=place.go("c", 1), device_id_type=MESH)
    pl.semaphore_wait(barrier, count + 1)


class Tensor:
    def __init__(self, turn, which):
        self.number, self.slot = 3 * turn + which, (turn + which) % 2
        self.layer, self.which = 1 - turn, which
        self.second = which == 0
        self.section = 2 * self.layer + (which == 1)


class Reduce:
    def __init__(self, place, **refs):
        self.place = place
        self.__dict__.update(refs)

    def link(self, t, number, src, dst, device):
        return pltpu.make_async_remote_copy(
            src_ref=src, dst_ref=dst, send_sem=self.sems.at[0, t.number, number],
            recv_sem=self.sems.at[1, t.number, number], device_id=device, device_id_type=MESH,
        )

    def ring(self, name, t, r):
        place, axis = self.place, ROUTES[r][0]
        own, far = self.pair.at[t.slot, r], self.far.at[t.slot, r]
        across, ahead, behind = place.index(axis, 2), place.index(axis, 1), place.index(axis, 3)
        source, number, step = {
            "fa": lambda: (own.at[across, 0:2], 0, 1),
            "fb": lambda: (own.at[across, 2:4], 1, 3),
            "db": lambda: (own.at[ahead, 2:4], 2, 1),
            "da": lambda: (own.at[behind, 0:2], 3, 3),
            "ma": lambda: (far.at[0], 4, 1),
            "mb": lambda: (far.at[1], 5, 3),
        }[name]()
        return self.link(t, 6 + 6 * r + number, source, far.at[number], place.go(axis, step))

    def line_copy(self, t, r, step):
        axis = ROUTES[r][1]
        source = self.line.at[t.slot, r, self.place.index(axis, step)]
        return self.link(t, 23 + 3 * r + step, source, self.line_in.at[t.slot, r, step - 1], self.place.go(axis, step))

    def spot_copy(self, t, r, step):
        axis = ROUTES[r][2]
        source = self.spot.at[t.slot, r, self.place.index(axis, step)]
        return self.link(t, 32 + 3 * r + step, source, self.spot_in.at[t.which, r, step - 1], self.place.go(axis, step))

    def rows_copy(self, t):
        source = self.rows.at[t.layer, 1 - self.place.at["c"]]
        return self.link(t, 42, source, self.rows_in.at[t.layer], self.place.go("c", 1))

    def part(self, buffer, t, i):
        pair = pl.ds(2 * i, 2)
        if not t.second:
            return [(3 * i, buffer.at[t.slot, :, :, :, pair])]
        return [
            (3 * i, buffer.at[t.slot, 0, :, :, pair]),
            (3 * i + 1, buffer.at[t.slot, 1, :, pair]),
            (3 * i + 2, buffer.at[t.slot, 2, pair]),
        ]

    def across(self, t, i):
        for (number, source), (_, target) in zip(self.part(self.stage, t, i), self.part(self.pair, t, i)):
            yield self.link(t, number, source, target, self.place.go("c", 1))

    def prepare(self, t, before):
        for i in range(2):
            for copy in self.across(before, i):
                copy.wait_send()
        pl.semaphore_wait(self.pair_credit, 1)

    def swap(self, t, i):
        for copy in self.across(t, i):
            copy.start()

    def swapped(self, t, i):
        for copy in self.across(t, i):
            copy.wait_recv()

    def first(self, t):
        for r in range(3):
            @pl.when(t.number >= 2)
            def _():
                pl.semaphore_wait(self.far_credit.at[r, 0], 1)
                pl.semaphore_wait(self.far_credit.at[r, 1], 1)

            for name in ("fa", "fb", "db", "da"):
                self.ring(name, t, r).start()

    def merge(self, t):
        place = self.place
        for r, (axis, _, _) in enumerate(ROUTES):
            own, far = self.pair.at[t.slot, r], self.far.at[t.slot, r]
            ahead, behind = place.index(axis, 1), place.index(axis, 3)
            self.ring("fa", t, r).wait_recv()
            far[0] = (far[0].astype(F32) + own[ahead, 0:2].astype(F32)).astype(BF16)
            self.ring("ma", t, r).start()
            self.ring("fb", t, r).wait_recv()
            far[1] = (far[1].astype(F32) + own[behind, 2:4].astype(F32)).astype(BF16)
            self.ring("mb", t, r).start()

    def second(self, t):
        place = self.place
        for r in range(3):
            for name in ("db", "da", "ma", "mb"):
                self.ring(name, t, r).wait_recv()
        for r, (axis, nxt, _) in enumerate(ROUTES):
            own, far = self.pair.at[t.slot, r], self.far.at[t.slot, r]
            me = place.index(axis)
            low = own[me, 0:2].astype(F32) + far[4].astype(F32) + far[3].astype(F32)
            high = own[me, 2:4].astype(F32) + far[2].astype(F32) + far[5].astype(F32)
            line = self.line.at[t.slot, r]
            line[0:2] = low.astype(BF16)
            line[2:4] = high.astype(BF16)
            for step in (1, 2, 3):
                self.line_copy(t, r, step).start()
        for r in range(3):
            for name in ("fa", "fb", "db", "da", "ma", "mb"):
                self.ring(name, t, r).wait_send()

        @pl.when(t.number + 2 < 6)
        def _():
            pl.semaphore_signal(self.pair_credit, inc=1, device_id=place.go("c", 1), device_id_type=MESH)
            for r, (axis, _, _) in enumerate(ROUTES):
                pl.semaphore_signal(self.far_credit.at[r, 0], inc=1, device_id=place.go(axis, 1), device_id_type=MESH)
                pl.semaphore_signal(self.far_credit.at[r, 1], inc=1, device_id=place.go(axis, 3), device_id_type=MESH)

    def third(self, t):
        for r, (_, axis, _) in enumerate(ROUTES):
            total = self.line[t.slot, r, self.place.index(axis)].astype(F32)
            for step in (1, 2, 3):
                self.line_copy(t, r, step).wait_recv()
                total = total + self.line_in[t.slot, r, step - 1].astype(F32)
            self.spot[t.slot, r] = total.astype(BF16)
            for step in (1, 2, 3):
                self.spot_copy(t, r, step).start()
        for r in range(3):
            for step in (1, 2, 3):
                self.line_copy(t, r, step).wait_send()

    def close(self, t):
        for r, (_, _, axis) in enumerate(ROUTES):
            total = self.spot[t.slot, r, self.place.index(axis)].astype(F32)
            for step in (1, 2, 3):
                self.spot_copy(t, r, step).wait_recv()
                total = total + self.spot_in[t.which, r, step - 1].astype(F32)
            if not t.second:
                self.first_out[t.section, 0, 0, r] = total.astype(BF16)
            elif r == 0:
                self.rows[t.layer, 0, 0:16] = total
            elif r == 1:
                self.rows[t.layer, 0, 16:24] = total[0:8]
                self.rows[t.layer, 1, 0:8] = total[8:16]
            else:
                self.rows[t.layer, 1, 8:24] = total
        for r in range(3):
            for step in (1, 2, 3):
                self.spot_copy(t, r, step).wait_send()
        if t.second:
            self.rows_copy(t).start()

    def finish(self):
        me = self.place.at["c"]
        for turn in range(2):
            t = Tensor(turn, 0)
            self.rows_copy(t).wait()
            self.second_out[t.layer, :, lanes(me * 384, 384)] = self.rows[t.layer, me]
            self.second_out[t.layer, :, lanes((1 - me) * 384, 384)] = self.rows_in[t.layer]
        for which in (1, 2):
            for i in range(2):
                for copy in self.across(Tensor(1, which), i):
                    copy.wait_send()


class Totals:
    def __init__(self, place, part, bufs, sems):
        self.place, self.part, self.bufs, self.sems = place, part, bufs, sems
        self.copies = []

    def send(self, src, dst, number, device):
        copy = pltpu.make_async_remote_copy(
            src_ref=src, dst_ref=dst, send_sem=self.sems.at[0, number], recv_sem=self.sems.at[1, number],
            device_id=device, device_id_type=MESH,
        )
        copy.start()
        self.copies.append(copy)
        return copy

    @staticmethod
    def half(core):
        return pl.ds(pl.multiple_of(core * 24, 8), 24)

    def start(self, small):
        me = self.place.at["c"]
        self.small = small
        self.now = [self.send(small.at[self.half(1 - me)], self.bufs.at[12], 0, self.place.go("c", 1))]

    def step(self, number):
        place, me = self.place, self.place.at["c"]
        for copy in self.now:
            copy.wait_recv()
            copy.wait_send()
        if number == 0:
            self.part[...] = self.small[self.half(me), :] + self.bufs[12]
        else:
            axis = AXES[number - 1]
            self.bufs[4 * number - 4 + place.at[axis]] = self.part[...]
            self.part[...] = (
                (self.bufs[4 * number - 4] + self.bufs[4 * number - 3])
                + (self.bufs[4 * number - 2] + self.bufs[4 * number - 1])
            )
        if number < 3:
            axis = AXES[number]
            self.now = [
                self.send(self.part, self.bufs.at[4 * number + place.at[axis]], 1 + 3 * number + step - 1, place.go(axis, step))
                for step in (1, 2, 3)
            ]
        else:
            self.now = [self.send(self.part, self.bufs.at[13], 10, place.go("c", 1))]

    def close(self, out):
        me = self.place.at["c"]
        for copy in self.now:
            copy.wait_recv()
        out[self.half(me), :] = self.part[...]
        out[self.half(1 - me), :] = self.bufs[13]
        self.copies[-1].wait_send()


class Spread:
    def __init__(self, place, sems):
        self.place, self.sems = place, sems
        self.sent = []

    def make(self, number, src, dst, device):
        return pltpu.make_async_remote_copy(
            src_ref=src, dst_ref=dst, send_sem=self.sems.at[0, number], recv_sem=self.sems.at[1, number],
            device_id=device, device_id_type=MESH,
        )

    def send(self, number, src, dst, device):
        copy = self.make(number, src, dst, device)
        copy.start()
        self.sent.append(copy)

    def wait(self, number, ref):
        pltpu.make_async_remote_copy(
            src_ref=ref, dst_ref=ref, send_sem=self.sems.at[0, number], recv_sem=self.sems.at[1, number],
            device_id=self.place.go("c", 1), device_id_type=MESH,
        ).wait_recv()

    def drain(self):
        for copy in self.sent:
            copy.wait_send()


GATHER_MESSAGES = 99


class Gather(Spread):
    def __init__(self, place, full, sems):
        super().__init__(place, sems)
        self.full = full
        y = place.at["y"]
        self.first = {"x": 3, "z": 1}
        self.second = {"x": jnp.where(y == 3, 1, 2), "z": jnp.where(y == 1, 3, 2)}
        self.third = {"x": jnp.where(y == 3, 2, 1), "z": jnp.where(y == 1, 2, 3)}

    def rows(self, route, step, sub=None, core=None):
        core = self.place.at["c"] if core is None else core
        block = (0 if route == "x" else 8) + self.place.index(route, step) * 2 + core
        return (block // 4, block % 4, slice(None) if sub is None else slice(16 * sub, 16 * sub + 16))

    def ref(self, rel, route, step, sub=None):
        return self.full.at[(self.place.index("y", rel),) + self.rows(route, step, sub)]

    @staticmethod
    def along_y(rel, route, sub):
        return 3 * (2 * (rel - 1) + (route == "z")) + sub

    @staticmethod
    def in_plane(rel, route, kind, sub):
        return 18 + 9 * (2 * (rel - 1) + (route == "z")) + 3 * kind + sub

    @staticmethod
    def across(rel, route, step):
        return 72 + 4 * (2 * (rel - 1) + (route == "z")) + step

    def load(self, source, sems):
        at = self.place.at
        mine, rest = [], []
        for half, route in enumerate(("x", "z")):
            for block in range(8):
                number = 8 * half + (at[route] * 2 + at["c"] + block) % 8
                rows = pl.ds(pl.multiple_of(number * 48, 16), 48)
                copy = pltpu.make_async_copy(
                    source.at[rows], self.full.at[at["y"], number // 4, number % 4], sems.at[half, block]
                )
                (rest if block else mine).append(copy)
        for copy in mine + rest:
            copy.start()
        return mine, rest

    def own(self, up, down):
        copies = []
        for sub in range(3):
            for route, step in ((up, 1), (down, 3)):
                mine = self.ref(0, route, 0, sub)
                copies.append(self.make(self.along_y(4 - step, route, sub), mine, mine, self.place.go("y", step)))
        self.sent += copies
        return copies

    def arrive(self, rels):
        for sub in range(3):
            for route, rel in rels.items():
                piece = self.ref(rel, route, 0, sub)
                self.wait(self.along_y(rel, route, sub), piece)
                if rels is self.first:
                    self.send(self.along_y(2, route, sub), piece, piece, self.place.go("y", 4 - rel))
                for kind, step in ((0, 1), (1, 3)):
                    self.send(self.in_plane(rel, route, kind, sub), piece, piece, self.place.go(route, step))
        for route, rel in rels.items():
            piece = self.ref(rel, route, 0)
            self.send(self.across(rel, route, 0), piece, piece, self.place.go("c", 1))

    def turn(self, rels):
        place = self.place
        clockwise = 1 - 2 * place.at["c"]
        for sub, way in ((0, 1), (1, clockwise), (2, -1)):
            for route, rel in rels.items():
                for kind, step in ((0, 3), (1, 1)):
                    self.wait(self.in_plane(rel, route, kind, sub), self.ref(rel, route, step, sub))
                piece = self.ref(rel, route, 4 - way, sub)
                self.send(self.in_plane(rel, route, 2, sub), piece, piece, place.go(route, 4 + way))
        for route, rel in rels.items():
            for step in (3, 1):
                piece = self.ref(rel, route, step)
                self.send(self.across(rel, route, step), piece, piece, place.go("c", 1))

    def end(self, rels):
        for route, rel in rels.items():
            for sub in range(3):
                self.wait(self.in_plane(rel, route, 2, sub), self.ref(rel, route, 2, sub))
            piece = self.ref(rel, route, 2)
            self.send(self.across(rel, route, 2), piece, piece, self.place.go("c", 1))

    def ending(self, rels):
        waits, copies = [], []
        for route, rel in rels.items():
            for sub in range(3):
                ref = self.ref(rel, route, 2, sub)
                waits.append(self.make(self.in_plane(rel, route, 2, sub), ref, ref, self.place.go("c", 1)))
            piece = self.ref(rel, route, 2)
            copies.append(self.make(self.across(rel, route, 2), piece, piece, self.place.go("c", 1)))
        self.sent += copies
        return waits, copies

    def settle(self, section):
        rel = (section - self.place.at["y"] + 4) % 4
        other = 1 - self.place.at["c"]

        def run():
            for route in ("x", "z"):
                for step in range(4):
                    self.wait(self.across(rel, route, step), self.full.at[(section,) + self.rows(route, step, core=other)])

        pl.when(rel > 0)(run)


def layers_kernel(
    tokens, masked, cotangent, live, mask_token, norm_gain, norm_shift, layer_scale, w_own, w2_hbm,
    tables,
    block_out, tokens_grad, first_grad, second_out, totals,
    w, w2, h, qkv, probs, a, slope, p, n, bias, table, select_f, by_x, fold_sums, du, dp, g, vec, vecs, small,
    stage, pair, far, line, line_in, spot, spot_in, rows, rows_in, part, bufs, first_out,
    tokens_in, cotangent_in, load_sems, w2_sems, image_sems, gather_sems, sems, small_sems, share_sems, share_out_sems, pair_credit, far_credit,
):
    place = Place()
    vec[0:1] = norm_gain[...]
    vec[1:2] = norm_shift[...]
    vec[2:3] = layer_scale[...]
    vec[3:8] = jnp.zeros((5, D), F32)
    y = place.at["y"]
    gather = Gather(place, w, gather_sems)
    own_first, own_rest = gather.load(w_own.at[0], load_sems)
    images = [
        pltpu.make_async_copy(source, target, image_sems.at[i])
        for i, (source, target) in enumerate(((tokens, tokens_in), (cotangent, cotangent_in)))
    ]
    for copy in images:
        copy.start()
    meet(place)
    for copy in own_first:
        copy.wait()
    for copy in gather.own("x", "z"):
        copy.start()
    own_later = gather.own("z", "x")

    @pl.when(y == 0)
    def _():
        for copy in own_later:
            copy.start()

    def second_weights(layer):
        copies = []
        for block in range(8):
            rows = pl.ds(block * 384, 384)
            copies.append(pltpu.make_async_copy(w2_hbm.at[layer, rows], w2.at[rows], w2_sems.at[block]))
        return copies

    def load_second(layer):
        for copy in second_weights(layer):
            copy.start()

    def loaded_second(layer):
        for copy in second_weights(layer):
            copy.wait()

    def loaded(copies):
        for copy in copies:
            copy.wait()

    load_second(0)
    vecs[y] = vec[...]
    for step in (1, 2, 3):
        gather.send(95 + step, vec, vecs.at[y], place.go("y", step))
    valid = jnp.where(y < live[lax.axis_index("dp")], 1.0, 0.0)
    body = Body(
        valid=valid, core=place.at["c"], vecs=vecs, table=table,
        select_forward=select_f, by_x=by_x, block_out=tokens_in, small=small,
        w=w, w2=w2, h=h, qkv=qkv, probs=probs, a=a, slope=slope, p=p, n=n, bias=bias,
        sums=fold_sums, du=du, dp=dp, g=g, stage=stage, pair=pair,
    )
    reduce = Reduce(
        place, stage=stage, pair=pair, far=far, line=line, line_in=line_in, spot=spot, spot_in=spot_in,
        rows=rows, rows_in=rows_in, first_out=first_out, second_out=second_out, sems=sems,
        pair_credit=pair_credit, far_credit=far_credit,
    )
    body.reduce = reduce
    sums = Totals(place, part, bufs, small_sems)

    gather.arrive(gather.first)

    @pl.when(y != 0)
    def _():
        for copy in own_later:
            copy.start()

    fold_sums[...] = jnp.zeros_like(fold_sums)
    square = (ROWS, KEYS)
    diagonal = lax.broadcasted_iota(jnp.int32, square, 0) == lax.broadcasted_iota(jnp.int32, square, 1)
    flags = jnp.concatenate([masked[...].astype(F32), jnp.zeros((1, KEYS - SEQ), F32)], axis=1)
    here = jnp.sum(jnp.where(diagonal, flags, 0.0), axis=1, keepdims=True)
    h[0, 192:] = jnp.zeros((16, D), BF16)
    for copy in images:
        copy.wait()
    start = tokens_in[0].astype(F32)
    h[0, :SEQ] = (start + here[:SEQ] * (mask_token[...].astype(F32).reshape(1, D) - start)).astype(BF16)
    g[192:] = jnp.zeros((16, D), BF16)
    g[:SEQ] = (cotangent_in[0].astype(F32) * valid).astype(BF16)
    body.make_selectors()
    body.read_tables(tables)
    body.expand_bias(0, 0, 6)
    gather.arrive(gather.second)
    body.expand_bias(0, 6, 12)
    gather.turn(gather.first)
    body.expand_bias(1, 0, 6)
    gather.arrive(gather.third)
    gather.turn(gather.second)
    body.expand_bias(1, 6, 12)
    gather.end(gather.first)
    gather.end(gather.second)
    for step in (1, 2, 3):
        gather.wait(95 + step, vecs.at[place.index("y", 4 - step)])
    loaded(own_rest)
    gather.turn(gather.third)
    last_waits, last_copies = gather.ending(gather.third)

    def forward_layer(layer, _):
        gather.settle(2 * layer)
        body.attend_forward(layer)

        @pl.when(layer == 0)
        def _():
            for copy in last_waits:
                copy.wait_recv()
            for copy in last_copies:
                copy.start()

        gather.settle(2 * layer + 1)
        loaded_second(layer)
        body.dense_forward(layer)

        @pl.when(layer == 0)
        def _():
            body.finish(1, a.at[0], w2[...])
            load_second(1)

        return 0

    lax.fori_loop(0, 2, forward_layer, 0)
    block_copy = pltpu.make_async_copy(tokens_in, block_out, image_sems.at[0])
    gather.drain()

    def backward_layer(turn, _):
        layer = 1 - turn
        again = turn > 0
        second, dense, attention = (Tensor(turn, which) for which in range(3))
        _, dense_before, attention_before = (Tensor(turn - 1, which) for which in range(3))
        body.enter(layer, 1)

        @pl.when(again)
        def _():
            reduce.prepare(second, dense_before)

        body.second_half(second, False)

        @pl.when(turn == 0)
        def _():
            body.last_finish()
            block_copy.start()

        @pl.when(again)
        def _():
            reduce.third(dense_before)
            loaded_second(0)

        body.down(layer)

        @pl.when(turn == 0)
        def _():
            load_second(0)

        @pl.when(again)
        def _():
            reduce.merge(attention_before)

        body.second_half(second, True)
        reduce.first(second)

        @pl.when(again)
        def _():
            reduce.second(attention_before)
            reduce.prepare(dense, attention_before)

        body.first_half(dense, False)

        @pl.when(again)
        def _():
            reduce.close(dense_before)

        body.leave(layer, 1)
        reduce.merge(second)
        body.first_half(dense, True)
        reduce.first(dense)
        body.enter(layer, 0)
        body.back_out(layer)

        @pl.when(again)
        def _():
            reduce.third(attention_before)

        body.pairs(layer, 0)
        reduce.second(second)
        body.pairs(layer, 1)
        reduce.merge(dense)

        reduce.prepare(attention, second)
        body.first_half(attention, False)
        body.fold_bias(layer)

        @pl.when(again)
        def _():
            reduce.close(attention_before)

        reduce.third(second)
        body.leave(layer, 0)
        reduce.second(dense)
        body.first_half(attention, True)
        reduce.first(attention)
        reduce.close(second)
        return 0

    lax.fori_loop(0, 2, backward_layer, 0)
    dense, attention = Tensor(1, 1), Tensor(1, 2)
    grad = g[...].astype(F32)
    cotangent_in[0] = (grad * (1.0 - here)).astype(BF16)[:SEQ]
    tokens_copy = pltpu.make_async_copy(cotangent_in, tokens_grad, image_sems.at[1])
    tokens_copy.start()
    small[20:21, :] = jnp.sum(grad * here, axis=0, keepdims=True)
    small[21:24, :] = jnp.zeros((3, D), F32)
    sums.start(small)
    reduce.third(dense)
    reduce.merge(attention)
    reduce.close(dense)
    reduce.second(attention)
    sums.step(0)
    reduce.third(attention)
    sums.step(1)
    reduce.close(attention)
    beside = [lambda: sums.step(2), lambda: sums.step(3), lambda: sums.close(totals)]
    Share(place, first_out, w.at[3], share_sems).run(first_grad, share_out_sems, beside)
    reduce.finish()
    block_copy.wait()
    tokens_copy.wait()


def layers(tokens, masked, cotangent, live, mask_token, norm_gain, norm_shift, layer_scale, w_own, w2, tables):
    vm = pl.BlockSpec(memory_space=pltpu.VMEM)
    hbm = pl.BlockSpec(memory_space=pl.ANY)
    sm = pl.BlockSpec(memory_space=pltpu.SMEM)
    V, DMA, REGULAR = pltpu.VMEM, pltpu.SemaphoreType.DMA, pltpu.SemaphoreType.REGULAR
    return pl.pallas_call(
        layers_kernel,
        out_shape=(
            jax.ShapeDtypeStruct((1, SEQ, D), BF16),
            jax.ShapeDtypeStruct((1, SEQ, D), BF16),
            jax.ShapeDtypeStruct((4, 4, 48, FF), BF16),
            jax.ShapeDtypeStruct((2, 24, D), F32),
            jax.ShapeDtypeStruct((48, D), F32),
        ),
        in_specs=[hbm, vm, hbm, sm, vm, vm, vm, vm, hbm, hbm, vm],
        out_specs=(hbm, hbm, hbm, vm, vm),
        scratch_shapes=[
            V((4, 4, 4, 48, FF), BF16), V((FF, D), BF16), V((4, ROWS, D), BF16), V((2, KEYS, 2304), BF16),
            V((2, HEADS, 16 * GRID, KEYS), BF16), V((2, ROWS, FF), BF16), V((2, ROWS, FF), BF16),
            V((4, ROWS, D), BF16), V((3, ROWS, D), BF16), V((2, HEADS, ROWS, KEYS), BF16), V((2 * HEADS, 896), F32), V((384, KEYS), BF16),
            V((16 * GRID, ROWS), BF16),
            V((3, ROWS, 128), F32), V((ROWS, FF), BF16), V((ROWS, D), BF16), V((ROWS, D), BF16),
            V((8, D), F32), V((4, 8, D), F32), V((48, D), F32),
            V((2,) + HALF, BF16), V((2,) + HALF, BF16), V((2, 3, 6, 2, 4, 16, 384), BF16),
            V((2, 3, 4, 4, 16, 384), BF16), V((2, 3, 3, 4, 16, 384), BF16),
            V((2, 3, 4, 16, 384), BF16), V((3, 3, 3, 16, 384), BF16),
            V((2, 2, 24, 384), F32), V((2, 24, 384), F32), V((24, D), F32), V((14, 24, D), F32),
            V((4, 1, 1, 3, 16, 384), BF16), V((1, SEQ, D), BF16), V((1, SEQ, D), BF16),
            DMA((2, 8)), DMA((8,)), DMA((2,)), DMA((2, GATHER_MESSAGES)), DMA((2, 6, 43)), DMA((2, 11)), DMA((2, 75)), DMA((48,)), REGULAR, REGULAR((3, 2)),
        ],
        compiler_params=pltpu.CompilerParams(
            collective_id=1, has_side_effects=True, vmem_limit_bytes=64 * 2**20
        ),
    )(tokens, masked, cotangent, live, mask_token, norm_gain, norm_shift, layer_scale, w_own, w2, tables)


class Share(Spread):
    def __init__(self, place, blocks, full, sems):
        super().__init__(place, sems)
        self.blocks, self.full = blocks, full

    def regions(self, c, x, y, z):
        def columns(third):
            return pl.ds(pl.multiple_of((c * 4 + third[0]) * 384, 128), third[1] * 384)

        for route, (a1, a2, a3) in enumerate(((x, y, z), (y, z, x), (z, x, y))):
            yield route, self.full.at[
                pl.ds(*a1), pl.ds(*a2), slice(16 * route, 16 * route + 16), columns(a3)
            ]

    def pass_on(self, base, regions, device):
        for route, region in regions:
            self.send(base + route, region, region, device)

    def await_all(self, base, regions):
        for route, region in regions:
            self.wait(base + route, region)

    def keep(self, out, c, x, y, z):
        for (route, region), (_, target) in zip(self.regions(c, x, y, z), Share(self.place, None, out, None).regions(c, x, y, z)):
            copy = pltpu.make_async_copy(region, target, self.out_sems.at[len(self.kept)])
            copy.start()
            self.kept.append(copy)

    def run(self, out, out_sems, beside):
        place = self.place
        at = place.at
        self.out_sems, self.kept = out_sems, []
        c, x, y, z = at["c"], (at["x"], 1), (at["y"], 1), (at["z"], 1)
        other = 1 - c
        every = (0, 4)
        halves = ((0, 2), (2, 2))

        def near(axis, step):
            return (place.index(axis, step), 1)

        for route, region in self.regions(c, x, y, z):
            for step in (1, 2, 3):
                source = self.blocks.at[place.index("y", step), :, :, route]
                self.send(3 * (step - 1) + route, source, region, place.go("y", step))
            region[...] = self.blocks[at["y"], :, :, route]
        beside[0]()
        for step in (1, 2, 3):
            self.await_all(3 * (step - 1), self.regions(c, x, near("y", 4 - step), z))
        for step in (1, 3, 2):
            self.pass_on(9 + 3 * (step - 1), self.regions(c, x, halves[0], z), place.go("x", step))
            self.pass_on(18 + 3 * (step - 1), self.regions(c, x, halves[1], z), place.go("z", step))
        beside[1]()
        for step in (1, 3, 2):
            self.await_all(9 + 3 * (step - 1), self.regions(c, near("x", 4 - step), halves[0], z))
            self.await_all(18 + 3 * (step - 1), self.regions(c, x, halves[1], near("z", 4 - step)))
        for step in (1, 3):
            self.pass_on(27 + 3 * (step - 1), self.regions(c, every, halves[0], z), place.go("z", step))
            self.pass_on(36 + 3 * (step - 1), self.regions(c, x, halves[1], every), place.go("x", step))
        self.pass_on(45, self.regions(c, every, halves[0], z), place.go("c", 1))
        self.pass_on(48, self.regions(c, x, halves[1], every), place.go("c", 1))
        self.keep(out, c, every, halves[0], z)
        self.keep(out, c, x, halves[1], every)
        beside[2]()
        for step, part, base in ((1, (0, 1), 30), (3, (1, 1), 69)):
            self.await_all(27 + 3 * (step - 1), self.regions(c, every, halves[0], near("z", 4 - step)))
            self.pass_on(base, self.regions(c, every, part, near("z", 4 - step)), place.go("z", step))
            part = (part[0] + 2, 1)
            self.await_all(36 + 3 * (step - 1), self.regions(c, near("x", 4 - step), halves[1], every))
            self.pass_on(base + (9 if base == 30 else 3), self.regions(c, near("x", 4 - step), part, every), place.go("x", step))
        for step in (1, 3):
            self.pass_on(51 + 3 * (step - 1), self.regions(c, every, halves[0], near("z", 4 - step)), place.go("c", 1))
            self.pass_on(60 + 3 * (step - 1), self.regions(c, near("x", 4 - step), halves[1], every), place.go("c", 1))
            self.keep(out, c, every, halves[0], near("z", 4 - step))
            self.keep(out, c, near("x", 4 - step), halves[1], every)
        self.await_all(45, self.regions(other, every, halves[0], z))
        self.keep(out, other, every, halves[0], z)
        self.await_all(48, self.regions(other, x, halves[1], every))
        self.keep(out, other, x, halves[1], every)
        for step in (1, 3):
            self.await_all(51 + 3 * (step - 1), self.regions(other, every, halves[0], near("z", 4 - step)))
            self.keep(out, other, every, halves[0], near("z", 4 - step))
            self.await_all(60 + 3 * (step - 1), self.regions(other, near("x", 4 - step), halves[1], every))
            self.keep(out, other, near("x", 4 - step), halves[1], every)
        for part, base in ((0, 30), (1, 69)):
            self.await_all(base, self.regions(c, every, (part, 1), near("z", 2)))
            self.await_all(base + (9 if base == 30 else 3), self.regions(c, near("x", 2), (part + 2, 1), every))
        self.pass_on(54, self.regions(c, every, halves[0], near("z", 2)), place.go("c", 1))
        self.pass_on(63, self.regions(c, near("x", 2), halves[1], every), place.go("c", 1))
        self.keep(out, c, every, halves[0], near("z", 2))
        self.keep(out, c, near("x", 2), halves[1], every)
        self.await_all(54, self.regions(other, every, halves[0], near("z", 2)))
        self.keep(out, other, every, halves[0], near("z", 2))
        self.await_all(63, self.regions(other, near("x", 2), halves[1], every))
        self.keep(out, other, near("x", 2), halves[1], every)
        for copy in self.kept:
            copy.wait()
        self.drain()


def finish_kernel(
    first, block_in, tokens_in, second_in, totals, live,
    block_out, tokens_grad, first_grad, second_grad, gain_grad, shift_grad, scale_grad, table_grad, mask_grad, rms_out,
    narrow, wide, images, load_sems, store_sems, image_sems,
):
    loads, stores = [], []
    through = []
    for i, (source, target) in enumerate(((block_in, block_out), (tokens_in, tokens_grad))):
        through.append((
            pltpu.make_async_copy(source, images.at[i], image_sems.at[i]),
            pltpu.make_async_copy(images.at[i], target, image_sems.at[2 + i]),
        ))
    for block in range(16):
        a1, a2 = block // 4, block % 4
        rows = pl.ds(block * 48, 48)
        loads.append(pltpu.make_async_copy(first.at[a1, a2], narrow.at[a1, a2], load_sems.at[block]))
        stores.append(pltpu.make_async_copy(wide.at[rows], first_grad.at[0, rows], store_sems.at[block]))
    for load in loads:
        load.start()
    for load, _ in through:
        load.start()
    for block in range(16):
        loads[block].wait()
        wide[block * 48 : block * 48 + 48, :] = narrow[block // 4, block % 4].astype(F32)
        stores[block].start()
    for load, store in through:
        load.wait()
        store.start()
    second_grad[...] = second_in[...]
    own = 8 + 3 * lax.axis_index("section")
    scale_grad[...] = totals[pl.ds(own, 1), :]
    gain_grad[...] = totals[pl.ds(own + 1, 1), :]
    shift_grad[...] = totals[pl.ds(own + 2, 1), :]
    mask_grad[...] = totals[20, :]
    count = lax.fori_loop(0, live.shape[0], lambda i, total: total + live[i], 0)
    tokens = count.astype(F32) * (SEQ * D)
    rms = jnp.sqrt(jnp.sum(totals[0:8, :], axis=1, keepdims=True) / tokens)
    rms_out[...] = jnp.concatenate(
        [jnp.concatenate([rms[2 * s + k : 2 * s + k + 1] for s in range(4)], axis=1) for k in range(2)], axis=0
    )
    for layer in range(2):
        table_grad[:, layer, :] = totals[24 + layer * HEADS : 24 + (layer + 1) * HEADS, : table_grad.shape[2]]
    for store in stores:
        store.wait()
    for _, store in through:
        store.wait()


def finish_all(first, block_out, tokens_grad, second, totals, live, entries):
    vm = pl.BlockSpec(memory_space=pltpu.VMEM)
    hbm = pl.BlockSpec(memory_space=pl.ANY)
    image, pair, vector = (1, SEQ, D), (2, 24, D), (1, D)
    return pl.pallas_call(
        finish_kernel,
        out_shape=(
            jax.ShapeDtypeStruct(image, BF16), jax.ShapeDtypeStruct(image, BF16), jax.ShapeDtypeStruct((1, D, FF), F32),
            jax.ShapeDtypeStruct(pair, F32), jax.ShapeDtypeStruct(vector, F32), jax.ShapeDtypeStruct(vector, F32),
            jax.ShapeDtypeStruct(vector, F32), jax.ShapeDtypeStruct((HEADS, 2, entries), F32),
            jax.ShapeDtypeStruct((D,), F32), jax.ShapeDtypeStruct((2, 4), F32),
        ),
        in_specs=[hbm, hbm, hbm, vm, vm, pl.BlockSpec(memory_space=pltpu.SMEM)],
        out_specs=(hbm, hbm, hbm) + (vm,) * 7,
        scratch_shapes=[
            pltpu.VMEM((4, 4, 48, FF), BF16), pltpu.VMEM((D, FF), F32), pltpu.VMEM((2, 1, SEQ, D), BF16),
            pltpu.SemaphoreType.DMA((16,)), pltpu.SemaphoreType.DMA((16,)), pltpu.SemaphoreType.DMA((4,)),
        ],
        compiler_params=pltpu.CompilerParams(vmem_limit_bytes=62 * 2**20),
    )(first, block_out, tokens_grad, second, totals, live)


def on_device(
    tokens, masked, live_images, mask_token, norm_gain, norm_shift, w_first, w_second, layer_scale, rel_table, cotangent
):
    block_out, tokens_grad, first, second, totals = layers(
        tokens, masked, cotangent, live_images, mask_token, norm_gain, norm_shift, layer_scale, w_first, w_second,
        jnp.transpose(rel_table, (2, 0, 1)),
    )
    *outs, table_grad, mask_grad, rms = finish_all(
        first, block_out, tokens_grad, second, totals, live_images, rel_table.shape[1]
    )
    return (*outs, jnp.transpose(table_grad, (1, 2, 0)), mask_grad, rms.T)


def solution(mesh):
    both = P(("dp", "section"), None, None)
    part = P("section", None)
    return jax.shard_map(
        on_device,
        mesh=mesh,
        in_specs=(both, P(("dp", "section"), None), P(), P(), part, part, P("section", None, None), P(), part, P(), both),
        out_specs=(
            both, both, P("section", None, None), P(None, ("dp", "section"), None), part, part, part, P(), P(), P(),
        ),
        check_vma=False,
    )
```
